32 devices in a mesh: tensor: 4 (over y, core), context: 4 (over z), dp: 2 (over x).
Axes of the slice: x: 2, y: 2, z: 4, core: 2. Of those that a mesh axis runs over, the one named last changes fastest.
Arguments:
- tokens: bfloat16 [4, 2048, 2048], P('dp', 'context'), may hold values from -6 to 6
- segment_ids: int32 [4, 2048], P('dp'), may hold values from 0 to 4, as said below
- norm_gain_1: float32 [2048], replicated, may hold values from 0.25 to 1.75
- w_query: bfloat16 [2048, 2048], P(None, 'tensor'), may hold values from -0.125 to 0.125
- w_key: bfloat16 [2048, 256], P(None, 'tensor'), may hold values from -0.125 to 0.125
- w_value: bfloat16 [2048, 256], P(None, 'tensor'), may hold values from -0.125 to 0.125
- w_output: bfloat16 [2048, 2048], P('tensor'), may hold values from -1.5 to 1.5
- norm_gain_2: float32 [2048], replicated, may hold values from 0.25 to 1.75
- w_gate: bfloat16 [2048, 5632], P(None, 'tensor'), may hold values from -0.125 to 0.125
- w_up: bfloat16 [2048, 5632], P(None, 'tensor'), may hold values from -0.125 to 0.125
- w_down: bfloat16 [5632, 2048], P('tensor'), may hold values from -0.078125 to 0.078125
- cotangent: bfloat16 [4, 2048, 2048], P('dp', 'context'), may hold values from -6 to 6
Outputs:
- layer_out: bfloat16 [4, 2048, 2048], P('dp', 'context')
- grad_tokens: float32 [4, 2048, 2048], P('dp', 'context')
- grad_gain_1: float32 [2048], P(('context', 'dp'))
- grad_query: float32 [2048, 2048], P(('context', 'dp'), 'tensor')
- grad_key: float32 [2048, 256], P(('context', 'dp'), 'tensor')
- grad_value: float32 [2048, 256], P(('context', 'dp'), 'tensor')
- grad_output: float32 [2048, 2048], P('tensor', ('context', 'dp'))
- grad_gain_2: float32 [2048], P(('context', 'dp'))
- grad_gate: float32 [2048, 5632], P(('context', 'dp'), 'tensor')
- grad_up: float32 [2048, 5632], P(('context', 'dp'), 'tensor')
- grad_down: float32 [5632, 2048], P('tensor', ('context', 'dp'))
The draws below stay inside these ranges and needn't reach their ends.
Inputs may be any that keep to these rules, and one draw needn't show every extreme that they name: Each row of segment_ids starts at 0, never falls, rises by at most one from a token to the next, and ends at 4.
All inputs are finite; a program needn't handle non-finite values.
Results may differ from the reference program's by a relative error of at most 0.02.
Values may be sent and summed in bfloat16 or wider, within the bound.
No kernel may reach another device: no remote copies, remote signals or barrier semaphores. Data moves between devices by JAX's collectives and lax.ppermute only.
A program may use at most 256 MiB of HBM per device.

```python
import jax
import jax.numpy as jnp
from jax import lax

D = 2048
H = 32
KVH = 4
HD = 64
FF = 5632
LEN = 2048
STRETCH = 512
NSEQ = 4


def draw_segment_ids(key, part):
    key = jax.random.fold_in(key, 7)
    key_start, key_end, key_front, key_back = jax.random.split(key, 4)
    reach = STRETCH // 2
    start_cut = jax.random.randint(key_start, (NSEQ, 1), 2, reach + 2)
    end_cut = LEN - jax.random.randint(key_end, (NSEQ, 1), 2, reach + 2)
    front_cut = jax.random.randint(key_front, (NSEQ, 1), 1, start_cut)
    back_cut = end_cut + jax.random.randint(key_back, (NSEQ, 1), 1, LEN - end_cut)
    token_index = jnp.arange(LEN, dtype=jnp.int32)[None, :]
    cut_mask = (token_index == front_cut) | (token_index == start_cut) | (token_index == end_cut) | (token_index == back_cut)
    return jnp.cumsum(cut_mask.astype(jnp.int32), axis=1).astype(jnp.int32)


def with_spikes(values, rng, source, target, parts, factor):
    def block_of(axis_at):
        return (jnp.arange(values.shape[axis_at]) // (values.shape[axis_at] // parts)).reshape((-1,) + (1,) * (values.ndim - 1 - axis_at))

    near = jax.random.permutation(rng, parts)[block_of(target)]
    second = (block_of(target) + parts // 2) % parts
    return jnp.where((block_of(source) == near) | (block_of(source) == second), factor * values, values)


def shard_levels(key, dims, cuts, least, high):
    level = 1.0
    for dim, blocks in cuts:
        draws = jax.random.uniform(jax.random.fold_in(jax.random.fold_in(key, 6), dim), (blocks,), jnp.float32, least / len(cuts), high / len(cuts))
        level = level * jnp.repeat(jnp.exp(draws), dims[dim] // blocks).reshape((-1,) + (1,) * (len(dims) - 1 - dim))
    return level


def scatter_about(own_key, shape, spread, most, cuts=(), kind=jnp.bfloat16):
    values = spread * jax.random.normal(own_key, shape, jnp.float32)
    if cuts:
        values = values * shard_levels(own_key, shape, cuts, -0.22, 0.18)
    return jnp.clip(values, -most, most).astype(kind)


def heavy_noise(stream_key, extent, scale, most, shards, heavy, kind=jnp.bfloat16):
    entries = scale * jax.random.normal(stream_key, extent, jnp.float32)
    if shards:
        entries = entries * shard_levels(stream_key, extent, shards, -0.22, 0.18)
    return jnp.clip(with_spikes(entries, jax.random.fold_in(stream_key, 3), *heavy), -most, most).astype(kind)


def setup_inputs(seed: int = 0) -> dict:
    keys = jax.random.split(jax.random.key(seed), 13)
    tokens = scatter_about(keys[0], (NSEQ, LEN, D), 1.0, 6.0, ((0, 2), (1, 4)))
    segment_ids = draw_segment_ids(jax.random.fold_in(keys[12], 71), 0)
    norm_gain_1 = jnp.clip(1.0 + 0.15 * jax.random.normal(keys[2], (D,), jnp.float32), 0.25, 1.75)
    w_query = scatter_about(keys[3], (D, H * HD), D ** -0.5, 0.125, ((1, 4),))
    w_key = scatter_about(keys[4], (D, KVH * HD), D ** -0.5, 0.125, ((1, 4),))
    w_value = scatter_about(keys[5], (D, KVH * HD), D ** -0.5, 0.125, ((1, 4),))
    w_output = scatter_about(keys[6], (H * HD, D), (max(H * HD // 128, 1)) ** -0.5, 1.5, ((0, 4),))
    norm_gain_2 = jnp.clip(1.0 + 0.15 * jax.random.normal(keys[7], (D,), jnp.float32), 0.25, 1.75)
    w_gate = scatter_about(keys[8], (D, FF), D ** -0.5, 0.125, ((1, 4),))
    w_up = scatter_about(keys[9], (D, FF), D ** -0.5, 0.125, ((1, 4),))
    w_down = scatter_about(keys[10], (FF, D), FF ** -0.5, 0.078125, ((0, 4),))
    cotangent = heavy_noise(keys[11], (NSEQ, LEN, D), 1.0, 6.0, ((0, 2), (1, 4)), (1, 2, 4, 2.0))
    return {"tokens": tokens, "segment_ids": segment_ids, "norm_gain_1": norm_gain_1, "w_query": w_query, "w_key": w_key, "w_value": w_value, "w_output": w_output, "norm_gain_2": norm_gain_2, "w_gate": w_gate, "w_up": w_up, "w_down": w_down, "cotangent": cotangent}


@jax.custom_vjp
def low(v):
    return lax.optimization_barrier(v.astype(jnp.bfloat16)).astype(jnp.float32)

@jax.custom_vjp
def low_back(v):
    return v

def low_keep(v):
    return (low(v), None)

def low_pass(kept, grad):
    return (grad,)

def back_keep(v):
    return (v, None)

def back_low(kept, grad):
    return (low(grad),)
low.defvjp(low_keep, low_pass)
low_back.defvjp(back_keep, back_low)
EPSILON = 1e-05
EXACT = lax.Precision.HIGHEST

def matmul(left_side, right_side):
    return jnp.dot(left_side, right_side, precision=EXACT, preferred_element_type=jnp.float32)

def doc_positions(segment_ids):
    length = segment_ids.shape[-1]
    token_index = jnp.arange(length, dtype=jnp.int32)
    previous = jnp.concatenate([segment_ids[..., :1] - 1, segment_ids[..., :-1]], -1)
    starts = jnp.where(segment_ids != previous, token_index, 0)
    return token_index - lax.cummax(starts, axis=starts.ndim - 1)

def rope_tables(positions, head_size):
    half_width = head_size // 2
    frequency = 10000.0 ** (-(2.0 * jnp.arange(half_width, dtype=jnp.float32)) / head_size)
    angles = positions.astype(jnp.float32)[..., None] * frequency
    cos_half = jnp.cos(angles)
    sin_half = jnp.sin(angles)
    return (jnp.concatenate([cos_half, cos_half], -1), jnp.concatenate([sin_half, sin_half], -1))

def rotate(vectors, cos_table, sine_table):
    half_width = vectors.shape[-1] // 2
    turned = jnp.concatenate([-vectors[..., half_width:], vectors[..., :half_width]], -1)
    return vectors * cos_table + turned * sine_table

def layer_forward(stream, seg_row, gain_one, query_w, key_w, value_w, output_w, gain_two, gate_w, up_w, down_w):
    length = stream.shape[0]
    group_size = H // KVH
    token_index = jnp.arange(length, dtype=jnp.int32)
    cos_table, sine_table = rope_tables(doc_positions(seg_row), HD)
    allowed = (seg_row[None, :] == seg_row[:, None]) & (token_index[None, :] <= token_index[:, None])
    scale_one = lax.rsqrt(lax.optimization_barrier(jnp.mean(stream * stream, -1, keepdims=True)) + EPSILON)
    attn_in = low(stream * scale_one * gain_one)
    query_proj = low_back(matmul(attn_in, query_w)).reshape(length, H, HD)
    query_rot = low(rotate(query_proj, cos_table[:, None, :], sine_table[:, None, :]))
    key_proj = low_back(matmul(attn_in, key_w)).reshape(length, KVH, HD)
    key_rot = low(rotate(key_proj, cos_table[:, None, :], sine_table[:, None, :]))
    value_proj = low_back(low(matmul(attn_in, value_w))).reshape(length, KVH, HD)
    query_heads = query_rot.transpose(1, 0, 2)
    key_heads = jnp.repeat(key_rot.transpose(1, 0, 2), group_size, axis=0)
    value_heads = jnp.repeat(value_proj.transpose(1, 0, 2), group_size, axis=0)

    def one_head(head_item):
        query_one, key_one, value_one = head_item
        raw_scores = low_back(jnp.dot(query_one, key_one.T, precision=EXACT))
        attn_probs = jax.nn.softmax(jnp.where(allowed, raw_scores * HD ** (-0.5), -1e+30), axis=-1)
        return jnp.dot(low(attn_probs), value_one, precision=EXACT)
    attn_heads = lax.map(jax.checkpoint(one_head), (query_heads, key_heads, value_heads))
    attn_cat = low_back(low(attn_heads.transpose(1, 0, 2).reshape(length, H * HD)))
    residual = stream + low_back(matmul(attn_cat, output_w))
    scale_two = lax.rsqrt(lax.optimization_barrier(jnp.mean(residual * residual, -1, keepdims=True)) + EPSILON)
    mlp_in = low(residual * scale_two * gain_two)
    gate_pre = low_back(matmul(mlp_in, gate_w))
    up_proj = low_back(matmul(mlp_in, up_w))
    hidden = low(jax.nn.silu(gate_pre) * up_proj)
    return residual + matmul(hidden, down_w)

def reference(tokens, segment_ids, norm_gain_1, w_query, w_key, w_value, w_output, norm_gain_2, w_gate, w_up, w_down, cotangent):
    weight_list = tuple((entry.astype(jnp.float32) for entry in (norm_gain_1, w_query, w_key, w_value, w_output, norm_gain_2, w_gate, w_up, w_down)))

    def per_sequence(totals, seq_item):
        token_row, seg_row, grad_row = seq_item

        def closed(stream, *weights):
            return layer_forward(stream, seg_row, *weights)
        result, pullback = jax.vjp(closed, token_row.astype(jnp.float32), *weight_list)
        gradients = pullback(grad_row.astype(jnp.float32))
        totals = tuple((earlier + update for earlier, update in zip(totals, gradients[1:])))
        return (totals, (result.astype(jnp.bfloat16), gradients[0]))
    zero_grads = tuple((jnp.zeros_like(entry) for entry in weight_list))
    totals, (layer_out, grad_tokens) = lax.scan(per_sequence, zero_grads, (tokens, segment_ids, cotangent))
    return (layer_out, grad_tokens, totals[0], totals[1], totals[2], totals[3], totals[4], totals[5], totals[6], totals[7], totals[8])
```

```python
import functools

import jax
import jax.numpy as jnp
from jax import lax
from jax.experimental import pallas as pl
from jax.experimental.pallas import tpu as pltpu
from jax.sharding import PartitionSpec as P

EPSILON = 1e-05
BF16 = jnp.bfloat16
F32 = jnp.float32
FAR = 1e30
AUX = 8
ONES_AT = 5
BLOCK = 256


def params():
    return pltpu.CompilerParams(vmem_limit_bytes=56 * 2**20)


def dot(left, right, dims):
    return lax.dot_general(left, right, (dims, ((), ())), preferred_element_type=F32)


NN, NT, TN = ((1,), (0,)), ((1,), (1,)), ((0,), (0,))


def turn(rows, cos_rows, sine_rows, sign):
    half = rows.shape[0] // 2
    first, second = rows[:half], rows[half:]
    return jnp.concatenate(
        [first * cos_rows - sign * second * sine_rows, second * cos_rows + sign * first * sine_rows], 0
    )


def project_kernel(x_ref, gain_ref, wq_ref, wkv_ref, cos_ref, sin_ref, h_ref, q_ref, kv_ref):
    x = x_ref[...].astype(F32)
    scale = lax.rsqrt(jnp.mean(x * x, -1, keepdims=True) + EPSILON)
    h = (x * scale * gain_ref[...]).astype(BF16)
    h_ref[...] = h
    cos_rows, sine_rows = cos_ref[...], sin_ref[...]
    head = kv_ref.shape[0] // 2
    score_scale = head ** (-0.5)
    q = dot(h, wq_ref[...], NN).T
    for at in range(0, q.shape[0], head):
        q_ref[at : at + head] = (turn(q[at : at + head], cos_rows, sine_rows, 1.0) * score_scale).astype(BF16)
    kv = dot(h, wkv_ref[...], NN).T
    kv_ref[:head] = turn(kv[:head], cos_rows, sine_rows, 1.0).astype(BF16)
    kv_ref[head:] = kv[head:].astype(BF16)


def project(x, gain, w_query, w_kv, cos_rows, sine_rows):
    rows, width = x.shape
    step = min(rows, 256)
    wide, both = w_query.shape[1], w_kv.shape[1]
    half = cos_rows.shape[0]
    whole = lambda shape: pl.BlockSpec(shape, lambda i: (0, 0))
    return pl.pallas_call(
        project_kernel,
        grid=(rows // step,),
        in_specs=[
            pl.BlockSpec((step, width), lambda i: (i, 0)),
            whole((1, width)),
            whole((width, wide)),
            whole((width, both)),
            pl.BlockSpec((half, step), lambda i: (0, i)),
            pl.BlockSpec((half, step), lambda i: (0, i)),
        ],
        out_specs=[
            pl.BlockSpec((step, width), lambda i: (i, 0)),
            pl.BlockSpec((wide, step), lambda i: (0, i)),
            pl.BlockSpec((both, step), lambda i: (0, i)),
        ],
        out_shape=[
            jax.ShapeDtypeStruct((rows, width), BF16),
            jax.ShapeDtypeStruct((wide, rows), BF16),
            jax.ShapeDtypeStruct((both, rows), BF16),
        ],
        compiler_params=params(),
        cost_estimate=pl.CostEstimate(
            flops=2 * rows * width * (wide + both), bytes_accessed=4 * rows * width + 2 * width * (wide + both), transcendentals=0
        ),
    )(x, gain, w_query, w_kv, cos_rows, sine_rows)


def pieces(value):
    high = value.astype(BF16).astype(F32)
    middle = (value - high).astype(BF16).astype(F32)
    low = value - high - middle
    return high, middle, low


def key_rows(kv, seg):
    head, count = kv.shape[0] // 2, kv.shape[1]
    row = lax.broadcasted_iota(jnp.int32, (2 * AUX, count), 0)
    extra = jnp.where(row < ONES_AT, jnp.where(seg == row, 0.0, -FAR), jnp.where(row < AUX, 1.0, 0.0))
    rest = jnp.zeros((head - 2 * AUX, count), F32)
    return jnp.concatenate([kv[:head].astype(F32), extra, rest], 0)


def value_rows(kv, fill):
    head, count = kv.shape[0] // 2, kv.shape[1]
    row = lax.broadcasted_iota(jnp.int32, (fill, count), 0)
    return jnp.concatenate([kv[head:].astype(F32), jnp.where(row < 3, 1.0, 0.0)], 0)


def causal(scores):
    key_at = lax.broadcasted_iota(jnp.int32, scores.shape, 0)
    query_at = lax.broadcasted_iota(jnp.int32, scores.shape, 1)
    return jnp.where(key_at <= query_at, scores, -FAR)


def attend_kernel(far_count, at_ref, q_ref, seg_ref, *refs):
    kv_refs = refs[: far_count + 1]
    qa_ref, o_ref, full_ref = refs[far_count + 1 : far_count + 4]
    ka_ref, va_ref, m_ref, acc_ref = refs[far_count + 4 :]
    me = at_ref[0]
    head, count = q_ref.shape

    @pl.when(pl.program_id(0) == 0)
    def _():
        for d, kv_ref in enumerate(kv_refs):
            kv = kv_ref[...]
            ka_ref[d] = key_rows(kv, seg_ref[d : d + 1]).T.astype(BF16)
            va_ref[d] = value_rows(kv, 2 * AUX).astype(BF16)

    row = lax.broadcasted_iota(jnp.int32, (2 * AUX, count), 0)
    same = jnp.where((seg_ref[0:1] == row) & (row < ONES_AT), 1.0, 0.0)
    q = q_ref[...].astype(F32)
    rest = jnp.zeros((head - 2 * AUX, count), F32)
    qa = jnp.concatenate([q, same, rest], 0).astype(BF16)

    scores = causal(dot(ka_ref[0], qa, NN))
    m = jnp.max(scores, 0, keepdims=True)
    probs = jnp.exp(scores - m).astype(BF16)
    m_ref[...] = m
    acc_ref[...] = dot(va_ref[0], probs, NN)
    for d in range(1, far_count + 1):

        @pl.when(d <= me)
        def _(d=d):
            scores = dot(ka_ref[d], qa, NN)
            before = m_ref[...]
            m = jnp.maximum(before, jnp.max(scores, 0, keepdims=True))
            probs = jnp.exp(scores - m).astype(BF16)
            m_ref[...] = m
            acc_ref[...] = acc_ref[...] * jnp.exp(before - m) + dot(va_ref[d], probs, NN)

    acc = acc_ref[...]
    total = acc[head : head + 1]
    out = acc[:head] / total
    full_ref[...] = out
    o_ref[...] = out.astype(BF16)
    high, middle, low = pieces(-(m_ref[...] + jnp.log(total)))
    extra = jnp.where(
        row == ONES_AT, high, jnp.where(row == ONES_AT + 1, middle, jnp.where(row == ONES_AT + 2, low, same))
    )
    qa_ref[...] = jnp.concatenate([q, extra, rest], 0).astype(BF16)


def attend(me, q, kvs, segs, item):
    far_count = len(kvs) - 1
    both = kvs[0].shape[0]
    head = both // 2
    wide, count = q.shape[0], segs.shape[-1]
    heads = wide // head
    return pl.pallas_call(
        functools.partial(attend_kernel, far_count),
        grid_spec=pltpu.PrefetchScalarGridSpec(
            num_scalar_prefetch=1,
            grid=(heads,),
            in_specs=[
                pl.BlockSpec((head, count), lambda h, at: (h, item)),
                pl.BlockSpec((None, far_count + 1, count), lambda h, at: (item, 0, 0)),
            ]
            + [pl.BlockSpec((both, count), lambda h, at: (0, item))] * (far_count + 1),
            out_specs=[
                pl.BlockSpec((None, both, count), lambda h, at: (h, 0, 0)),
                pl.BlockSpec((head, count), lambda h, at: (h, 0)),
                pl.BlockSpec((head, count), lambda h, at: (h, 0)),
            ],
            scratch_shapes=[
                pltpu.VMEM((far_count + 1, count, both), BF16),
                pltpu.VMEM((far_count + 1, head + 2 * AUX, count), BF16),
                pltpu.VMEM((1, count), F32),
                pltpu.VMEM((head + 2 * AUX, count), F32),
            ],
        ),
        out_shape=[
            jax.ShapeDtypeStruct((heads, both, count), BF16),
            jax.ShapeDtypeStruct((wide, count), BF16),
            jax.ShapeDtypeStruct((wide, count), F32),
        ],
        compiler_params=params(),
        cost_estimate=pl.CostEstimate(
            flops=16 * wide * count * count * (far_count + 1), bytes_accessed=12 * wide * count, transcendentals=0
        ),
    )(me, q, segs, *kvs)


def back_kernel(far_count, at_ref, qa_ref, do_ref, full_ref, seg_ref, cos_ref, sin_ref, *refs):
    kv_refs = refs[: far_count + 1]
    dq_ref = refs[far_count + 1]
    out_refs = refs[far_count + 2 : 2 * far_count + 3]
    ka_ref, kt_ref, va_ref, dk_ref, dv_ref, dq_acc = refs[2 * far_count + 3 :]
    me = at_ref[0]
    head, count = do_ref.shape
    step = pl.program_id(0)

    @pl.when(step == 0)
    def _():
        for d, kv_ref in enumerate(kv_refs):
            kv = kv_ref[...]
            ka_ref[d] = key_rows(kv, seg_ref[d : d + 1]).T.astype(BF16)
            kt_ref[d] = kv[:head]
            va_ref[d] = value_rows(kv, head).T.astype(BF16)
        dk_ref[...] = jnp.zeros_like(dk_ref)
        dv_ref[...] = jnp.zeros_like(dv_ref)

    qa = qa_ref[...]
    do = do_ref[...].astype(F32)
    high, middle, low = pieces(-jnp.sum(do * full_ref[...], 0, keepdims=True))
    row = lax.broadcasted_iota(jnp.int32, (2 * AUX, count), 0)
    extra = jnp.where(row == 0, high, jnp.where(row == 1, middle, jnp.where(row == 2, low, 0.0)))
    rest = jnp.zeros((head - 2 * AUX, count), F32)
    da = jnp.concatenate([do, extra, rest], 0).astype(BF16)
    for d in range(far_count + 1):

        def part(d=d):
            scores = dot(ka_ref[d], qa, NN)
            probs = jnp.exp(causal(scores) if d == 0 else scores)
            d_scores = (probs * dot(va_ref[d], da, NN)).astype(BF16)
            dv_ref[d] += dot(probs.astype(BF16), da[:head], NT)
            dk_ref[d] += dot(d_scores, qa[:head], NT)
            update = dot(kt_ref[d], d_scores, NN)
            if d == 0:
                dq_acc[...] = update
            else:
                dq_acc[...] += update

        if d == 0:
            part()
        else:
            pl.when(d <= me)(part)
    score_scale = head ** (-0.5)
    dq_ref[...] = turn(dq_acc[...] * score_scale, cos_ref[...], sin_ref[...], -1.0).astype(BF16)

    @pl.when(step == pl.num_programs(0) - 1)
    def _():
        for d, out_ref in enumerate(out_refs):
            out_ref[...] = jnp.concatenate([dk_ref[d], dv_ref[d]], 1).T.astype(out_ref.dtype)


def attend_back(me, qa, do, full, kvs, segs, cos_rows, sine_rows, item):
    far_count = len(kvs) - 1
    heads, both, count = qa.shape
    head = both // 2
    wide, half = heads * head, cos_rows.shape[0]
    return pl.pallas_call(
        functools.partial(back_kernel, far_count),
        grid_spec=pltpu.PrefetchScalarGridSpec(
            num_scalar_prefetch=1,
            grid=(heads,),
            in_specs=[
                pl.BlockSpec((None, both, count), lambda h, at: (h, 0, 0)),
                pl.BlockSpec((head, count), lambda h, at: (h, 0)),
                pl.BlockSpec((head, count), lambda h, at: (h, 0)),
                pl.BlockSpec((None, far_count + 1, count), lambda h, at: (item, 0, 0)),
                pl.BlockSpec((half, count), lambda h, at: (0, item)),
                pl.BlockSpec((half, count), lambda h, at: (0, item)),
            ]
            + [pl.BlockSpec((both, count), lambda h, at: (0, item))] * (far_count + 1),
            out_specs=[pl.BlockSpec((head, count), lambda h, at: (h, 0))]
            + [pl.BlockSpec((both, count), lambda h, at: (0, 0))] * (far_count + 1),
            scratch_shapes=[
                pltpu.VMEM((far_count + 1, count, both), BF16),
                pltpu.VMEM((far_count + 1, head, count), BF16),
                pltpu.VMEM((far_count + 1, count, both), BF16),
                pltpu.VMEM((far_count + 1, count, head), F32),
                pltpu.VMEM((far_count + 1, count, head), F32),
                pltpu.VMEM((head, count), F32),
            ],
        ),
        out_shape=[jax.ShapeDtypeStruct((wide, count), BF16), jax.ShapeDtypeStruct((both, count), F32)]
        + [jax.ShapeDtypeStruct((both, count), BF16)] * far_count,
        compiler_params=params(),
        cost_estimate=pl.CostEstimate(
            flops=40 * wide * count * count * (far_count + 1), bytes_accessed=12 * wide * count, transcendentals=0
        ),
    )(me, qa, do, full, segs, cos_rows, sine_rows, *kvs)


def grad_kernel(count, form, has_recv, split, *refs):
    refs = refs[1:]
    lefts, rights = refs[:count], refs[count : 2 * count]
    at = 2 * count
    total = None
    for left, right in zip(lefts, rights):
        term = dot(left[...], right[...], form)
        total = term if total is None else total + term
    if has_recv:
        total = total + refs[at][...].astype(F32)
        at += 1
    if not split:
        refs[at][...] = total.astype(BF16)
        return
    send, keep = refs[at], refs[at + 1]
    first = pl.program_id(0) < split

    @pl.when(first)
    def _():
        send[...] = total.astype(BF16)

    @pl.when(jnp.logical_not(first))
    def _():
        keep[...] = total.astype(BF16)


def grad_blocks(table, wide_set, narrow_set, natural, recv=None, split=0):
    n = table.shape[0]
    count = len(wide_set)
    tokens, width = wide_set[0].shape
    blk = BLOCK
    wide_spec = pl.BlockSpec((tokens, blk), lambda i, t: (0, t[i]))
    narrow_spec = [pl.BlockSpec(a.shape, lambda i, t: (0, 0)) for a in narrow_set]
    if natural:
        ins, specs, form = list(wide_set) + list(narrow_set), [wide_spec] * count + narrow_spec, TN
        block = (blk, narrow_set[0].shape[1])
    else:
        ins, specs, form = list(narrow_set) + list(wide_set), narrow_spec + [wide_spec] * count, NN
        block = (narrow_set[0].shape[0], blk)
    full = (None,) + block
    if recv is not None:
        ins.append(recv)
        specs.append(pl.BlockSpec(full, lambda i, t: (lax.rem(i + split, n), 0, 0)))
    if split:
        out_specs = [
            pl.BlockSpec(full, lambda i, t: (jnp.minimum(i, split - 1), 0, 0)),
            pl.BlockSpec(full, lambda i, t: (jnp.maximum(i - split, 0), 0, 0)),
        ]
        out_shape = [jax.ShapeDtypeStruct((split,) + block, BF16), jax.ShapeDtypeStruct((n - split,) + block, BF16)]
    else:
        out_specs = pl.BlockSpec(full, lambda i, t: (i, 0, 0))
        out_shape = jax.ShapeDtypeStruct((n,) + block, BF16)
    size = n * block[0] * block[1]
    return pl.pallas_call(
        functools.partial(grad_kernel, count, form, recv is not None, split),
        grid_spec=pltpu.PrefetchScalarGridSpec(
            num_scalar_prefetch=1, grid=(n,), in_specs=specs, out_specs=out_specs
        ),
        out_shape=out_shape,
        compiler_params=params(),
        cost_estimate=pl.CostEstimate(
            flops=2 * count * tokens * size, bytes_accessed=2 * size, transcendentals=0
        ),
    )(table, *ins)


class Scatter:
    def __init__(self, stages, sizes):
        self.stages, self.sizes = stages, sizes
        ctx, dp = lax.axis_index("context"), lax.axis_index("dp")
        blocks = []
        for p in range(2 ** len(stages)):
            c, d = ctx, dp
            for j, (axis, bit) in enumerate(stages):
                if p >> (len(stages) - 1 - j) & 1:
                    if axis == "context":
                        c = c ^ (1 << bit)
                    else:
                        d = d ^ (1 << bit)
            blocks.append(c * sizes["dp"] + d)
        self.table = jnp.stack(blocks).astype(jnp.int32)

    def swap(self, j, x):
        axis, bit = self.stages[j]
        return lax.ppermute(x, axis, [(i, i ^ (1 << bit)) for i in range(self.sizes[axis])])

    def run(self, wide_set, narrow_set, natural):
        n = self.table.shape[0]
        theirs = grad_blocks(self.table[n // 2 :], wide_set, narrow_set, natural)
        recv = self.swap(0, theirs)
        half = n // 2
        order = jnp.concatenate([self.table[half // 2 : half], self.table[: half // 2]])
        send, keep = grad_blocks(order, wide_set, narrow_set, natural, recv, half // 2)
        for j in range(1, len(self.stages)):
            recv = self.swap(j, send)
            if j == len(self.stages) - 1:
                return (keep.astype(F32) + recv.astype(F32))[0]
            half = keep.shape[0] // 2
            total = keep.astype(F32) + recv.astype(F32)
            send, keep = total[half:].astype(BF16), total[:half]


def swap(x, axis, size, bit):
    return lax.ppermute(x, axis, [(i, i ^ (1 << bit)) for i in range(size)])


def rows_at(x, at, count):
    return lax.dynamic_slice_in_dim(x, at, count, 0)


def local(sizes, tokens, segment_ids, norm_gain_1, w_query, w_key, w_value, w_output, norm_gain_2, w_gate, w_up, w_down, cotangent):
    seqs, stretch, width = tokens.shape
    length = segment_ids.shape[1]
    rows = seqs * stretch
    head = w_key.shape[1]
    n_tensor, n_context, n_dp = sizes["tensor"], sizes["context"], sizes["dp"]
    me_t, me_c = lax.axis_index("tensor"), lax.axis_index("context")
    core, high = me_t % 2, me_t // 2
    half, quarter = stretch // 2, stretch // 4
    offset = me_c * stretch

    seg_here = lax.dynamic_slice_in_dim(segment_ids, offset, stretch, 1)
    start = jnp.zeros(seg_here.shape, jnp.int32)
    for number in range(1, ONES_AT):
        before = jnp.sum((segment_ids < number).astype(jnp.int32), 1, keepdims=True)
        start = jnp.where(seg_here == number, before, start)
    positions = (offset + jnp.arange(stretch, dtype=jnp.int32))[None, :] - start
    frequency = 10000.0 ** (-(2.0 * jnp.arange(head // 2, dtype=F32)) / head)
    angles = frequency[:, None] * positions.reshape(1, rows).astype(F32)
    cos_rows, sine_rows = jnp.cos(angles), jnp.sin(angles)
    padded = jnp.concatenate([jnp.zeros((seqs, (n_context - 1) * stretch), jnp.int32), segment_ids], 1)
    segs = jnp.stack(
        [
            lax.dynamic_slice_in_dim(padded, offset + (n_context - 1 - d) * stretch, stretch, 1)
            for d in range(n_context)
        ],
        1,
    )
    at = jnp.reshape(me_c, (1,)).astype(jnp.int32)

    x_rows = tokens.reshape(rows, width)
    ct_rows = cotangent.reshape(rows, width)
    gain_1, gain_2 = norm_gain_1.reshape(1, width), norm_gain_2.reshape(1, width)
    w_kv = jnp.concatenate([w_key, w_value], 1)
    h1, q_t, kv_t = project(x_rows, gain_1, w_query, w_kv, cos_rows, sine_rows)
    kvs = [kv_t] + [
        lax.ppermute(kv_t, "context", [(i, i + d) for i in range(n_context - d)]) for d in range(1, n_context)
    ]
    d_hidden = [dot(ct_rows[s * stretch : (s + 1) * stretch], w_down, NT) for s in range(seqs)]

    def scatter(make):
        theirs = make((1 - core) * half, half).astype(BF16)
        got = swap(theirs, "tensor", n_tensor, 0)
        mine = make(core * half, half) + got.astype(F32)
        away = rows_at(mine, (1 - high) * quarter, quarter).astype(BF16)
        got = swap(away, "tensor", n_tensor, 1)
        return rows_at(mine, high * quarter, quarter) + got.astype(F32)

    def gather(part):
        got = swap(part, "tensor", n_tensor, 1)
        block = jnp.zeros((half, width), part.dtype)
        block = lax.dynamic_update_slice(block, part, (high * quarter, 0))
        block = lax.dynamic_update_slice(block, got, ((1 - high) * quarter, 0))
        got = swap(block, "tensor", n_tensor, 0)
        full = jnp.zeros((stretch, width), part.dtype)
        full = lax.dynamic_update_slice(full, block, (core * half, 0))
        return lax.dynamic_update_slice(full, got, ((1 - core) * half, 0))

    def quarter_of(x, s):
        return rows_at(x, s * stretch + core * half + high * quarter, quarter)

    seq = []
    for s in range(seqs):
        qa, o_t, full_o = attend(at, q_t, kvs, segs, s)
        part = scatter(
            lambda start, count: dot(lax.dynamic_slice_in_dim(o_t, start, count, 1), w_output, TN)
        )
        residual = quarter_of(x_rows, s).astype(F32) + part
        scale_2 = lax.rsqrt(jnp.mean(residual * residual, -1, keepdims=True) + EPSILON)
        normed_2 = residual * scale_2
        h2 = gather((normed_2 * gain_2).astype(BF16))
        seq.append(dict(qa=qa, o_t=o_t, full_o=full_o, residual=residual, scale_2=scale_2, normed_2=normed_2, h2=h2))
    for s in range(seqs):
        item = seq[s]
        gate = dot(item["h2"], w_gate, NN)
        up = dot(item["h2"], w_up, NN)
        sig = jax.nn.sigmoid(gate)
        item["hidden"] = (gate * sig * up).astype(BF16)
        item["d_gate"] = (d_hidden[s] * up * sig * (1.0 + gate * (1.0 - sig))).astype(BF16)
        item["d_up"] = (d_hidden[s] * gate * sig).astype(BF16)

    of = lambda name: [item[name] for item in seq]
    cts = [ct_rows[s * stretch : (s + 1) * stretch] for s in range(seqs)]
    blocks = n_context * n_dp
    fast = width // blocks == BLOCK and n_dp == 2 and n_context == 4
    if fast:
        x_first = Scatter([("dp", 0), ("context", 0), ("context", 1)], sizes)
        z_first = Scatter([("context", 0), ("dp", 0), ("context", 1)], sizes)
        down_sum = x_first.run(cts, of("hidden"), True).T
        gate_sum = x_first.run(of("h2"), of("d_gate"), True)
        up_sum = x_first.run(of("h2"), of("d_up"), True)
    else:

        def plain(left, right, dim):
            total = sum(dot(a, b, TN) for a, b in zip(left, right))
            return lax.psum_scatter(
                total.astype(BF16), ("context", "dp"), scatter_dimension=dim, tiled=True
            ).astype(F32)

        down_sum = plain(of("hidden"), cts, 1)
        gate_sum = plain(of("h2"), of("d_gate"), 0)
        up_sum = plain(of("h2"), of("d_up"), 0)

    for s in range(seqs):
        item = seq[s]
        back = scatter(
            lambda start, count: dot(rows_at(item["d_gate"], start, count), w_gate, NT)
            + dot(rows_at(item["d_up"], start, count), w_up, NT)
        )
        item["gain"] = jnp.sum(back * item["normed_2"], 0)
        scaled = back * gain_2
        item["d_res"] = quarter_of(ct_rows, s).astype(F32) + item["scale_2"] * (
            scaled - item["normed_2"] * jnp.mean(scaled * item["normed_2"], -1, keepdims=True)
        )
        item["d_low"] = gather(item["d_res"].astype(BF16))
        part = scatter(lambda start, count: dot(rows_at(item["hidden"], start, count), w_down, NN))
        item["out"] = gather((item["residual"] + part).astype(BF16))

    for s in range(seqs):
        item = seq[s]
        do_t = dot(w_output, item["d_low"], NT).astype(BF16)
        item["dq_t"], *item["dkvs"] = attend_back(
            at, item["qa"], do_t, item["full_o"], kvs, segs, cos_rows, sine_rows, s
        )
    dkv = jnp.concatenate([item["dkvs"][0] for item in seq], 1)
    for d in range(1, n_context):
        sent = jnp.concatenate([item["dkvs"][d] for item in seq], 1)
        dkv = dkv + lax.ppermute(sent, "context", [(i + d, i) for i in range(n_context - d)]).astype(F32)
    dkv_t = jnp.concatenate([turn(dkv[:head], cos_rows, sine_rows, -1.0), dkv[head:]], 0).astype(BF16)
    for s in range(seqs):
        item = seq[s]
        item["dqkv_t"] = jnp.concatenate([item["dq_t"], dkv_t[:, s * stretch : (s + 1) * stretch]], 0)
        item["h1"] = h1[s * stretch : (s + 1) * stretch]
    wide = w_query.shape[1]
    if fast:
        output_sum = z_first.run(of("d_low"), of("o_t"), False)
        mixed = z_first.run(of("h1"), of("dqkv_t"), False).T
    else:
        output_sum = lax.psum_scatter(
            sum(dot(a, b, NN) for a, b in zip(of("o_t"), of("d_low"))).astype(BF16),
            ("context", "dp"), scatter_dimension=1, tiled=True,
        ).astype(F32)
        mixed = lax.psum_scatter(
            sum(dot(b, a, NN).T for a, b in zip(of("h1"), of("dqkv_t"))).astype(BF16),
            ("context", "dp"), scatter_dimension=0, tiled=True,
        ).astype(F32)
    query_sum, key_sum, value_sum = mixed[:, :wide], mixed[:, wide : wide + head], mixed[:, wide + head :]

    w_all = jnp.concatenate([w_query, w_kv], 1)
    gains = []
    for s in range(seqs):
        item = seq[s]
        back = scatter(
            lambda start, count: dot(
                lax.dynamic_slice_in_dim(item["dqkv_t"], start, count, 1), w_all, ((0,), (1,))
            )
        )
        stream = quarter_of(x_rows, s).astype(F32)
        scale_1 = lax.rsqrt(jnp.mean(stream * stream, -1, keepdims=True) + EPSILON)
        normed_1 = stream * scale_1
        gains.append(jnp.sum(back * normed_1, 0))
        scaled = back * gain_1
        grad = item["d_res"] + scale_1 * (scaled - normed_1 * jnp.mean(scaled * normed_1, -1, keepdims=True))
        item["grad"] = gather(grad.astype(BF16))
    layer_out = jnp.stack(of("out"))
    grad_tokens = jnp.stack(of("grad")).astype(F32)

    gain_sum = jnp.stack([sum(gains), sum(of("gain"))])
    for axis in ("tensor", "context", "dp"):
        bit = 0
        while 1 << bit < sizes[axis]:
            gain_sum = gain_sum + swap(gain_sum, axis, sizes[axis], bit)
            bit += 1
    per = width // blocks
    gain_sum = lax.dynamic_slice_in_dim(gain_sum, (me_c * n_dp + lax.axis_index("dp")) * per, per, 1)
    return (
        layer_out,
        grad_tokens,
        gain_sum[0],
        query_sum,
        key_sum,
        value_sum,
        output_sum,
        gain_sum[1],
        gate_sum,
        up_sum,
        down_sum,
    )


def solution(mesh):
    in_specs = (
        P("dp", "context", None),
        P("dp", None),
        P(),
        P(None, "tensor"),
        P(None, "tensor"),
        P(None, "tensor"),
        P("tensor", None),
        P(),
        P(None, "tensor"),
        P(None, "tensor"),
        P("tensor", None),
        P("dp", "context", None),
    )
    out_specs = (
        P("dp", "context", None),
        P("dp", "context", None),
        P(("context", "dp")),
        P(("context", "dp"), "tensor"),
        P(("context", "dp"), "tensor"),
        P(("context", "dp"), "tensor"),
        P("tensor", ("context", "dp")),
        P(("context", "dp")),
        P(("context", "dp"), "tensor"),
        P(("context", "dp"), "tensor"),
        P("tensor", ("context", "dp")),
    )
    run = functools.partial(local, dict(mesh.shape))
    return jax.shard_map(run, mesh=mesh, in_specs=in_specs, out_specs=out_specs, check_vma=False)
```

```python
import functools

import jax
import jax.numpy as jnp
from jax import lax
from jax.experimental import pallas as pl
from jax.experimental.pallas import tpu as pltpu
from jax.sharding import PartitionSpec as P

EPSILON = 1e-05
BF16 = jnp.bfloat16
F32 = jnp.float32
FAR = 1e30
AUX = 8
ONES_AT = 5
BLOCK = 256


COST = pl.CostEstimate(flops=1024, bytes_accessed=1024, transcendentals=0)


def params():
    return pltpu.CompilerParams(vmem_limit_bytes=56 * 2**20)


def dot(left, right, dims):
    return lax.dot_general(left, right, (dims, ((), ())), preferred_element_type=F32)


NN, NT, TN, TT = ((1,), (0,)), ((1,), (1,)), ((0,), (0,)), ((0,), (1,))


def turn(rows, cos_rows, sine_rows, sign):
    half = rows.shape[0] // 2
    first, second = rows[:half], rows[half:]
    return jnp.concatenate(
        [first * cos_rows - sign * second * sine_rows, second * cos_rows + sign * first * sine_rows], 0
    )


def project_kernel(at_ref, x_ref, gain_ref, wq_ref, wkv_ref, cos_ref, sin_ref, h_ref, q_ref, kv_ref):
    x = x_ref[...].astype(F32)
    scale = lax.rsqrt(jnp.mean(x * x, -1, keepdims=True) + EPSILON)
    h = (x * scale * gain_ref[...]).astype(BF16)
    part = h.shape[0] // 2
    swapped = at_ref[2] * part
    h_ref[pl.ds(pl.multiple_of(swapped, part), part)] = h[:part]
    h_ref[pl.ds(pl.multiple_of(part - swapped, part), part)] = h[part:]
    cos_rows, sine_rows = cos_ref[...], sin_ref[...]
    head = kv_ref.shape[0] // 2
    score_scale = head ** (-0.5)
    q = dot(h, wq_ref[...], NN).T
    for at in range(0, q.shape[0], head):
        q_ref[at : at + head] = (turn(q[at : at + head], cos_rows, sine_rows, 1.0) * score_scale).astype(BF16)
    kv = dot(wkv_ref[...], h, NT)
    kv_ref[:head] = turn(kv[:head], cos_rows, sine_rows, 1.0).astype(BF16)
    kv_ref[head:] = kv[head:].astype(BF16)


def project(at, x, gain, w_query, w_kv, cos_rows, sine_rows, stretch):
    rows, width = x.shape
    step = stretch // 2
    wide, both = w_query.shape[1], w_kv.shape[0]
    half = cos_rows.shape[0]
    whole = lambda shape: pl.BlockSpec(shape, lambda i, at: (0, 0))
    return pl.pallas_call(
        project_kernel,
        grid_spec=pltpu.PrefetchScalarGridSpec(
            num_scalar_prefetch=1,
            grid=(rows // step,),
            in_specs=[
                pl.BlockSpec((step, width), lambda i, at: (i, 0)),
                whole((1, width)),
                whole((width, wide)),
                whole((both, width)),
                pl.BlockSpec((half, step), lambda i, at: (0, i)),
                pl.BlockSpec((half, step), lambda i, at: (0, i)),
            ],
            out_specs=[
                pl.BlockSpec((step, width), lambda i, at: (i + at[1] - 2 * at[1] * lax.rem(i, 2), 0)),
                pl.BlockSpec((wide, step), lambda i, at: (0, i)),
                pl.BlockSpec((both, step), lambda i, at: (0, i)),
            ],
        ),
        out_shape=[
            jax.ShapeDtypeStruct((rows, width), BF16),
            jax.ShapeDtypeStruct((wide, rows), BF16),
            jax.ShapeDtypeStruct((both, rows), BF16),
        ],
        compiler_params=params(),
        cost_estimate=COST,
    )(at, x, gain, w_query, w_kv, cos_rows, sine_rows)


def pieces(value):
    high = value.astype(BF16).astype(F32)
    middle = (value - high).astype(BF16).astype(F32)
    low = value - high - middle
    return high, middle, low


def key_rows(kv, seg):
    head, count = kv.shape[0] // 2, kv.shape[1]
    row = lax.broadcasted_iota(jnp.int32, (2 * AUX, count), 0)
    extra = jnp.where(row < ONES_AT, jnp.where(seg == row, 0.0, -FAR), jnp.where(row < AUX, 1.0, 0.0))
    rest = jnp.zeros((head - 2 * AUX, count), F32)
    return jnp.concatenate([kv[:head].astype(F32), extra, rest], 0)


def value_rows(kv, fill):
    head, count = kv.shape[0] // 2, kv.shape[1]
    row = lax.broadcasted_iota(jnp.int32, (fill, count), 0)
    return jnp.concatenate([kv[head:].astype(F32), jnp.where(row < 3, 1.0, 0.0)], 0)


def places(at_ref, count):
    quarter = count // 4
    mine = 2 * at_ref[1] + at_ref[2]
    return [pl.ds(pl.multiple_of((b ^ mine) * quarter, quarter), quarter) for b in range(4)]


def causal(scores):
    key_at = lax.broadcasted_iota(jnp.int32, scores.shape, 0)
    query_at = lax.broadcasted_iota(jnp.int32, scores.shape, 1)
    return jnp.where(key_at <= query_at, scores, -FAR)


def attend_kernel(far_count, at_ref, q_ref, seg_ref, *refs):
    kv_refs = refs[: far_count + 1]
    qa_ref, o_ref, full_ref = refs[far_count + 1 : far_count + 4]
    ka_ref, va_ref = refs[far_count + 4 :]
    me = at_ref[0]
    head = kv_refs[0].shape[0] // 2
    count = q_ref.shape[1]

    @pl.when(pl.program_id(0) == 0)
    def _():
        for d, kv_ref in enumerate(kv_refs):
            kv = kv_ref[...]
            ka_ref[d] = key_rows(kv, seg_ref[d : d + 1]).T.astype(BF16)
            va_ref[d] = value_rows(kv, 2 * AUX).astype(BF16)

    row = lax.broadcasted_iota(jnp.int32, (2 * AUX, count), 0)
    same = jnp.where((seg_ref[0:1] == row) & (row < ONES_AT), 1.0, 0.0)
    rest = jnp.zeros((head - 2 * AUX, count), F32)

    def heads(blocks):
        for h in range(q_ref.shape[0] // head):
            q = q_ref[h * head : (h + 1) * head].astype(F32)
            qa = jnp.concatenate([q, same, rest], 0).astype(BF16)
            scores = [dot(ka_ref[d], qa, NN) for d in range(blocks)]
            scores[0] = causal(scores[0])
            m = jnp.max(scores[0], 0, keepdims=True)
            for d in range(1, blocks):
                m = jnp.maximum(m, jnp.max(scores[d], 0, keepdims=True))
            acc = None
            for d in range(blocks):
                term = dot(va_ref[d], jnp.exp(scores[d] - m).astype(BF16), NN)
                acc = term if acc is None else acc + term
            total = acc[head : head + 1]
            out = acc[:head] / total
            for b, place in enumerate(places(at_ref, count)):
                quarter = out[:, b * (count // 4) : (b + 1) * (count // 4)]
                full_ref[h * head : (h + 1) * head, place] = quarter
                o_ref[h * head : (h + 1) * head, place] = quarter.astype(BF16)
            high, middle, low = pieces(-(m + jnp.log(total)))
            extra = jnp.where(
                row == ONES_AT, high, jnp.where(row == ONES_AT + 1, middle, jnp.where(row == ONES_AT + 2, low, same))
            )
            qa_ref[h] = jnp.concatenate([q, extra, rest], 0).astype(BF16)

    for blocks in range(1, far_count + 2):
        pl.when(me == blocks - 1)(functools.partial(heads, blocks))


def attend(me, q, kvs, segs, item, group=2):
    far_count = len(kvs) - 1
    both = kvs[0].shape[0]
    head = both // 2
    wide, count = q.shape[0], segs.shape[-1]
    heads = wide // head
    return pl.pallas_call(
        functools.partial(attend_kernel, far_count),
        grid_spec=pltpu.PrefetchScalarGridSpec(
            num_scalar_prefetch=1,
            grid=(heads // group,),
            in_specs=[
                pl.BlockSpec((group * head, count), lambda h, at: (h, item)),
                pl.BlockSpec((None, far_count + 1, count), lambda h, at: (item, 0, 0)),
            ]
            + [pl.BlockSpec((both, count), lambda h, at: (0, item))] * (far_count + 1),
            out_specs=[
                pl.BlockSpec((group, both, count), lambda h, at: (h, 0, 0)),
                pl.BlockSpec((group * head, count), lambda h, at: (h, 0)),
                pl.BlockSpec((group * head, count), lambda h, at: (h, 0)),
            ],
            scratch_shapes=[
                pltpu.VMEM((far_count + 1, count, both), BF16),
                pltpu.VMEM((far_count + 1, head + 2 * AUX, count), BF16),
            ],
        ),
        out_shape=[
            jax.ShapeDtypeStruct((heads, both, count), BF16),
            jax.ShapeDtypeStruct((wide, count), BF16),
            jax.ShapeDtypeStruct((wide, count), F32),
        ],
        compiler_params=params(),
        cost_estimate=COST,
    )(me, q, segs, *kvs)


def back_kernel(far_count, at_ref, qa_ref, do_ref, full_ref, seg_ref, cos_ref, sin_ref, *refs):
    kv_refs = refs[: far_count + 1]
    dq_ref, keep_ref, send_ref = refs[far_count + 1 : far_count + 4]
    ka_ref, kt_ref, va_ref, dk_ref, dv_ref, dq_acc = refs[far_count + 4 :]
    me = at_ref[0]
    head, count = do_ref.shape
    step = pl.program_id(0)

    @pl.when(step == 0)
    def _():
        for d, kv_ref in enumerate(kv_refs):
            kv = kv_ref[...]
            ka_ref[d] = key_rows(kv, seg_ref[d : d + 1]).T.astype(BF16)
            kt_ref[d] = kv[:head]
            va_ref[d] = value_rows(kv, head).T.astype(BF16)
        dk_ref[...] = jnp.zeros_like(dk_ref)
        dv_ref[...] = jnp.zeros_like(dv_ref)

    qa = qa_ref[...]
    here = places(at_ref, count)
    do = jnp.concatenate([do_ref[:, place] for place in here], 1).astype(F32)
    full = jnp.concatenate([full_ref[:, place] for place in here], 1)
    high, middle, low = pieces(-jnp.sum(do * full, 0, keepdims=True))
    row = lax.broadcasted_iota(jnp.int32, (2 * AUX, count), 0)
    extra = jnp.where(row == 0, high, jnp.where(row == 1, middle, jnp.where(row == 2, low, 0.0)))
    rest = jnp.zeros((head - 2 * AUX, count), F32)
    da = jnp.concatenate([do, extra, rest], 0).astype(BF16)
    for d in range(far_count + 1):

        def part(d=d):
            scores = dot(ka_ref[d], qa, NN)
            probs = jnp.exp(causal(scores) if d == 0 else scores)
            d_scores = (probs * dot(va_ref[d], da, NN)).astype(BF16)
            dv_ref[d] += dot(probs.astype(BF16), da[:head], NT)
            dk_ref[d] += dot(d_scores, qa[:head], NT)
            update = dot(kt_ref[d], d_scores, NN)
            if d == 0:
                dq_acc[...] = update
            else:
                dq_acc[...] += update

        if d == 0:
            part()
        else:
            pl.when(d <= me)(part)
    score_scale = head ** (-0.5)
    dq = turn(dq_acc[...] * score_scale, cos_ref[...], sin_ref[...], -1.0).astype(BF16)
    for b, place in enumerate(here):
        dq_ref[:, place] = dq[:, b * (count // 4) : (b + 1) * (count // 4)]

    @pl.when(step == pl.num_programs(0) - 1)
    def _():
        keep_ref[...] = jnp.zeros_like(keep_ref)
        send_ref[...] = jnp.zeros_like(send_ref)
        keep_ref[0] = jnp.concatenate([dk_ref[0], dv_ref[0]], 1).T.astype(BF16)
        for d in range(1, far_count + 1):

            @pl.when(d <= me)
            def _(d=d):
                part = jnp.concatenate([dk_ref[d], dv_ref[d]], 1).T.astype(BF16)
                place = (me - d) ^ me

                @pl.when(place % 2 == 0)
                def _():
                    keep_ref[place // 2] = part

                @pl.when(place % 2 == 1)
                def _():
                    send_ref[place // 2] = part


def attend_back(me, qa, do, full, kvs, segs, cos_rows, sine_rows, item):
    far_count = len(kvs) - 1
    heads, both, count = qa.shape
    head = both // 2
    wide, half = heads * head, cos_rows.shape[0]
    return pl.pallas_call(
        functools.partial(back_kernel, far_count),
        grid_spec=pltpu.PrefetchScalarGridSpec(
            num_scalar_prefetch=1,
            grid=(heads,),
            in_specs=[
                pl.BlockSpec((None, both, count), lambda h, at: (h, 0, 0)),
                pl.BlockSpec((head, count), lambda h, at: (h, 0)),
                pl.BlockSpec((head, count), lambda h, at: (h, 0)),
                pl.BlockSpec((None, far_count + 1, count), lambda h, at: (item, 0, 0)),
                pl.BlockSpec((half, count), lambda h, at: (0, item)),
                pl.BlockSpec((half, count), lambda h, at: (0, item)),
            ]
            + [pl.BlockSpec((both, count), lambda h, at: (0, item))] * (far_count + 1),
            out_specs=[pl.BlockSpec((head, count), lambda h, at: (h, 0))]
            + [pl.BlockSpec(((far_count + 1) // 2, both, count), lambda h, at: (0, 0, 0))] * 2,
            scratch_shapes=[
                pltpu.VMEM((far_count + 1, count, both), BF16),
                pltpu.VMEM((far_count + 1, head, count), BF16),
                pltpu.VMEM((far_count + 1, count, both), BF16),
                pltpu.VMEM((far_count + 1, count, head), F32),
                pltpu.VMEM((far_count + 1, count, head), F32),
                pltpu.VMEM((head, count), F32),
            ],
        ),
        out_shape=[jax.ShapeDtypeStruct((wide, count), BF16)]
        + [jax.ShapeDtypeStruct(((far_count + 1) // 2, both, count), BF16)] * 2,
        compiler_params=params(),
        cost_estimate=COST,
    )(me, qa, do, full, segs, cos_rows, sine_rows, *kvs)


def merge_kernel(at_ref, own_ref, recv_ref, cos_ref, sin_ref, out_ref):
    head, count = out_ref.shape[0] // 2, out_ref.shape[1]
    total = own_ref[...].astype(F32) + recv_ref[...].astype(F32)
    turned = turn(total[:head], cos_ref[...], sin_ref[...], -1.0)
    out = jnp.concatenate([turned, total[head:]], 0).astype(BF16)
    for b, place in enumerate(places(at_ref, count)):
        out_ref[:, place] = out[:, b * (count // 4) : (b + 1) * (count // 4)]


def merge(at, own, received, cos_rows, sine_rows):
    seqs, both, count = own.shape
    half = cos_rows.shape[0]
    block = pl.BlockSpec((None, both, count), lambda s, at: (s, 0, 0))
    table = pl.BlockSpec((half, count), lambda s, at: (0, s))
    return pl.pallas_call(
        merge_kernel,
        grid_spec=pltpu.PrefetchScalarGridSpec(
            num_scalar_prefetch=1,
            grid=(seqs,),
            in_specs=[block, block, table, table],
            out_specs=block,
        ),
        out_shape=jax.ShapeDtypeStruct(own.shape, BF16),
        compiler_params=params(),
        cost_estimate=COST,
    )(at, own, received, cos_rows, sine_rows)


def product(order, pieces, *items):
    total = order.mark(sum(dot(a, b, form) for a, b, form in items).astype(BF16))
    half = total.shape[0] // 2
    return cut(total[half:], pieces), total[:half]


def cut(x, pieces):
    size = x.shape[0] // pieces
    return [x[j * size : (j + 1) * size] for j in range(pieces)]


def unfold_kernel(near_ref, *refs):
    *far_refs, w_ref, out_ref, full_ref = refs
    half = near_ref.shape[0]
    full_ref[:half] = near_ref[...]
    piece = far_refs[0].shape[0]
    for j, far_ref in enumerate(far_refs):
        full_ref[half + j * piece : half + (j + 1) * piece] = far_ref[...]
    out_ref[...] = dot(w_ref[...], full_ref[...], NT).astype(BF16)


def unfold(near, far, w):
    rows, width = 2 * near.shape[0], near.shape[1]
    return pl.pallas_call(
        unfold_kernel,
        out_shape=[
            jax.ShapeDtypeStruct((w.shape[0], rows), BF16),
            jax.ShapeDtypeStruct((rows, width), BF16),
        ],
        compiler_params=params(),
        cost_estimate=COST,
    )(near, *far, w)


def grad_kernel(groups, has_recv, split, table_ref, *refs):
    out = []
    for form, pairs in groups:
        total = None
        for narrow, wide in pairs:
            both = jnp.concatenate([refs[wide][...], refs[wide + 1][...]], 1)
            if form == TN:
                term = dot(both, refs[narrow][...], TN)
            else:
                term = dot(refs[narrow][...], both, NN)
            total = term if total is None else total + term
        out.append(total)
    at = len(refs) - (2 if split else 1) - (1 if has_recv else 0)
    recv = None
    if has_recv:
        recv, at = refs[at], at + 1

    def put(ref):
        if groups[0][0] == TN:
            rows = out[0].shape[0] // 2
            for j in range(2):
                block = out[0][j * rows : (j + 1) * rows]
                ref[j] = (block if recv is None else block + recv[j].astype(F32)).astype(BF16)
            return
        row = 0
        for total in out:
            count, wide = total.shape[0], total.shape[1] // 2
            for j in range(2):
                block = total[:, j * wide : (j + 1) * wide]
                if recv is not None:
                    block = block + recv[j, row : row + count].astype(F32)
                ref[j, row : row + count] = block.astype(BF16)
            row += count

    if not split:
        put(refs[at])
        return
    first = pl.program_id(0) < split // 2
    pl.when(first)(lambda: put(refs[at]))
    pl.when(jnp.logical_not(first))(lambda: put(refs[at + 1]))


def grad_blocks(table, form, sets, recv=None, split=0):
    n = table.shape[0]
    ins, specs, groups = [], [], []
    for wide_set, narrow_set in sets:
        pairs = []
        for wide, narrow in zip(wide_set, narrow_set):
            pairs.append((len(ins), len(ins) + 1))
            ins += [narrow, wide, wide]
            specs.append(pl.BlockSpec(narrow.shape, lambda i, t: (0, 0)))
            for j in range(2):
                specs.append(pl.BlockSpec((wide.shape[0], BLOCK), lambda i, t, j=j: (0, t[2 * i + j])))
        groups.append((form, pairs))
    if form == TN:
        block = (BLOCK, sets[0][1][0].shape[1])
    else:
        block = (sum(narrow_set[0].shape[0] for _, narrow_set in sets), BLOCK)
    two = (2,) + block
    if recv is not None:
        ins.append(recv)
        specs.append(pl.BlockSpec(two, lambda i, t: (lax.rem(i + split // 2, n // 2), 0, 0)))
    if split:
        out_specs = [
            pl.BlockSpec(two, lambda i, t: (jnp.minimum(i, split // 2 - 1), 0, 0)),
            pl.BlockSpec(two, lambda i, t: (jnp.maximum(i - split // 2, 0), 0, 0)),
        ]
        out_shape = [jax.ShapeDtypeStruct((split,) + block, BF16), jax.ShapeDtypeStruct((n - split,) + block, BF16)]
    else:
        out_specs = pl.BlockSpec(two, lambda i, t: (i, 0, 0))
        out_shape = jax.ShapeDtypeStruct((n,) + block, BF16)
    return pl.pallas_call(
        functools.partial(grad_kernel, groups, recv is not None, split),
        grid_spec=pltpu.PrefetchScalarGridSpec(num_scalar_prefetch=1, grid=(n // 2,), in_specs=specs, out_specs=out_specs),
        out_shape=out_shape,
        compiler_params=params(),
        cost_estimate=COST,
    )(table, *ins)


class Order:
    def __init__(self):
        self.last = None

    def take_all(self, xs):
        if self.last is not None:
            xs = lax.optimization_barrier((self.last, *xs))[1:]
        return xs

    def take(self, *xs):
        xs = self.take_all(xs)
        return xs if len(xs) > 1 else xs[0]

    def mark(self, x):
        self.last = x
        return x


class Scatter:
    def __init__(self, stages, sizes, form, fast):
        self.stages, self.sizes, self.form, self.fast = stages, sizes, form, fast
        ctx, dp = lax.axis_index("context"), lax.axis_index("dp")
        blocks = []
        for p in range(2 ** len(stages)):
            c, d = ctx, dp
            for j, (axis, bit) in enumerate(stages):
                if p >> (len(stages) - 1 - j) & 1:
                    if axis == "context":
                        c = c ^ (1 << bit)
                    else:
                        d = d ^ (1 << bit)
            blocks.append(c * sizes["dp"] + d)
        self.away = jnp.stack(blocks[4:]).astype(jnp.int32)
        self.near = jnp.stack([blocks[p] for p in (2, 3, 0, 1)]).astype(jnp.int32)

    def send(self, j, x):
        axis, bit = self.stages[j]
        self.got = swap(x, axis, self.sizes[axis], bit)

    def first(self, order, sets):
        if self.fast:
            wide = order.take(*sets[0][0])
            self.sets = [(list(wide), sets[0][1])] + sets[1:]
            self.send(0, order.mark(grad_blocks(self.away, self.form, self.sets)))

    def second(self, order):
        if self.fast:
            send, self.keep = grad_blocks(self.near, self.form, self.sets, order.take(self.got), 2)
            self.send(1, order.mark(send))

    def third(self, order):
        if self.fast:
            recv = order.take(self.got)
            send = (self.keep[1].astype(F32) + recv[1].astype(F32)).astype(BF16)
            self.rest = self.keep[0].astype(F32) + recv[0].astype(F32)
            self.send(2, order.mark(send))

    def final(self, order):
        if self.fast:
            return order.mark(self.rest + order.take(self.got).astype(F32))


def place_kernel(at_ref, near_ref, far_ref, out_ref):
    p = pl.program_id(1)

    @pl.when(p < 2)
    def _():
        out_ref[...] = near_ref[...].astype(out_ref.dtype)

    @pl.when(p >= 2)
    def _():
        out_ref[...] = far_ref[...].astype(out_ref.dtype)


def place(at, near, far, dtype):
    seqs, half, width = near.shape
    quarter = half // 2
    block = (None, quarter, width)
    return pl.pallas_call(
        place_kernel,
        grid_spec=pltpu.PrefetchScalarGridSpec(
            num_scalar_prefetch=1,
            grid=(seqs, 4),
            in_specs=[
                pl.BlockSpec(block, lambda s, p, at: (s, jnp.minimum(p, 1), 0)),
                pl.BlockSpec(block, lambda s, p, at: (s, jnp.maximum(p - 2, 0), 0)),
            ],
            out_specs=pl.BlockSpec(block, lambda s, p, at: (s, p ^ (2 * at[1] + at[2]), 0)),
        ),
        out_shape=jax.ShapeDtypeStruct((seqs, 2 * half, width), dtype),
        compiler_params=params(),
        cost_estimate=COST,
    )(at, near, far)


def sealed(fn, *args):
    def never(*args):
        return jax.tree.map(lambda leaf: jnp.zeros(leaf.shape, leaf.dtype), jax.eval_shape(fn, *args))

    return lax.cond(lax.axis_index("tensor") >= 0, fn, never, *args)


def swap(x, axis, size, bit):
    return lax.ppermute(x, axis, [(i, i ^ (1 << bit)) for i in range(size)])


def rows_at(x, at, count):
    return lax.dynamic_slice_in_dim(x, at, count, 0)


def local(sizes, tokens, segment_ids, norm_gain_1, w_query, w_key, w_value, w_output, norm_gain_2, w_gate, w_up, w_down, cotangent):
    seqs, stretch, width = tokens.shape
    rows = seqs * stretch
    head = w_key.shape[1]
    wide = w_query.shape[1]
    n_tensor, n_context, n_dp = sizes["tensor"], sizes["context"], sizes["dp"]
    me_t, me_c = lax.axis_index("tensor"), lax.axis_index("context")
    core, high = me_t % 2, me_t // 2
    mine = 2 * core + high
    half, quarter = stretch // 2, stretch // 4
    offset = me_c * stretch
    order = Order()
    each = range(seqs)

    seg_here = lax.dynamic_slice_in_dim(segment_ids, offset, stretch, 1)
    start = jnp.zeros(seg_here.shape, jnp.int32)
    for number in range(1, ONES_AT):
        before = jnp.sum((segment_ids < number).astype(jnp.int32), 1, keepdims=True)
        start = jnp.where(seg_here == number, before, start)
    positions = (offset + jnp.arange(stretch, dtype=jnp.int32))[None, :] - start
    frequency = 10000.0 ** (-(2.0 * jnp.arange(head // 2, dtype=F32)) / head)
    angles = frequency[:, None] * positions.reshape(1, rows).astype(F32)
    cos_rows, sine_rows = jnp.cos(angles), jnp.sin(angles)
    padded = jnp.concatenate([jnp.zeros((seqs, (n_context - 1) * stretch), jnp.int32), segment_ids], 1)
    segs = jnp.stack(
        [
            lax.dynamic_slice_in_dim(padded, offset + (n_context - 1 - d) * stretch, stretch, 1)
            for d in range(n_context)
        ],
        1,
    )
    at = jnp.stack([me_c, core, high]).astype(jnp.int32)

    x_rows = tokens.reshape(rows, width)
    ct_rows = cotangent.reshape(rows, width)
    gain_1, gain_2 = norm_gain_1.reshape(1, width), norm_gain_2.reshape(1, width)
    w_kv = jnp.concatenate([w_key.T, w_value.T], 0)
    h1, q_t, kv_t = project(at, x_rows, gain_1, w_query, w_kv, cos_rows, sine_rows, stretch)
    order.mark(kv_t)
    kvs = [kv_t] + [
        lax.ppermute(kv_t, "context", [(i, i + d) for i in range(n_context - d)]) for d in range(1, n_context)
    ]

    def own_order(x, s):
        return jnp.concatenate([rows_at(x, s * stretch + (p ^ mine) * quarter, quarter) for p in range(4)], 0)

    def fold(pair):
        sends, keep = pair
        return [swap(x, "tensor", n_tensor, 0) for x in sends], keep

    def join(pieces):
        return jnp.concatenate(order.take_all(pieces), 0)

    def fold_more(kept, got):
        total = kept.astype(F32) + got.astype(F32)
        send = total[quarter:].astype(BF16)
        return swap(order.mark(send), "tensor", n_tensor, 1), total[:quarter]

    def core_swap(x):
        return swap(x, "tensor", n_tensor, 0)

    def fold_now(total):
        near = total[:, :half].astype(F32) + core_swap(total[:, half:]).astype(F32)
        return near[:, quarter:].astype(BF16), near[:, :quarter]

    def spread(part):
        return swap(part, "tensor", n_tensor, 1)

    def spread_more(part, got, pieces):
        got = order.take(got)
        block = order.mark(jnp.concatenate([part, got], 0))
        return [swap(x, "tensor", n_tensor, 0) for x in cut(block, pieces)], block

    cts, d_hidden = [], []
    for s in each:
        cts.append(own_order(order.take(ct_rows), s))
        d_hidden.append(order.mark(dot(cts[s], w_down, NT)))

    stream = [rows_at(x_rows, s * stretch + mine * quarter, quarter).astype(F32) for s in each]
    ct_own = [rows_at(ct_rows, s * stretch + mine * quarter, quarter).astype(F32) for s in each]

    qa, o_t, full_o = [None] * seqs, [None] * seqs, [None] * seqs
    got_o, kept_o = [None] * seqs, [None] * seqs
    residual, scale_2, normed_2, h2_own, got_h = ([None] * seqs for _ in range(5))

    def after_attention(s):
        total = kept_o[s] + order.take(got_o[s]).astype(F32)
        residual[s] = stream[s] + total
        scale_2[s] = lax.rsqrt(jnp.mean(residual[s] * residual[s], -1, keepdims=True) + EPSILON)
        normed_2[s] = residual[s] * scale_2[s]
        h2_own[s] = order.mark((normed_2[s] * gain_2).astype(BF16))
        got_h[s] = spread(h2_own[s])

    for s in each:
        qa[s], o_t[s], full_o[s] = attend(at, order.take(q_t), kvs, segs, s)
        order.mark(o_t[s])
        if s:
            after_attention(s - 1)
        got, kept = fold(product(order, 1, (order.take(o_t[s]), w_output, TN)))
        got_o[s], kept_o[s] = fold_more(kept, join(got))

    hidden, d_gate, d_up, h2 = ([None] * seqs for _ in range(4))
    got_b, kept_b = [None] * seqs, [None] * seqs

    def whole(part, got):
        got, block = spread_more(part, got, 1)
        return order.mark(jnp.concatenate([block, *order.take_all(got)], 0))

    def back_partial(s, pieces):
        left, right = order.take(d_gate[s], d_up[s])
        got, kept = fold(product(order, pieces, (left, w_gate, NT), (right, w_up, NT)))
        got_b[s], kept_b[s] = fold_more(kept, join(got))

    d_res, d_low_own, got_d, gains_2 = ([None] * seqs for _ in range(4))

    def after_back(s):
        back = kept_b[s] + order.take(got_b[s]).astype(F32)
        gains_2[s] = jnp.sum(back * normed_2[s], 0)
        scaled = back * gain_2
        d_res[s] = ct_own[s] + scale_2[s] * (
            scaled - normed_2[s] * jnp.mean(scaled * normed_2[s], -1, keepdims=True)
        )
        d_low_own[s] = order.mark(d_res[s].astype(BF16))
        got_d[s] = spread(d_low_own[s])

    blocks = n_context * n_dp
    fast = width // blocks == BLOCK and n_dp == 2 and n_context == 4
    x_first = [("dp", 0), ("context", 0), ("context", 1)]
    z_first = [("context", 0), ("dp", 0), ("context", 1)]
    down_job = Scatter(x_first, sizes, TN, fast)
    gate_job = Scatter(x_first, sizes, TN, fast)
    up_job = Scatter(z_first, sizes, TN, fast)
    mix_job = Scatter(x_first, sizes, NN, fast)
    kv_job = Scatter(x_first, sizes, NN, fast)

    downs = []
    for s in each:
        h2[s] = whole(h2_own[s], got_h[s])
        gate = order.mark(dot(h2[s], w_gate, NN))
        if s + 1 < seqs:
            after_attention(s + 1)
        if s:
            after_back(s - 1)
        up = dot(order.take(h2[s]), w_up, NN)
        sig = jax.nn.sigmoid(gate)
        hidden[s] = (gate * sig * up).astype(BF16)
        d_gate[s] = (d_hidden[s] * up * sig * (1.0 + gate * (1.0 - sig))).astype(BF16)
        d_up[s] = order.mark((d_hidden[s] * gate * sig).astype(BF16))
        if s + 1 < seqs:
            back_partial(s, 1)
        downs.append(order.mark(dot(order.take(hidden[s]), w_down, NN).astype(BF16)))

    d_low, dq_t, dkvs = [None] * seqs, [None] * seqs, [None] * seqs

    do_t = [None] * seqs

    def unfolded(s):
        def run(part, got):
            block = jnp.concatenate([part, got], 0)
            return unfold(block, [core_swap(block)], w_output)

        do_t[s], d_low[s] = sealed(run, d_low_own[s], order.take(got_d[s]))
        order.mark(do_t[s])

    def back_sealed(s):
        def run(left, right):
            return fold_now((dot(left, w_gate, NT) + dot(right, w_up, NT)).astype(BF16)[None])

        send, kept = sealed(run, *order.take(d_gate[s], d_up[s]))
        got_b[s], kept_b[s] = swap(order.mark(send)[0], "tensor", n_tensor, 1), kept[0]

    def attention_back(s):
        dq_t[s], *dkvs[s] = attend_back(
            at, qa[s], order.take(do_t[s]), full_o[s], kvs, segs, cos_rows, sine_rows, s
        )
        order.mark(dq_t[s])

    def gather_natural(part):
        part = order.mark(part)
        return part, swap(part, "tensor", n_tensor, 1)

    def gather_more(part, got):
        block = order.mark(jnp.concatenate([part, order.take(got)], 1))
        return block, order.mark(sealed(core_swap, block))

    def natural(block, far, dtype):
        return order.mark(place(at, block, order.take(far), dtype))

    last = seqs - 1
    down_job.first(order, [(cts, hidden)])
    unfolded(0)
    back_sealed(last)
    up_job.first(order, [(h2, d_up)])
    attention_back(0)
    after_back(last)
    gate_job.first(order, [(h2, d_gate)])
    unfolded(last)
    down_job.second(order)
    send, kept_out = sealed(lambda *parts: fold_now(jnp.stack(parts)), *order.take_all(downs))
    got_out = swap(order.mark(send), "tensor", n_tensor, 1)
    attention_back(last)

    h1s = [h1[s * stretch : (s + 1) * stretch] for s in each]
    send = order.mark(jnp.stack([dkvs[s][1] for s in each]))
    got_kv = swap(send, "context", n_context, 0)
    kept_kv = jnp.stack([dkvs[s][0] for s in each])
    out_own = (jnp.stack(residual) + kept_out + order.take(got_out).astype(F32)).astype(BF16)
    out_part = gather_natural(out_own)
    up_job.second(order)
    mix_job.first(order, [(d_low, o_t), (h1s, dq_t)])
    got_kv = order.take(got_kv)
    send = order.mark((kept_kv[:, 1].astype(F32) + got_kv[:, 1].astype(F32)).astype(BF16))
    kept_kv = (kept_kv[:, 0].astype(F32) + got_kv[:, 0].astype(F32)).astype(BF16)
    got_kv = swap(send, "context", n_context, 1)
    gate_job.second(order)
    layer_out = natural(*gather_more(*out_part), BF16)
    down_job.third(order)
    dkv_t = order.mark(merge(at, kept_kv, order.take(got_kv), cos_rows, sine_rows))
    dkv_ts = [dkv_t[s] for s in each]
    def input_partial(*parts):
        rows_q, rows_kv = jnp.concatenate(parts[:seqs], 1), jnp.concatenate(parts[seqs:], 1)
        total = dot(rows_q, w_query, TT) + dot(rows_kv, w_kv, TN)
        return fold_now(total.astype(BF16).reshape(seqs, stretch, width))

    send, kept_x = sealed(input_partial, *dq_t, *order.take_all(dkv_ts))
    got_x = swap(order.mark(send), "tensor", n_tensor, 1)
    up_job.third(order)
    kv_job.first(order, [(h1s, dkv_ts)])
    mix_job.second(order)
    gate_job.third(order)

    back = kept_x + order.take(got_x).astype(F32)
    streams = jnp.stack(stream)
    scale_1 = lax.rsqrt(jnp.mean(streams * streams, -1, keepdims=True) + EPSILON)
    normed_1 = streams * scale_1
    gains_1 = jnp.sum(back * normed_1, (0, 1))
    scaled = back * gain_1
    grad = jnp.stack(d_res) + scale_1 * (scaled - normed_1 * jnp.mean(scaled * normed_1, -1, keepdims=True))
    grad_part = gather_natural(grad.astype(BF16))
    hops = [(axis, bit) for axis in ("tensor", "context", "dp") for bit in range((sizes[axis] - 1).bit_length())]
    gain_sum = jnp.stack([gains_1, sum(gains_2)])

    def hop():
        axis, bit = hops.pop(0)
        return order.mark(gain_sum + order.take(swap(gain_sum, axis, sizes[axis], bit)))

    down_sum = down_job.final(order)
    gain_sum = hop()
    up_sum = up_job.final(order)
    gain_sum = hop()
    kv_job.second(order)
    mix_job.third(order)
    grad_tokens = natural(*gather_more(*grad_part), F32)
    kv_job.third(order)
    gain_sum = hop()
    gate_sum = gate_job.final(order)
    while hops:
        gain_sum = hop()
    per = width // blocks
    gain_sum = lax.dynamic_slice_in_dim(gain_sum, (me_c * n_dp + lax.axis_index("dp")) * per, per, 1)

    if fast:
        down_sum = down_sum.T
        kv_sum = kv_job.final(order)
        mixed = mix_job.final(order)
        output_sum, query_sum = mixed[:wide], mixed[wide:].T
        key_sum, value_sum = kv_sum[:head].T, kv_sum[head:].T
    else:

        def plain(left, right, dim):
            total = sum(dot(a, b, TN) for a, b in zip(left, right))
            return lax.psum_scatter(
                total.astype(BF16), ("context", "dp"), scatter_dimension=dim, tiled=True
            ).astype(F32)

        down_sum = plain(hidden, cts, 1)
        gate_sum = plain(h2, d_gate, 0)
        up_sum = plain(h2, d_up, 0)
        output_sum = plain([a.T for a in o_t], d_low, 1)
        query_sum = plain(h1s, [a.T for a in dq_t], 0)
        kv_sum = plain(h1s, [a.T for a in dkv_ts], 0)
        key_sum, value_sum = kv_sum[:, :head], kv_sum[:, head:]
    return (
        layer_out,
        grad_tokens,
        gain_sum[0],
        query_sum,
        key_sum,
        value_sum,
        output_sum,
        gain_sum[1],
        gate_sum,
        up_sum,
        down_sum,
    )


def solution(mesh):
    in_specs = (
        P("dp", "context", None),
        P("dp", None),
        P(),
        P(None, "tensor"),
        P(None, "tensor"),
        P(None, "tensor"),
        P("tensor", None),
        P(),
        P(None, "tensor"),
        P(None, "tensor"),
        P("tensor", None),
        P("dp", "context", None),
    )
    out_specs = (
        P("dp", "context", None),
        P("dp", "context", None),
        P(("context", "dp")),
        P(("context", "dp"), "tensor"),
        P(("context", "dp"), "tensor"),
        P(("context", "dp"), "tensor"),
        P("tensor", ("context", "dp")),
        P(("context", "dp")),
        P(("context", "dp"), "tensor"),
        P(("context", "dp"), "tensor"),
        P("tensor", ("context", "dp")),
    )
    run = functools.partial(local, dict(mesh.shape))
    return jax.shard_map(run, mesh=mesh, in_specs=in_specs, out_specs=out_specs, check_vma=False)
```

```python
import functools

import jax
import jax.numpy as jnp
from jax import lax
from jax.experimental import pallas as pl
from jax.experimental.pallas import tpu as pltpu
from jax.sharding import PartitionSpec as P

EPSILON = 1e-05
BF16 = jnp.bfloat16
F32 = jnp.float32
FAR = 1e30
AUX = 8
ONES_AT = 5
BLOCK = 256


def cost(us=0):
    return pl.CostEstimate(flops=int(us * 1.15e9) + 1024, bytes_accessed=1024, transcendentals=0)


COST = cost()


def params():
    return pltpu.CompilerParams(vmem_limit_bytes=56 * 2**20)


def dot(left, right, dims):
    return lax.dot_general(left, right, (dims, ((), ())), preferred_element_type=F32)


NN, NT, TN, TT = ((1,), (0,)), ((1,), (1,)), ((0,), (0,)), ((0,), (1,))


def turn(rows, cos_rows, sine_rows, sign):
    half = rows.shape[0] // 2
    first, second = rows[:half], rows[half:]
    return jnp.concatenate(
        [first * cos_rows - sign * second * sine_rows, second * cos_rows + sign * first * sine_rows], 0
    )


def project_kernel(at_ref, x_ref, gain_ref, wq_ref, wkv_ref, cos_ref, sin_ref, h_ref, q_ref, kv_ref):
    x = x_ref[...].astype(F32)
    scale = lax.rsqrt(jnp.mean(x * x, -1, keepdims=True) + EPSILON)
    h = (x * scale * gain_ref[...]).astype(BF16)
    part = h.shape[0] // 2
    swapped = at_ref[2] * part
    h_ref[pl.ds(pl.multiple_of(swapped, part), part)] = h[:part]
    h_ref[pl.ds(pl.multiple_of(part - swapped, part), part)] = h[part:]
    cos_rows, sine_rows = cos_ref[...], sin_ref[...]
    head = kv_ref.shape[0] // 2
    score_scale = head ** (-0.5)
    q = dot(h, wq_ref[...], NN).T
    for at in range(0, q.shape[0], head):
        q_ref[at : at + head] = (turn(q[at : at + head], cos_rows, sine_rows, 1.0) * score_scale).astype(BF16)
    kv = dot(wkv_ref[...], h, NT)
    kv_ref[:head] = turn(kv[:head], cos_rows, sine_rows, 1.0).astype(BF16)
    kv_ref[head:] = kv[head:].astype(BF16)


def project(at, x, gain, w_query, w_kv, cos_rows, sine_rows, stretch):
    rows, width = x.shape
    step = stretch // 2
    wide, both = w_query.shape[1], w_kv.shape[0]
    half = cos_rows.shape[0]
    whole = lambda shape: pl.BlockSpec(shape, lambda i, at: (0, 0))
    return pl.pallas_call(
        project_kernel,
        grid_spec=pltpu.PrefetchScalarGridSpec(
            num_scalar_prefetch=1,
            grid=(rows // step,),
            in_specs=[
                pl.BlockSpec((step, width), lambda i, at: (i, 0)),
                whole((1, width)),
                whole((width, wide)),
                whole((both, width)),
                pl.BlockSpec((half, step), lambda i, at: (0, i)),
                pl.BlockSpec((half, step), lambda i, at: (0, i)),
            ],
            out_specs=[
                pl.BlockSpec((step, width), lambda i, at: (i + at[1] - 2 * at[1] * lax.rem(i, 2), 0)),
                pl.BlockSpec((wide, step), lambda i, at: (0, i)),
                pl.BlockSpec((both, step), lambda i, at: (0, i)),
            ],
        ),
        out_shape=[
            jax.ShapeDtypeStruct((rows, width), BF16),
            jax.ShapeDtypeStruct((wide, rows), BF16),
            jax.ShapeDtypeStruct((both, rows), BF16),
        ],
        compiler_params=params(),
        cost_estimate=COST,
    )(at, x, gain, w_query, w_kv, cos_rows, sine_rows)


def pieces(value):
    high = value.astype(BF16).astype(F32)
    middle = (value - high).astype(BF16).astype(F32)
    low = value - high - middle
    return high, middle, low


def key_rows(kv, seg):
    head, count = kv.shape[0] // 2, kv.shape[1]
    row = lax.broadcasted_iota(jnp.int32, (2 * AUX, count), 0)
    extra = jnp.where(row < ONES_AT, jnp.where(seg == row, 0.0, -FAR), jnp.where(row < AUX, 1.0, 0.0))
    rest = jnp.zeros((head - 2 * AUX, count), F32)
    return jnp.concatenate([kv[:head].astype(F32), extra, rest], 0)


def value_rows(kv, fill):
    head, count = kv.shape[0] // 2, kv.shape[1]
    row = lax.broadcasted_iota(jnp.int32, (fill, count), 0)
    return jnp.concatenate([kv[head:].astype(F32), jnp.where(row < 3, 1.0, 0.0)], 0)


def places(at_ref, count):
    quarter = count // 4
    mine = 2 * at_ref[1] + at_ref[2]
    return [pl.ds(pl.multiple_of((b ^ mine) * quarter, quarter), quarter) for b in range(4)]


def causal(scores):
    key_at = lax.broadcasted_iota(jnp.int32, scores.shape, 0)
    query_at = lax.broadcasted_iota(jnp.int32, scores.shape, 1)
    return jnp.where(key_at <= query_at, scores, -FAR)


def attend_kernel(far_count, at_ref, q_ref, seg_ref, *refs):
    kv_refs = refs[: far_count + 1]
    qa_ref, o_ref, full_ref = refs[far_count + 1 : far_count + 4]
    ka_ref, va_ref = refs[far_count + 4 :]
    me = at_ref[0]
    head = kv_refs[0].shape[0] // 2
    count = q_ref.shape[1]

    @pl.when(pl.program_id(0) == 0)
    def _():
        for d, kv_ref in enumerate(kv_refs):
            kv = kv_ref[...]
            ka_ref[d] = key_rows(kv, seg_ref[d : d + 1]).T.astype(BF16)
            va_ref[d] = value_rows(kv, 2 * AUX).astype(BF16)

    row = lax.broadcasted_iota(jnp.int32, (2 * AUX, count), 0)
    same = jnp.where((seg_ref[0:1] == row) & (row < ONES_AT), 1.0, 0.0)
    rest = jnp.zeros((head - 2 * AUX, count), F32)

    def heads(blocks):
        for h in range(q_ref.shape[0] // head):
            q = q_ref[h * head : (h + 1) * head].astype(F32)
            qa = jnp.concatenate([q, same, rest], 0).astype(BF16)
            scores = [dot(ka_ref[d], qa, NN) for d in range(blocks)]
            scores[0] = causal(scores[0])
            m = jnp.max(scores[0], 0, keepdims=True)
            for d in range(1, blocks):
                m = jnp.maximum(m, jnp.max(scores[d], 0, keepdims=True))
            acc = None
            for d in range(blocks):
                term = dot(va_ref[d], jnp.exp(scores[d] - m).astype(BF16), NN)
                acc = term if acc is None else acc + term
            total = acc[head : head + 1]
            out = acc[:head] / total
            for b, place in enumerate(places(at_ref, count)):
                quarter = out[:, b * (count // 4) : (b + 1) * (count // 4)]
                full_ref[h * head : (h + 1) * head, place] = quarter
                o_ref[h * head : (h + 1) * head, place] = quarter.astype(BF16)
            high, middle, low = pieces(-(m + jnp.log(total)))
            extra = jnp.where(
                row == ONES_AT, high, jnp.where(row == ONES_AT + 1, middle, jnp.where(row == ONES_AT + 2, low, same))
            )
            qa_ref[h] = jnp.concatenate([q, extra, rest], 0).astype(BF16)

    for blocks in range(1, far_count + 2):
        pl.when(me == blocks - 1)(functools.partial(heads, blocks))


def attend(me, q, kvs, segs, item, group=2):
    far_count = len(kvs) - 1
    both = kvs[0].shape[0]
    head = both // 2
    wide, count = q.shape[0], segs.shape[-1]
    heads = wide // head
    return pl.pallas_call(
        functools.partial(attend_kernel, far_count),
        grid_spec=pltpu.PrefetchScalarGridSpec(
            num_scalar_prefetch=1,
            grid=(heads // group,),
            in_specs=[
                pl.BlockSpec((group * head, count), lambda h, at: (h, item)),
                pl.BlockSpec((None, far_count + 1, count), lambda h, at: (item, 0, 0)),
            ]
            + [pl.BlockSpec((both, count), lambda h, at: (0, item))] * (far_count + 1),
            out_specs=[
                pl.BlockSpec((group, both, count), lambda h, at: (h, 0, 0)),
                pl.BlockSpec((group * head, count), lambda h, at: (h, 0)),
                pl.BlockSpec((group * head, count), lambda h, at: (h, 0)),
            ],
            scratch_shapes=[
                pltpu.VMEM((far_count + 1, count, both), BF16),
                pltpu.VMEM((far_count + 1, head + 2 * AUX, count), BF16),
            ],
        ),
        out_shape=[
            jax.ShapeDtypeStruct((heads, both, count), BF16),
            jax.ShapeDtypeStruct((wide, count), BF16),
            jax.ShapeDtypeStruct((wide, count), F32),
        ],
        compiler_params=params(),
        cost_estimate=COST,
    )(me, q, segs, *kvs)


def back_kernel(far_count, at_ref, qa_ref, do_ref, full_ref, seg_ref, cos_ref, sin_ref, *refs):
    kv_refs = refs[: far_count + 1]
    dq_ref, keep_ref, send_ref = refs[far_count + 1 : far_count + 4]
    ka_ref, kt_ref, va_ref, dk_ref, dv_ref, dq_acc = refs[far_count + 4 :]
    me = at_ref[0]
    head, count = do_ref.shape
    step = pl.program_id(0)

    @pl.when(step == 0)
    def _():
        for d, kv_ref in enumerate(kv_refs):
            kv = kv_ref[...]
            ka_ref[d] = key_rows(kv, seg_ref[d : d + 1]).T.astype(BF16)
            kt_ref[d] = kv[:head]
            va_ref[d] = value_rows(kv, head).T.astype(BF16)
        dk_ref[...] = jnp.zeros_like(dk_ref)
        dv_ref[...] = jnp.zeros_like(dv_ref)

    qa = qa_ref[...]
    here = places(at_ref, count)
    do = jnp.concatenate([do_ref[:, place] for place in here], 1).astype(F32)
    full = jnp.concatenate([full_ref[:, place] for place in here], 1)
    high, middle, low = pieces(-jnp.sum(do * full, 0, keepdims=True))
    row = lax.broadcasted_iota(jnp.int32, (2 * AUX, count), 0)
    extra = jnp.where(row == 0, high, jnp.where(row == 1, middle, jnp.where(row == 2, low, 0.0)))
    rest = jnp.zeros((head - 2 * AUX, count), F32)
    da = jnp.concatenate([do, extra, rest], 0).astype(BF16)
    for d in range(far_count + 1):

        def part(d=d):
            scores = dot(ka_ref[d], qa, NN)
            probs = jnp.exp(causal(scores) if d == 0 else scores)
            d_scores = (probs * dot(va_ref[d], da, NN)).astype(BF16)
            dv_ref[d] += dot(probs.astype(BF16), da[:head], NT)
            dk_ref[d] += dot(d_scores, qa[:head], NT)
            update = dot(kt_ref[d], d_scores, NN)
            if d == 0:
                dq_acc[...] = update
            else:
                dq_acc[...] += update

        if d == 0:
            part()
        else:
            pl.when(d <= me)(part)
    score_scale = head ** (-0.5)
    dq = turn(dq_acc[...] * score_scale, cos_ref[...], sin_ref[...], -1.0).astype(BF16)
    for b, place in enumerate(here):
        dq_ref[:, place] = dq[:, b * (count // 4) : (b + 1) * (count // 4)]

    @pl.when(step == pl.num_programs(0) - 1)
    def _():
        keep_ref[...] = jnp.zeros_like(keep_ref)
        send_ref[...] = jnp.zeros_like(send_ref)
        keep_ref[0] = jnp.concatenate([dk_ref[0], dv_ref[0]], 1).T.astype(BF16)
        for d in range(1, far_count + 1):

            @pl.when(d <= me)
            def _(d=d):
                part = jnp.concatenate([dk_ref[d], dv_ref[d]], 1).T.astype(BF16)
                place = (me - d) ^ me

                @pl.when(place % 2 == 0)
                def _():
                    keep_ref[place // 2] = part

                @pl.when(place % 2 == 1)
                def _():
                    send_ref[place // 2] = part


def attend_back(me, qa, do, full, kvs, segs, cos_rows, sine_rows, item):
    far_count = len(kvs) - 1
    heads, both, count = qa.shape
    head = both // 2
    wide, half = heads * head, cos_rows.shape[0]
    return pl.pallas_call(
        functools.partial(back_kernel, far_count),
        grid_spec=pltpu.PrefetchScalarGridSpec(
            num_scalar_prefetch=1,
            grid=(heads,),
            in_specs=[
                pl.BlockSpec((None, both, count), lambda h, at: (h, 0, 0)),
                pl.BlockSpec((head, count), lambda h, at: (h, 0)),
                pl.BlockSpec((head, count), lambda h, at: (h, 0)),
                pl.BlockSpec((None, far_count + 1, count), lambda h, at: (item, 0, 0)),
                pl.BlockSpec((half, count), lambda h, at: (0, item)),
                pl.BlockSpec((half, count), lambda h, at: (0, item)),
            ]
            + [pl.BlockSpec((both, count), lambda h, at: (0, item))] * (far_count + 1),
            out_specs=[pl.BlockSpec((head, count), lambda h, at: (h, 0))]
            + [pl.BlockSpec(((far_count + 1) // 2, both, count), lambda h, at: (0, 0, 0))] * 2,
            scratch_shapes=[
                pltpu.VMEM((far_count + 1, count, both), BF16),
                pltpu.VMEM((far_count + 1, head, count), BF16),
                pltpu.VMEM((far_count + 1, count, both), BF16),
                pltpu.VMEM((far_count + 1, count, head), F32),
                pltpu.VMEM((far_count + 1, count, head), F32),
                pltpu.VMEM((head, count), F32),
            ],
        ),
        out_shape=[jax.ShapeDtypeStruct((wide, count), BF16)]
        + [jax.ShapeDtypeStruct(((far_count + 1) // 2, both, count), BF16)] * 2,
        compiler_params=params(),
        cost_estimate=COST,
    )(me, qa, do, full, segs, cos_rows, sine_rows, *kvs)


def merge_kernel(at_ref, own_ref, recv_ref, cos_ref, sin_ref, out_ref):
    head, count = out_ref.shape[0] // 2, out_ref.shape[1]
    total = own_ref[...].astype(F32) + recv_ref[...].astype(F32)
    turned = turn(total[:head], cos_ref[...], sin_ref[...], -1.0)
    out = jnp.concatenate([turned, total[head:]], 0).astype(BF16)
    for b, place in enumerate(places(at_ref, count)):
        out_ref[:, place] = out[:, b * (count // 4) : (b + 1) * (count // 4)]


def merge(at, own, received, cos_rows, sine_rows):
    seqs, both, count = own.shape
    half = cos_rows.shape[0]
    block = pl.BlockSpec((None, both, count), lambda s, at: (s, 0, 0))
    table = pl.BlockSpec((half, count), lambda s, at: (0, s))
    return pl.pallas_call(
        merge_kernel,
        grid_spec=pltpu.PrefetchScalarGridSpec(
            num_scalar_prefetch=1,
            grid=(seqs,),
            in_specs=[block, block, table, table],
            out_specs=block,
        ),
        out_shape=jax.ShapeDtypeStruct(own.shape, BF16),
        compiler_params=params(),
        cost_estimate=COST,
    )(at, own, received, cos_rows, sine_rows)


def product(order, pieces, *items):
    total = order.mark(sum(dot(a, b, form) for a, b, form in items).astype(BF16))
    half = total.shape[0] // 2
    return cut(total[half:], pieces), total[:half]


def cut(x, pieces):
    size = x.shape[0] // pieces
    return [x[j * size : (j + 1) * size] for j in range(pieces)]


def unfold_kernel(*refs):
    *part_refs, w_ref, out_ref, full_ref = refs
    size = part_refs[0].shape[0]
    for j, ref in enumerate(part_refs):
        full_ref[j * size : (j + 1) * size] = ref[...]
    out_ref[...] = dot(w_ref[...], full_ref[...], NT).astype(BF16)


def unfold(parts, w):
    rows, width = len(parts) * parts[0].shape[0], parts[0].shape[1]
    return pl.pallas_call(
        unfold_kernel,
        out_shape=[
            jax.ShapeDtypeStruct((w.shape[0], rows), BF16),
            jax.ShapeDtypeStruct((rows, width), BF16),
        ],
        compiler_params=params(),
        cost_estimate=COST,
    )(*parts, w)


def grad_kernel(groups, has_recv, split, table_ref, *refs):
    out = []
    for form, pairs in groups:
        total = None
        for narrow, wide in pairs:
            both = jnp.concatenate([refs[wide][...], refs[wide + 1][...]], 1)
            if form == TN:
                term = dot(both, refs[narrow][...], TN)
            else:
                term = dot(refs[narrow][...], both, NN)
            total = term if total is None else total + term
        out.append(total)
    at = len(refs) - (2 if split else 1) - (1 if has_recv else 0)
    recv = None
    if has_recv:
        recv, at = refs[at], at + 1

    def put(ref):
        if groups[0][0] == TN:
            rows = out[0].shape[0] // 2
            for j in range(2):
                block = out[0][j * rows : (j + 1) * rows]
                ref[j] = (block if recv is None else block + recv[j].astype(F32)).astype(BF16)
            return
        row = 0
        for total in out:
            count, wide = total.shape[0], total.shape[1] // 2
            for j in range(2):
                block = total[:, j * wide : (j + 1) * wide]
                if recv is not None:
                    block = block + recv[j, row : row + count].astype(F32)
                ref[j, row : row + count] = block.astype(BF16)
            row += count

    if not split:
        put(refs[at])
        return
    first = pl.program_id(0) < split // 2
    pl.when(first)(lambda: put(refs[at]))
    pl.when(jnp.logical_not(first))(lambda: put(refs[at + 1]))


def grad_blocks(table, form, sets, recv=None, split=0, us=0):
    n = table.shape[0]
    ins, specs, groups = [], [], []
    for wide_set, narrow_set in sets:
        pairs = []
        for s, (wide, narrow) in enumerate(zip(wide_set, narrow_set)):
            pairs.append((len(ins), len(ins) + 1))
            ins += [narrow, wide, wide]
            specs.append(pl.BlockSpec(narrow.shape, lambda i, t: (0, 0)))
            tokens = narrow.shape[0 if form == TN else 1]
            item = s if wide.shape[0] > tokens else 0
            for j in range(2):
                specs.append(pl.BlockSpec((tokens, BLOCK), lambda i, t, j=j, item=item: (item, t[2 * i + j])))
        groups.append((form, pairs))
    if form == TN:
        block = (BLOCK, sets[0][1][0].shape[1])
    else:
        block = (sum(narrow_set[0].shape[0] for _, narrow_set in sets), BLOCK)
    two = (2,) + block
    if recv is not None:
        ins.append(recv)
        specs.append(pl.BlockSpec(two, lambda i, t: (lax.rem(i + split // 2, n // 2), 0, 0)))
    if split:
        out_specs = [
            pl.BlockSpec(two, lambda i, t: (jnp.minimum(i, split // 2 - 1), 0, 0)),
            pl.BlockSpec(two, lambda i, t: (jnp.maximum(i - split // 2, 0), 0, 0)),
        ]
        out_shape = [jax.ShapeDtypeStruct((split,) + block, BF16), jax.ShapeDtypeStruct((n - split,) + block, BF16)]
    else:
        out_specs = pl.BlockSpec(two, lambda i, t: (i, 0, 0))
        out_shape = jax.ShapeDtypeStruct((n,) + block, BF16)
    return pl.pallas_call(
        functools.partial(grad_kernel, groups, recv is not None, split),
        grid_spec=pltpu.PrefetchScalarGridSpec(num_scalar_prefetch=1, grid=(n // 2,), in_specs=specs, out_specs=out_specs),
        out_shape=out_shape,
        compiler_params=params(),
        cost_estimate=cost(us),
    )(table, *ins)


def add_send_kernel(keep_ref, recv_ref, send_ref, rest_ref):
    send_ref[...] = (keep_ref[1].astype(F32) + recv_ref[1].astype(F32)).astype(BF16)
    rest_ref[...] = keep_ref[0].astype(F32) + recv_ref[0].astype(F32)


def add_send(keep, recv, us):
    shape = keep.shape[1:]
    return pl.pallas_call(
        add_send_kernel,
        out_shape=[jax.ShapeDtypeStruct(shape, BF16), jax.ShapeDtypeStruct(shape, F32)],
        compiler_params=params(),
        cost_estimate=cost(us),
    )(keep, recv)


def add_last_kernel(turned, rest_ref, got_ref, *out_refs):
    row = 0
    for (count, flip), out_ref in zip(turned, out_refs):
        total = rest_ref[row : row + count] + got_ref[row : row + count].astype(F32)
        out_ref[...] = total.T if flip else total
        row += count


def add_last(rest, got, turned, us):
    wide = rest.shape[1]
    return pl.pallas_call(
        functools.partial(add_last_kernel, turned),
        out_shape=[
            jax.ShapeDtypeStruct((wide, count) if flip else (count, wide), F32) for count, flip in turned
        ],
        compiler_params=params(),
        cost_estimate=cost(us),
    )(rest, got)


class Order:
    def __init__(self):
        self.last = None

    def take_all(self, xs):
        if self.last is not None:
            xs = lax.optimization_barrier((self.last, *xs))[1:]
        return xs

    def take(self, *xs):
        xs = self.take_all(xs)
        return xs if len(xs) > 1 else xs[0]

    def mark(self, x):
        self.last = x
        return x


def sealed(fn, *args):
    def never(*args):
        return jax.tree.map(lambda leaf: jnp.zeros(leaf.shape, leaf.dtype), jax.eval_shape(fn, *args))

    return lax.cond(lax.axis_index("tensor") >= 0, fn, never, *args)


class Scatter:
    def __init__(self, stages, sizes, form, fast):
        self.stages, self.sizes, self.form, self.fast = stages, sizes, form, fast
        ctx, dp = lax.axis_index("context"), lax.axis_index("dp")
        blocks = []
        for p in range(2 ** len(stages)):
            c, d = ctx, dp
            for j, (axis, bit) in enumerate(stages):
                if p >> (len(stages) - 1 - j) & 1:
                    if axis == "context":
                        c = c ^ (1 << bit)
                    else:
                        d = d ^ (1 << bit)
            blocks.append(c * sizes["dp"] + d)
        self.away = jnp.stack(blocks[4:]).astype(jnp.int32)
        self.near = jnp.stack([blocks[p] for p in (2, 3, 0, 1)]).astype(jnp.int32)

    def send(self, j, x):
        axis, bit = self.stages[j]
        self.got = swap(x, axis, self.sizes[axis], bit)

    def first(self, order, sets, us=0):
        if self.fast:
            wide = order.take(*sets[0][0])
            self.sets = [(list(wide), sets[0][1])] + sets[1:]
            self.send(0, order.mark(grad_blocks(self.away, self.form, self.sets, us=us)))

    def second(self, order, us=0):
        if self.fast:
            send, self.keep = grad_blocks(self.near, self.form, self.sets, order.take(self.got), 2, us)
            self.send(1, order.mark(send))

    def third(self, order, us=0):
        if self.fast:
            send, self.rest = add_send(self.keep, order.take(self.got), us)
            self.send(2, order.mark(send))

    def final(self, order, turned, us=0):
        if self.fast:
            out = add_last(self.rest, order.take(self.got), turned, us)
            order.mark(out[0])
            return out if len(out) > 1 else out[0]


def place_kernel(at_ref, *refs):
    *part_refs, out_ref = refs
    quarter = part_refs[0].shape[0]
    mine = 2 * at_ref[1] + at_ref[2]
    for p, ref in enumerate(part_refs):
        where = pl.ds(pl.multiple_of((p ^ mine) * quarter, quarter), quarter)
        out_ref[where] = ref[...].astype(out_ref.dtype)


def place(at, parts, dtype, us):
    seqs, quarter, width = parts[0].shape
    spec = lambda rows: pl.BlockSpec((None, rows, width), lambda s, at: (s, 0, 0))
    return pl.pallas_call(
        place_kernel,
        grid_spec=pltpu.PrefetchScalarGridSpec(
            num_scalar_prefetch=1, grid=(seqs,), in_specs=[spec(quarter)] * 4, out_specs=spec(4 * quarter)
        ),
        out_shape=jax.ShapeDtypeStruct((seqs, 4 * quarter, width), dtype),
        compiler_params=params(),
        cost_estimate=cost(us),
    )(at, *parts)


def swap(x, axis, size, bit):
    return lax.ppermute(x, axis, [(i, i ^ (1 << bit)) for i in range(size)])


def rows_at(x, at, count):
    return lax.dynamic_slice_in_dim(x, at, count, 0)


def local(sizes, tokens, segment_ids, norm_gain_1, w_query, w_key, w_value, w_output, norm_gain_2, w_gate, w_up, w_down, cotangent):
    seqs, stretch, width = tokens.shape
    rows = seqs * stretch
    head = w_key.shape[1]
    wide = w_query.shape[1]
    n_tensor, n_context, n_dp = sizes["tensor"], sizes["context"], sizes["dp"]
    me_t, me_c = lax.axis_index("tensor"), lax.axis_index("context")
    core, high = me_t % 2, me_t // 2
    mine = 2 * core + high
    half, quarter = stretch // 2, stretch // 4
    offset = me_c * stretch
    order = Order()
    each = range(seqs)

    seg_here = lax.dynamic_slice_in_dim(segment_ids, offset, stretch, 1)
    start = jnp.zeros(seg_here.shape, jnp.int32)
    for number in range(1, ONES_AT):
        before = jnp.sum((segment_ids < number).astype(jnp.int32), 1, keepdims=True)
        start = jnp.where(seg_here == number, before, start)
    positions = (offset + jnp.arange(stretch, dtype=jnp.int32))[None, :] - start
    frequency = 10000.0 ** (-(2.0 * jnp.arange(head // 2, dtype=F32)) / head)
    angles = frequency[:, None] * positions.reshape(1, rows).astype(F32)
    cos_rows, sine_rows = jnp.cos(angles), jnp.sin(angles)
    padded = jnp.concatenate([jnp.zeros((seqs, (n_context - 1) * stretch), jnp.int32), segment_ids], 1)
    segs = jnp.stack(
        [
            lax.dynamic_slice_in_dim(padded, offset + (n_context - 1 - d) * stretch, stretch, 1)
            for d in range(n_context)
        ],
        1,
    )
    at = jnp.stack([me_c, core, high]).astype(jnp.int32)

    x_rows = tokens.reshape(rows, width)
    ct_rows = cotangent.reshape(rows, width)
    gain_1, gain_2 = norm_gain_1.reshape(1, width), norm_gain_2.reshape(1, width)
    w_kv = jnp.concatenate([w_key.T, w_value.T], 0)
    h1, q_t, kv_t = project(at, x_rows, gain_1, w_query, w_kv, cos_rows, sine_rows, stretch)
    order.mark(kv_t)
    kvs = [kv_t] + [
        lax.ppermute(kv_t, "context", [(i, i + d) for i in range(n_context - d)]) for d in range(1, n_context)
    ]

    def own_order(x, s):
        return jnp.concatenate([rows_at(x, s * stretch + (p ^ mine) * quarter, quarter) for p in range(4)], 0)

    def fold(pair):
        sends, keep = pair
        return [swap(x, "tensor", n_tensor, 0) for x in sends], keep

    def join(pieces):
        return jnp.concatenate(order.take_all(pieces), 0)

    def fold_more(kept, got):
        total = kept.astype(F32) + got.astype(F32)
        send = total[quarter:].astype(BF16)
        return swap(order.mark(send), "tensor", n_tensor, 1), total[:quarter]

    def core_swap(x):
        return swap(x, "tensor", n_tensor, 0)

    def core_swaps(first, second):
        first = core_swap(first)
        first, second = lax.optimization_barrier((first, second))
        return first, core_swap(second)

    def fold_now(total):
        near = total[:, :half].astype(F32) + core_swap(total[:, half:]).astype(F32)
        return near[:, quarter:].astype(BF16), near[:, :quarter]

    def spread(part):
        return swap(part, "tensor", n_tensor, 1)

    def spread_more(part, got, pieces):
        got = order.take(got)
        block = order.mark(jnp.concatenate([part, got], 0))
        return [swap(x, "tensor", n_tensor, 0) for x in cut(block, pieces)], block

    cts, d_hidden = [], []
    for s in each:
        cts.append(own_order(order.take(ct_rows), s))
        d_hidden.append(order.mark(dot(cts[s], w_down, NT)))

    stream = [rows_at(x_rows, s * stretch + mine * quarter, quarter).astype(F32) for s in each]
    ct_own = [rows_at(ct_rows, s * stretch + mine * quarter, quarter).astype(F32) for s in each]

    qa, o_t, full_o = [None] * seqs, [None] * seqs, [None] * seqs
    got_o, kept_o = [None] * seqs, [None] * seqs
    residual, scale_2, normed_2, h2_own, got_h = ([None] * seqs for _ in range(5))

    def after_attention(s):
        total = kept_o[s] + order.take(got_o[s]).astype(F32)
        residual[s] = stream[s] + total
        scale_2[s] = lax.rsqrt(jnp.mean(residual[s] * residual[s], -1, keepdims=True) + EPSILON)
        normed_2[s] = residual[s] * scale_2[s]
        h2_own[s] = order.mark((normed_2[s] * gain_2).astype(BF16))
        got_h[s] = spread(h2_own[s])

    for s in each:
        qa[s], o_t[s], full_o[s] = attend(at, order.take(q_t), kvs, segs, s)
        order.mark(o_t[s])
        if s:
            after_attention(s - 1)
        got, kept = fold(product(order, 1, (order.take(o_t[s]), w_output, TN)))
        got_o[s], kept_o[s] = fold_more(kept, join(got))

    hidden, d_gate, d_up, h2 = ([None] * seqs for _ in range(4))
    got_b, kept_b = [None] * seqs, [None] * seqs

    def whole(part, got):
        got, block = spread_more(part, got, 1)
        return order.mark(jnp.concatenate([block, *order.take_all(got)], 0))

    def back_sealed(s):
        def run(left, right):
            return fold_now((dot(left, w_gate, NT) + dot(right, w_up, NT)).astype(BF16)[None])

        send, kept = sealed(run, *order.take(d_gate[s], d_up[s]))
        got_b[s], kept_b[s] = swap(order.mark(send)[0], "tensor", n_tensor, 1), kept[0]

    d_res, d_low_own, got_d, gains_2 = ([None] * seqs for _ in range(4))

    def norm_back(scaled_grad, normed, scale, gain):
        scaled = scaled_grad * gain
        return scale * (scaled - normed * jnp.mean(scaled * normed, -1, keepdims=True))

    def after_back(s):
        def run(kept, got, normed, scale, own):
            back = kept + got.astype(F32)
            grad = own + norm_back(back, normed, scale, gain_2)
            return grad.astype(BF16), grad, jnp.sum(back * normed, 0)

        d_low_own[s], d_res[s], gains_2[s] = sealed(
            run, kept_b[s], order.take(got_b[s]), normed_2[s], scale_2[s], ct_own[s]
        )
        got_d[s] = spread(order.mark(d_low_own[s]))

    blocks = n_context * n_dp
    fast = width // blocks == BLOCK and n_dp == 2 and n_context == 4
    x_first = [("dp", 0), ("context", 0), ("context", 1)]
    z_first = [("context", 0), ("dp", 0), ("context", 1)]
    down_job = Scatter(x_first, sizes, TN, fast)
    gate_job = Scatter(x_first, sizes, TN, fast)
    up_job = Scatter(z_first, sizes, TN, fast)
    mix_job = Scatter(x_first, sizes, NN, fast)
    kv_job = Scatter(x_first, sizes, NN, fast)

    downs = []

    def feed_forward(rows, d_rows):
        gate, up = dot(rows, w_gate, NN), dot(rows, w_up, NN)
        sig = jax.nn.sigmoid(gate)
        return (
            (gate * sig * up).astype(BF16),
            (d_rows * up * sig * (1.0 + gate * (1.0 - sig))).astype(BF16),
            (d_rows * gate * sig).astype(BF16),
        )

    def add_down(s):
        run = lambda rows: dot(rows, w_down, NN).astype(BF16)
        downs.append(order.mark(sealed(run, order.take(hidden[s]))))

    for s in each:
        h2[s] = whole(h2_own[s], got_h[s])
        if s:
            after_back(s - 1)
        hidden[s], d_gate[s], d_up[s] = sealed(feed_forward, order.take(h2[s]), d_hidden[s])
        order.mark(d_up[s])
        if s + 1 < seqs:
            after_attention(s + 1)
            back_sealed(s)
            add_down(s)

    d_low, dq_t, dkvs = [None] * seqs, [None] * seqs, [None] * seqs

    do_t = [None] * seqs

    def unfolded(s):
        def run(part, got):
            return unfold([part, got, *core_swaps(part, got)], w_output)

        do_t[s], d_low[s] = sealed(run, d_low_own[s], order.take(got_d[s]))
        order.mark(do_t[s])

    def attention_back(s):
        dq_t[s], *dkvs[s] = attend_back(
            at, qa[s], order.take(do_t[s]), full_o[s], kvs, segs, cos_rows, sine_rows, s
        )
        order.mark(dq_t[s])

    def place_all(part, got, dtype, us=0):
        far = sealed(core_swaps, part, order.take(got))
        return order.mark(place(at, [part, got, *far], dtype, us))

    last = seqs - 1
    down_job.first(order, [(cts, hidden)])
    back_sealed(last)
    unfolded(0)
    up_job.first(order, [(h2, d_up)])
    after_back(last)
    gate_job.first(order, [(h2, d_gate)], 12)
    add_down(last)
    send, kept_out = sealed(lambda *parts: fold_now(jnp.stack(parts)), *order.take_all(downs))
    got_out = swap(order.mark(send), "tensor", n_tensor, 1)
    attention_back(0)
    unfolded(last)
    down_job.second(order, 6)
    up_job.second(order)

    def out_rows(got, kept, *rows):
        return (jnp.stack(rows) + kept + got.astype(F32)).astype(BF16)

    out_own = order.mark(sealed(out_rows, order.take(got_out), kept_out, *residual))
    got_out = spread(out_own)
    attention_back(last)

    keep_send = [x for s in each for x in dkvs[s]]
    kept_kv, send = sealed(lambda *xs: (jnp.stack(xs[0::2]), jnp.stack(xs[1::2])), *keep_send)
    got_kv = swap(order.mark(send), "context", n_context, 0)
    layer_out = place_all(out_own, got_out, BF16)
    mix_job.first(order, [(d_low, o_t), ([h1] * seqs, dq_t)])

    def add_kv(kept, got):
        total = kept.astype(F32) + got.astype(F32)
        return total[:, 0].astype(BF16), total[:, 1].astype(BF16)

    kept_kv, send = sealed(add_kv, kept_kv, order.take(got_kv))
    got_kv = swap(order.mark(send), "context", n_context, 1)
    gate_job.second(order)
    down_job.third(order, 2)
    up_job.third(order, 12)

    def input_partial(kept, got, *parts):
        both = merge(at, kept, got, cos_rows, sine_rows)
        rows_q, rows_kv = jnp.concatenate(parts, 1), jnp.concatenate([both[s] for s in each], 1)
        total = dot(rows_q, w_query, TT) + dot(rows_kv, w_kv, TN)
        return *fold_now(total.astype(BF16).reshape(seqs, stretch, width)), *[both[s] for s in each]

    send, kept_x, *dkv_ts = sealed(input_partial, kept_kv, order.take(got_kv), *dq_t)
    got_x = swap(order.mark(send), "tensor", n_tensor, 1)
    down_sum = down_job.final(order, [(BLOCK, True)], 2)
    kv_job.first(order, [([h1] * seqs, dkv_ts)])
    mix_job.second(order)
    up_sum = up_job.final(order, [(BLOCK, False)], 4)

    def input_grad(kept, got, sums_0, sums_1, *parts):
        back = kept + got.astype(F32)
        streams, res = jnp.stack(parts[:seqs]), jnp.stack(parts[seqs:])
        scale = lax.rsqrt(jnp.mean(streams * streams, -1, keepdims=True) + EPSILON)
        normed = streams * scale
        grad = res + norm_back(back, normed, scale, gain_1)
        return grad.astype(BF16), jnp.stack([jnp.sum(back * normed, (0, 1)), sums_0 + sums_1])

    grad_own, gain_sum = sealed(input_grad, kept_x, order.take(got_x), *gains_2, *stream, *d_res)
    got_grad = spread(order.mark(grad_own))
    gate_job.third(order, 4)
    kv_job.second(order, 8)

    def all_sum(total):
        for axis in ("tensor", "context", "dp"):
            for bit in range((sizes[axis] - 1).bit_length()):
                total = total + swap(total, axis, sizes[axis], bit)
        return total

    gain_sum = order.mark(sealed(all_sum, order.take(gain_sum)))
    mix_job.third(order)
    gate_sum = gate_job.final(order, [(BLOCK, False)])
    kv_job.third(order)
    grad_tokens = place_all(grad_own, got_grad, F32, 6)
    per = width // blocks
    gain_sum = lax.dynamic_slice_in_dim(gain_sum, (me_c * n_dp + lax.axis_index("dp")) * per, per, 1)

    if fast:
        key_sum, value_sum = kv_job.final(order, [(head, True), (head, True)])
        output_sum, query_sum = mix_job.final(order, [(wide, False), (wide, True)])
    else:

        def plain(left, right, dim):
            total = sum(dot(a, b, TN) for a, b in zip(left, right))
            return lax.psum_scatter(
                total.astype(BF16), ("context", "dp"), scatter_dimension=dim, tiled=True
            ).astype(F32)

        down_sum = plain(hidden, cts, 1)
        gate_sum = plain(h2, d_gate, 0)
        up_sum = plain(h2, d_up, 0)
        output_sum = plain([a.T for a in o_t], d_low, 1)
        h1s = [h1[s * stretch : (s + 1) * stretch] for s in each]
        query_sum = plain(h1s, [a.T for a in dq_t], 0)
        kv_sum = plain(h1s, [a.T for a in dkv_ts], 0)
        key_sum, value_sum = kv_sum[:, :head], kv_sum[:, head:]
    return (
        layer_out,
        grad_tokens,
        gain_sum[0],
        query_sum,
        key_sum,
        value_sum,
        output_sum,
        gain_sum[1],
        gate_sum,
        up_sum,
        down_sum,
    )


def solution(mesh):
    in_specs = (
        P("dp", "context", None),
        P("dp", None),
        P(),
        P(None, "tensor"),
        P(None, "tensor"),
        P(None, "tensor"),
        P("tensor", None),
        P(),
        P(None, "tensor"),
        P(None, "tensor"),
        P("tensor", None),
        P("dp", "context", None),
    )
    out_specs = (
        P("dp", "context", None),
        P("dp", "context", None),
        P(("context", "dp")),
        P(("context", "dp"), "tensor"),
        P(("context", "dp"), "tensor"),
        P(("context", "dp"), "tensor"),
        P("tensor", ("context", "dp")),
        P(("context", "dp")),
        P(("context", "dp"), "tensor"),
        P(("context", "dp"), "tensor"),
        P("tensor", ("context", "dp")),
    )
    run = functools.partial(local, dict(mesh.shape))
    return jax.shard_map(run, mesh=mesh, in_specs=in_specs, out_specs=out_specs, check_vma=False)
```

```python
import functools

import jax
import jax.numpy as jnp
from jax import lax
from jax.experimental import pallas as pl
from jax.experimental.pallas import tpu as pltpu
from jax.sharding import PartitionSpec as P

EPSILON = 1e-05
BF16 = jnp.bfloat16
F32 = jnp.float32
FAR = 1e30
AUX = 8
ONES_AT = 5
BLOCK = 256


def cost(us=0):
    return pl.CostEstimate(flops=int(us * 1.15e9) + 1024, bytes_accessed=1024, transcendentals=0)


COST = cost()


def params():
    return pltpu.CompilerParams(vmem_limit_bytes=56 * 2**20)


def dot(left, right, dims):
    return lax.dot_general(left, right, (dims, ((), ())), preferred_element_type=F32)


NN, NT, TN, TT = ((1,), (0,)), ((1,), (1,)), ((0,), (0,)), ((0,), (1,))


def turn(rows, cos_rows, sine_rows, sign):
    half = rows.shape[0] // 2
    first, second = rows[:half], rows[half:]
    return jnp.concatenate(
        [first * cos_rows - sign * second * sine_rows, second * cos_rows + sign * first * sine_rows], 0
    )


def project_kernel(at_ref, x_ref, gain_ref, wq_ref, wkv_ref, cos_ref, sin_ref, h_ref, q_ref, kv_ref):
    x = x_ref[...].astype(F32)
    scale = lax.rsqrt(jnp.mean(x * x, -1, keepdims=True) + EPSILON)
    h = (x * scale * gain_ref[...]).astype(BF16)
    part = h.shape[0] // 2
    swapped = at_ref[2] * part
    h_ref[pl.ds(pl.multiple_of(swapped, part), part)] = h[:part]
    h_ref[pl.ds(pl.multiple_of(part - swapped, part), part)] = h[part:]
    cos_rows, sine_rows = cos_ref[...], sin_ref[...]
    head = kv_ref.shape[0] // 2
    score_scale = head ** (-0.5)
    q = dot(h, wq_ref[...], NN).T
    for at in range(0, q.shape[0], head):
        q_ref[at : at + head] = (turn(q[at : at + head], cos_rows, sine_rows, 1.0) * score_scale).astype(BF16)
    kv = dot(wkv_ref[...], h, NT)
    kv_ref[:head] = turn(kv[:head], cos_rows, sine_rows, 1.0).astype(BF16)
    kv_ref[head:] = kv[head:].astype(BF16)


def project(at, x, gain, w_query, w_kv, cos_rows, sine_rows, stretch):
    rows, width = x.shape
    step = stretch // 2
    wide, both = w_query.shape[1], w_kv.shape[0]
    half = cos_rows.shape[0]
    whole = lambda shape: pl.BlockSpec(shape, lambda i, at: (0, 0))
    return pl.pallas_call(
        project_kernel,
        grid_spec=pltpu.PrefetchScalarGridSpec(
            num_scalar_prefetch=1,
            grid=(rows // step,),
            in_specs=[
                pl.BlockSpec((step, width), lambda i, at: (i, 0)),
                whole((1, width)),
                whole((width, wide)),
                whole((both, width)),
                pl.BlockSpec((half, step), lambda i, at: (0, i)),
                pl.BlockSpec((half, step), lambda i, at: (0, i)),
            ],
            out_specs=[
                pl.BlockSpec((step, width), lambda i, at: (i + at[1] - 2 * at[1] * lax.rem(i, 2), 0)),
                pl.BlockSpec((wide, step), lambda i, at: (0, i)),
                pl.BlockSpec((both, step), lambda i, at: (0, i)),
            ],
        ),
        out_shape=[
            jax.ShapeDtypeStruct((rows, width), BF16),
            jax.ShapeDtypeStruct((wide, rows), BF16),
            jax.ShapeDtypeStruct((both, rows), BF16),
        ],
        compiler_params=params(),
        cost_estimate=COST,
    )(at, x, gain, w_query, w_kv, cos_rows, sine_rows)


def pieces(value):
    high = value.astype(BF16).astype(F32)
    middle = (value - high).astype(BF16).astype(F32)
    low = value - high - middle
    return high, middle, low


def key_rows(kv, seg):
    head, count = kv.shape[0] // 2, kv.shape[1]
    row = lax.broadcasted_iota(jnp.int32, (2 * AUX, count), 0)
    extra = jnp.where(row < ONES_AT, jnp.where(seg == row, 0.0, -FAR), jnp.where(row < AUX, 1.0, 0.0))
    rest = jnp.zeros((head - 2 * AUX, count), F32)
    return jnp.concatenate([kv[:head].astype(F32), extra, rest], 0)


def value_rows(kv, fill):
    head, count = kv.shape[0] // 2, kv.shape[1]
    row = lax.broadcasted_iota(jnp.int32, (fill, count), 0)
    return jnp.concatenate([kv[head:].astype(F32), jnp.where(row < 3, 1.0, 0.0)], 0)


def places(at_ref, count):
    quarter = count // 4
    mine = 2 * at_ref[1] + at_ref[2]
    return [pl.ds(pl.multiple_of((b ^ mine) * quarter, quarter), quarter) for b in range(4)]


def causal(scores):
    key_at = lax.broadcasted_iota(jnp.int32, scores.shape, 0)
    query_at = lax.broadcasted_iota(jnp.int32, scores.shape, 1)
    return jnp.where(key_at <= query_at, scores, -FAR)


def attend_kernel(far_count, at_ref, q_ref, seg_ref, *refs):
    kv_refs = refs[: far_count + 1]
    qa_ref, o_ref, full_ref = refs[far_count + 1 : far_count + 4]
    ka_ref, va_ref = refs[far_count + 4 :]
    me = at_ref[0]
    head = kv_refs[0].shape[0] // 2
    count = q_ref.shape[1]

    @pl.when(pl.program_id(0) == 0)
    def _():
        for d, kv_ref in enumerate(kv_refs):
            kv = kv_ref[...]
            ka_ref[d] = key_rows(kv, seg_ref[d : d + 1]).T.astype(BF16)
            va_ref[d] = value_rows(kv, 2 * AUX).astype(BF16)

    row = lax.broadcasted_iota(jnp.int32, (2 * AUX, count), 0)
    same = jnp.where((seg_ref[0:1] == row) & (row < ONES_AT), 1.0, 0.0)
    rest = jnp.zeros((head - 2 * AUX, count), F32)

    def heads(blocks):
        for h in range(q_ref.shape[0] // head):
            q = q_ref[h * head : (h + 1) * head].astype(F32)
            qa = jnp.concatenate([q, same, rest], 0).astype(BF16)
            scores = [dot(ka_ref[d], qa, NN) for d in range(blocks)]
            scores[0] = causal(scores[0])
            m = jnp.max(scores[0], 0, keepdims=True)
            for d in range(1, blocks):
                m = jnp.maximum(m, jnp.max(scores[d], 0, keepdims=True))
            acc = None
            for d in range(blocks):
                term = dot(va_ref[d], jnp.exp(scores[d] - m).astype(BF16), NN)
                acc = term if acc is None else acc + term
            total = acc[head : head + 1]
            out = acc[:head] / total
            for b, place in enumerate(places(at_ref, count)):
                quarter = out[:, b * (count // 4) : (b + 1) * (count // 4)]
                full_ref[h * head : (h + 1) * head, place] = quarter
                o_ref[h * head : (h + 1) * head, place] = quarter.astype(BF16)
            high, middle, low = pieces(-(m + jnp.log(total)))
            extra = jnp.where(
                row == ONES_AT, high, jnp.where(row == ONES_AT + 1, middle, jnp.where(row == ONES_AT + 2, low, same))
            )
            qa_ref[h] = jnp.concatenate([q, extra, rest], 0).astype(BF16)

    for blocks in range(1, far_count + 2):
        pl.when(me == blocks - 1)(functools.partial(heads, blocks))


def attend(me, q, kvs, segs, item, group=2):
    far_count = len(kvs) - 1
    both = kvs[0].shape[0]
    head = both // 2
    wide, count = q.shape[0], segs.shape[-1]
    heads = wide // head
    return pl.pallas_call(
        functools.partial(attend_kernel, far_count),
        grid_spec=pltpu.PrefetchScalarGridSpec(
            num_scalar_prefetch=1,
            grid=(heads // group,),
            in_specs=[
                pl.BlockSpec((group * head, count), lambda h, at: (h, item)),
                pl.BlockSpec((None, far_count + 1, count), lambda h, at: (item, 0, 0)),
            ]
            + [pl.BlockSpec((both, count), lambda h, at: (0, item))] * (far_count + 1),
            out_specs=[
                pl.BlockSpec((group, both, count), lambda h, at: (h, 0, 0)),
                pl.BlockSpec((group * head, count), lambda h, at: (h, 0)),
                pl.BlockSpec((group * head, count), lambda h, at: (h, 0)),
            ],
            scratch_shapes=[
                pltpu.VMEM((far_count + 1, count, both), BF16),
                pltpu.VMEM((far_count + 1, head + 2 * AUX, count), BF16),
            ],
        ),
        out_shape=[
            jax.ShapeDtypeStruct((heads, both, count), BF16),
            jax.ShapeDtypeStruct((wide, count), BF16),
            jax.ShapeDtypeStruct((wide, count), F32),
        ],
        compiler_params=params(),
        cost_estimate=COST,
    )(me, q, segs, *kvs)


def back_kernel(far_count, at_ref, qa_ref, do_ref, full_ref, seg_ref, cos_ref, sin_ref, *refs):
    kv_refs = refs[: far_count + 1]
    dq_ref, keep_ref, send_ref = refs[far_count + 1 : far_count + 4]
    ka_ref, kt_ref, va_ref, dk_ref, dv_ref, dq_acc = refs[far_count + 4 :]
    me = at_ref[0]
    head, count = do_ref.shape
    step = pl.program_id(0)

    @pl.when(step == 0)
    def _():
        for d, kv_ref in enumerate(kv_refs):
            kv = kv_ref[...]
            ka_ref[d] = key_rows(kv, seg_ref[d : d + 1]).T.astype(BF16)
            kt_ref[d] = kv[:head]
            va_ref[d] = value_rows(kv, head).T.astype(BF16)
        dk_ref[...] = jnp.zeros_like(dk_ref)
        dv_ref[...] = jnp.zeros_like(dv_ref)

    qa = qa_ref[...]
    here = places(at_ref, count)
    do = jnp.concatenate([do_ref[:, place] for place in here], 1).astype(F32)
    full = jnp.concatenate([full_ref[:, place] for place in here], 1)
    high, middle, low = pieces(-jnp.sum(do * full, 0, keepdims=True))
    row = lax.broadcasted_iota(jnp.int32, (2 * AUX, count), 0)
    extra = jnp.where(row == 0, high, jnp.where(row == 1, middle, jnp.where(row == 2, low, 0.0)))
    rest = jnp.zeros((head - 2 * AUX, count), F32)
    da = jnp.concatenate([do, extra, rest], 0).astype(BF16)
    def run(blocks):
        total = None
        for d in range(blocks):
            scores = dot(ka_ref[d], qa, NN)
            probs = jnp.exp(causal(scores) if d == 0 else scores)
            d_scores = (probs * dot(va_ref[d], da, NN)).astype(BF16)
            dv_ref[d] += dot(probs.astype(BF16), da[:head], NT)
            dk_ref[d] += dot(d_scores, qa[:head], NT)
            update = dot(kt_ref[d], d_scores, NN)
            total = update if total is None else total + update
        dq_acc[...] = total

    for blocks in range(1, far_count + 2):
        pl.when(me == blocks - 1)(functools.partial(run, blocks))
    score_scale = head ** (-0.5)
    dq = turn(dq_acc[...] * score_scale, cos_ref[...], sin_ref[...], -1.0).astype(BF16)
    for b, place in enumerate(here):
        dq_ref[:, place] = dq[:, b * (count // 4) : (b + 1) * (count // 4)]

    @pl.when(step == pl.num_programs(0) - 1)
    def _():
        keep_ref[...] = jnp.zeros_like(keep_ref)
        send_ref[...] = jnp.zeros_like(send_ref)
        keep_ref[0] = jnp.concatenate([dk_ref[0], dv_ref[0]], 1).T.astype(BF16)
        for d in range(1, far_count + 1):

            @pl.when(d <= me)
            def _(d=d):
                part = jnp.concatenate([dk_ref[d], dv_ref[d]], 1).T.astype(BF16)
                place = (me - d) ^ me

                @pl.when(place % 2 == 0)
                def _():
                    keep_ref[place // 2] = part

                @pl.when(place % 2 == 1)
                def _():
                    send_ref[place // 2] = part


def attend_back(me, qa, do, full, kvs, segs, cos_rows, sine_rows, item, us):
    far_count = len(kvs) - 1
    heads, both, count = qa.shape
    head = both // 2
    wide, half = heads * head, cos_rows.shape[0]
    return pl.pallas_call(
        functools.partial(back_kernel, far_count),
        grid_spec=pltpu.PrefetchScalarGridSpec(
            num_scalar_prefetch=1,
            grid=(heads,),
            in_specs=[
                pl.BlockSpec((None, both, count), lambda h, at: (h, 0, 0)),
                pl.BlockSpec((head, count), lambda h, at: (h, 0)),
                pl.BlockSpec((head, count), lambda h, at: (h, 0)),
                pl.BlockSpec((None, far_count + 1, count), lambda h, at: (item, 0, 0)),
                pl.BlockSpec((half, count), lambda h, at: (0, item)),
                pl.BlockSpec((half, count), lambda h, at: (0, item)),
            ]
            + [pl.BlockSpec((both, count), lambda h, at: (0, item))] * (far_count + 1),
            out_specs=[pl.BlockSpec((head, count), lambda h, at: (h, 0))]
            + [pl.BlockSpec(((far_count + 1) // 2, both, count), lambda h, at: (0, 0, 0))] * 2,
            scratch_shapes=[
                pltpu.VMEM((far_count + 1, count, both), BF16),
                pltpu.VMEM((far_count + 1, head, count), BF16),
                pltpu.VMEM((far_count + 1, count, both), BF16),
                pltpu.VMEM((far_count + 1, count, head), F32),
                pltpu.VMEM((far_count + 1, count, head), F32),
                pltpu.VMEM((head, count), F32),
            ],
        ),
        out_shape=[jax.ShapeDtypeStruct((wide, count), BF16)]
        + [jax.ShapeDtypeStruct(((far_count + 1) // 2, both, count), BF16)] * 2,
        compiler_params=params(),
        cost_estimate=cost(us),
    )(me, qa, do, full, segs, cos_rows, sine_rows, *kvs)


def merge_kernel(at_ref, own_ref, recv_ref, cos_ref, sin_ref, out_ref):
    head, count = out_ref.shape[0] // 2, out_ref.shape[1]
    total = own_ref[...].astype(F32) + recv_ref[...].astype(F32)
    turned = turn(total[:head], cos_ref[...], sin_ref[...], -1.0)
    out = jnp.concatenate([turned, total[head:]], 0).astype(BF16)
    for b, place in enumerate(places(at_ref, count)):
        out_ref[:, place] = out[:, b * (count // 4) : (b + 1) * (count // 4)]


def merge(at, own, received, cos_rows, sine_rows):
    seqs, both, count = own.shape
    half = cos_rows.shape[0]
    block = pl.BlockSpec((None, both, count), lambda s, at: (s, 0, 0))
    table = pl.BlockSpec((half, count), lambda s, at: (0, s))
    return pl.pallas_call(
        merge_kernel,
        grid_spec=pltpu.PrefetchScalarGridSpec(
            num_scalar_prefetch=1,
            grid=(seqs,),
            in_specs=[block, block, table, table],
            out_specs=block,
        ),
        out_shape=jax.ShapeDtypeStruct(own.shape, BF16),
        compiler_params=params(),
        cost_estimate=COST,
    )(at, own, received, cos_rows, sine_rows)


def product(order, pieces, *items):
    total = order.mark(sum(dot(a, b, form) for a, b, form in items).astype(BF16))
    half = total.shape[0] // 2
    return cut(total[half:], pieces), total[:half]


def cut(x, pieces):
    size = x.shape[0] // pieces
    return [x[j * size : (j + 1) * size] for j in range(pieces)]


def unfold_kernel(*refs):
    *part_refs, w_ref, out_ref, full_ref = refs
    size = part_refs[0].shape[0]
    for j, ref in enumerate(part_refs):
        full_ref[j * size : (j + 1) * size] = ref[...]
    out_ref[...] = dot(w_ref[...], full_ref[...], NT).astype(BF16)


def unfold(parts, w):
    rows, width = len(parts) * parts[0].shape[0], parts[0].shape[1]
    return pl.pallas_call(
        unfold_kernel,
        out_shape=[
            jax.ShapeDtypeStruct((w.shape[0], rows), BF16),
            jax.ShapeDtypeStruct((rows, width), BF16),
        ],
        compiler_params=params(),
        cost_estimate=COST,
    )(*parts, w)


def grad_kernel(groups, has_recv, split, table_ref, *refs):
    out = []
    for form, pairs in groups:
        total = None
        for narrow, wide in pairs:
            both = jnp.concatenate([refs[wide][...], refs[wide + 1][...]], 1)
            if form == TN:
                term = dot(both, refs[narrow][...], TN)
            else:
                term = dot(refs[narrow][...], both, NN)
            total = term if total is None else total + term
        out.append(total)
    at = len(refs) - (2 if split else 1) - (1 if has_recv else 0)
    recv = None
    if has_recv:
        recv, at = refs[at], at + 1

    def put(ref):
        if groups[0][0] == TN:
            rows = out[0].shape[0] // 2
            for j in range(2):
                block = out[0][j * rows : (j + 1) * rows]
                ref[j] = (block if recv is None else block + recv[j].astype(F32)).astype(BF16)
            return
        row = 0
        for total in out:
            count, wide = total.shape[0], total.shape[1] // 2
            for j in range(2):
                block = total[:, j * wide : (j + 1) * wide]
                if recv is not None:
                    block = block + recv[j, row : row + count].astype(F32)
                ref[j, row : row + count] = block.astype(BF16)
            row += count

    if not split:
        put(refs[at])
        return
    first = pl.program_id(0) < split // 2
    pl.when(first)(lambda: put(refs[at]))
    pl.when(jnp.logical_not(first))(lambda: put(refs[at + 1]))


def grad_blocks(table, form, sets, recv=None, split=0, us=0):
    n = table.shape[0]
    ins, specs, groups = [], [], []
    for wide_set, narrow_set in sets:
        pairs = []
        for s, (wide, narrow) in enumerate(zip(wide_set, narrow_set)):
            pairs.append((len(ins), len(ins) + 1))
            ins += [narrow, wide, wide]
            specs.append(pl.BlockSpec(narrow.shape, lambda i, t: (0, 0)))
            tokens = narrow.shape[0 if form == TN else 1]
            item = s if wide.shape[0] > tokens else 0
            for j in range(2):
                specs.append(pl.BlockSpec((tokens, BLOCK), lambda i, t, j=j, item=item: (item, t[2 * i + j])))
        groups.append((form, pairs))
    if form == TN:
        block = (BLOCK, sets[0][1][0].shape[1])
    else:
        block = (sum(narrow_set[0].shape[0] for _, narrow_set in sets), BLOCK)
    two = (2,) + block
    if recv is not None:
        ins.append(recv)
        specs.append(pl.BlockSpec(two, lambda i, t: (lax.rem(i + split // 2, n // 2), 0, 0)))
    if split:
        out_specs = [
            pl.BlockSpec(two, lambda i, t: (jnp.minimum(i, split // 2 - 1), 0, 0)),
            pl.BlockSpec(two, lambda i, t: (jnp.maximum(i - split // 2, 0), 0, 0)),
        ]
        out_shape = [jax.ShapeDtypeStruct((split,) + block, BF16), jax.ShapeDtypeStruct((n - split,) + block, BF16)]
    else:
        out_specs = pl.BlockSpec(two, lambda i, t: (i, 0, 0))
        out_shape = jax.ShapeDtypeStruct((n,) + block, BF16)
    return pl.pallas_call(
        functools.partial(grad_kernel, groups, recv is not None, split),
        grid_spec=pltpu.PrefetchScalarGridSpec(num_scalar_prefetch=1, grid=(n // 2,), in_specs=specs, out_specs=out_specs),
        out_shape=out_shape,
        compiler_params=params(),
        cost_estimate=cost(us),
    )(table, *ins)


def add_send_kernel(keep_ref, recv_ref, send_ref, rest_ref):
    send_ref[...] = (keep_ref[1].astype(F32) + recv_ref[1].astype(F32)).astype(BF16)
    rest_ref[...] = keep_ref[0].astype(F32) + recv_ref[0].astype(F32)


def add_send(keep, recv, us):
    shape = keep.shape[1:]
    return pl.pallas_call(
        add_send_kernel,
        out_shape=[jax.ShapeDtypeStruct(shape, BF16), jax.ShapeDtypeStruct(shape, F32)],
        compiler_params=params(),
        cost_estimate=cost(us),
    )(keep, recv)


def add_pair_kernel(a_ref, b_ref, out_ref):
    out_ref[...] = a_ref[...] + b_ref[...]


def add_pair(a, b, us):
    return pl.pallas_call(
        add_pair_kernel,
        out_shape=jax.ShapeDtypeStruct(a.shape, a.dtype),
        compiler_params=params(),
        cost_estimate=cost(us),
    )(a, b)


def add_last_kernel(turned, rest_ref, got_ref, *out_refs):
    row = 0
    for (count, flip), out_ref in zip(turned, out_refs):
        total = rest_ref[row : row + count] + got_ref[row : row + count].astype(F32)
        out_ref[...] = total.T if flip else total
        row += count


def add_last(rest, got, turned, us):
    wide = rest.shape[1]
    return pl.pallas_call(
        functools.partial(add_last_kernel, turned),
        out_shape=[
            jax.ShapeDtypeStruct((wide, count) if flip else (count, wide), F32) for count, flip in turned
        ],
        compiler_params=params(),
        cost_estimate=cost(us),
    )(rest, got)


class Order:
    def __init__(self):
        self.last = None

    def take_all(self, xs):
        if self.last is not None:
            xs = lax.optimization_barrier((self.last, *xs))[1:]
        return xs

    def take(self, *xs):
        xs = self.take_all(xs)
        return xs if len(xs) > 1 else xs[0]

    def mark(self, x):
        self.last = x
        return x


def sealed(fn, *args):
    def never(*args):
        return jax.tree.map(lambda leaf: jnp.zeros(leaf.shape, leaf.dtype), jax.eval_shape(fn, *args))

    return lax.cond(lax.axis_index("tensor") >= 0, fn, never, *args)


class Scatter:
    def __init__(self, stages, sizes, form, fast):
        self.stages, self.sizes, self.form, self.fast = stages, sizes, form, fast
        ctx, dp = lax.axis_index("context"), lax.axis_index("dp")
        blocks = []
        for p in range(2 ** len(stages)):
            c, d = ctx, dp
            for j, (axis, bit) in enumerate(stages):
                if p >> (len(stages) - 1 - j) & 1:
                    if axis == "context":
                        c = c ^ (1 << bit)
                    else:
                        d = d ^ (1 << bit)
            blocks.append(c * sizes["dp"] + d)
        self.away = jnp.stack(blocks[4:]).astype(jnp.int32)
        self.near = jnp.stack([blocks[p] for p in (2, 3, 0, 1)]).astype(jnp.int32)

    def send(self, j, x):
        axis, bit = self.stages[j]
        self.got = swap(x, axis, self.sizes[axis], bit)

    def first(self, order, sets, us=0):
        if self.fast:
            wide = order.take(*sets[0][0])
            self.sets = [(list(wide), sets[0][1])] + sets[1:]
            self.send(0, order.mark(grad_blocks(self.away, self.form, self.sets, us=us)))

    def second(self, order, us=0):
        if self.fast:
            send, self.keep = grad_blocks(self.near, self.form, self.sets, order.take(self.got), 2, us)
            self.send(1, order.mark(send))

    def third(self, order, us=0):
        if self.fast:
            send, self.rest = add_send(self.keep, order.take(self.got), us)
            self.send(2, order.mark(send))

    def final(self, order, turned, us=0):
        if self.fast:
            out = add_last(self.rest, order.take(self.got), turned, us)
            order.mark(out[0])
            return out if len(out) > 1 else out[0]


def place_kernel(at_ref, *refs):
    *part_refs, out_ref = refs
    quarter = part_refs[0].shape[0]
    mine = 2 * at_ref[1] + at_ref[2]
    for p, ref in enumerate(part_refs):
        where = pl.ds(pl.multiple_of((p ^ mine) * quarter, quarter), quarter)
        out_ref[where] = ref[...].astype(out_ref.dtype)


def place(at, parts, dtype, us):
    seqs, quarter, width = parts[0].shape
    spec = lambda rows: pl.BlockSpec((None, rows, width), lambda s, at: (s, 0, 0))
    return pl.pallas_call(
        place_kernel,
        grid_spec=pltpu.PrefetchScalarGridSpec(
            num_scalar_prefetch=1, grid=(seqs,), in_specs=[spec(quarter)] * 4, out_specs=spec(4 * quarter)
        ),
        out_shape=jax.ShapeDtypeStruct((seqs, 4 * quarter, width), dtype),
        compiler_params=params(),
        cost_estimate=cost(us),
    )(at, *parts)


def swap(x, axis, size, bit):
    return lax.ppermute(x, axis, [(i, i ^ (1 << bit)) for i in range(size)])


def rows_at(x, at, count):
    return lax.dynamic_slice_in_dim(x, at, count, 0)


def local(sizes, tokens, segment_ids, norm_gain_1, w_query, w_key, w_value, w_output, norm_gain_2, w_gate, w_up, w_down, cotangent):
    seqs, stretch, width = tokens.shape
    rows = seqs * stretch
    head = w_key.shape[1]
    wide = w_query.shape[1]
    n_tensor, n_context, n_dp = sizes["tensor"], sizes["context"], sizes["dp"]
    me_t, me_c = lax.axis_index("tensor"), lax.axis_index("context")
    core, high = me_t % 2, me_t // 2
    mine = 2 * core + high
    half, quarter = stretch // 2, stretch // 4
    offset = me_c * stretch
    order = Order()
    each = range(seqs)

    seg_here = lax.dynamic_slice_in_dim(segment_ids, offset, stretch, 1)
    start = jnp.zeros(seg_here.shape, jnp.int32)
    for number in range(1, ONES_AT):
        before = jnp.sum((segment_ids < number).astype(jnp.int32), 1, keepdims=True)
        start = jnp.where(seg_here == number, before, start)
    positions = (offset + jnp.arange(stretch, dtype=jnp.int32))[None, :] - start
    frequency = 10000.0 ** (-(2.0 * jnp.arange(head // 2, dtype=F32)) / head)
    angles = frequency[:, None] * positions.reshape(1, rows).astype(F32)
    cos_rows, sine_rows = jnp.cos(angles), jnp.sin(angles)
    padded = jnp.concatenate([jnp.zeros((seqs, (n_context - 1) * stretch), jnp.int32), segment_ids], 1)
    segs = jnp.stack(
        [
            lax.dynamic_slice_in_dim(padded, offset + (n_context - 1 - d) * stretch, stretch, 1)
            for d in range(n_context)
        ],
        1,
    )
    at = jnp.stack([me_c, core, high]).astype(jnp.int32)

    x_rows = tokens.reshape(rows, width)
    ct_rows = cotangent.reshape(rows, width)
    gain_1, gain_2 = norm_gain_1.reshape(1, width), norm_gain_2.reshape(1, width)
    w_kv = jnp.concatenate([w_key.T, w_value.T], 0)
    h1, q_t, kv_t = project(at, x_rows, gain_1, w_query, w_kv, cos_rows, sine_rows, stretch)
    order.mark(kv_t)
    kvs = [kv_t] + [
        lax.ppermute(kv_t, "context", [(i, i + d) for i in range(n_context - d)]) for d in range(1, n_context)
    ]

    def own_order(x, s):
        return jnp.concatenate([rows_at(x, s * stretch + (p ^ mine) * quarter, quarter) for p in range(4)], 0)

    def fold(pair):
        sends, keep = pair
        return [swap(x, "tensor", n_tensor, 0) for x in sends], keep

    def join(pieces):
        return jnp.concatenate(order.take_all(pieces), 0)

    def fold_more(kept, got):
        total = kept.astype(F32) + got.astype(F32)
        send = total[quarter:].astype(BF16)
        return swap(order.mark(send), "tensor", n_tensor, 1), total[:quarter]

    def core_swap(x):
        return swap(x, "tensor", n_tensor, 0)

    def core_swaps(first, second):
        first = core_swap(first)
        first, second = lax.optimization_barrier((first, second))
        return first, core_swap(second)

    def fold_now(total):
        near = total[:, :half].astype(F32) + core_swap(total[:, half:]).astype(F32)
        return near[:, quarter:].astype(BF16), near[:, :quarter]

    def spread(part):
        return swap(part, "tensor", n_tensor, 1)

    cts, d_hidden = [], []
    for s in each:
        cts.append(own_order(order.take(ct_rows), s))
        d_hidden.append(order.mark(dot(cts[s], w_down, NT)))

    stream = [rows_at(x_rows, s * stretch + mine * quarter, quarter).astype(F32) for s in each]
    ct_own = [rows_at(ct_rows, s * stretch + mine * quarter, quarter).astype(F32) for s in each]

    qa, o_t, full_o = [None] * seqs, [None] * seqs, [None] * seqs
    got_o, kept_o = [None] * seqs, [None] * seqs
    residual, scale_2, normed_2, h2_own, got_h = ([None] * seqs for _ in range(5))

    def after_attention(s):
        total = kept_o[s] + order.take(got_o[s]).astype(F32)
        residual[s] = stream[s] + total
        scale_2[s] = lax.rsqrt(jnp.mean(residual[s] * residual[s], -1, keepdims=True) + EPSILON)
        normed_2[s] = residual[s] * scale_2[s]
        h2_own[s] = order.mark((normed_2[s] * gain_2).astype(BF16))
        got_h[s] = spread(h2_own[s])

    for s in each:
        qa[s], o_t[s], full_o[s] = attend(at, order.take(q_t), kvs, segs, s)
        order.mark(o_t[s])
        if s:
            after_attention(s - 1)
        got, kept = fold(product(order, 1, (order.take(o_t[s]), w_output, TN)))
        got_o[s], kept_o[s] = fold_more(kept, join(got))

    hidden, d_gate, d_up, h2 = ([None] * seqs for _ in range(4))
    got_b, kept_b = [None] * seqs, [None] * seqs

    def back_sealed(s):
        def run(left, right):
            return fold_now((dot(left, w_gate, NT) + dot(right, w_up, NT)).astype(BF16)[None])

        send, kept = sealed(run, *order.take(d_gate[s], d_up[s]))
        got_b[s], kept_b[s] = swap(order.mark(send)[0], "tensor", n_tensor, 1), kept[0]

    d_res, d_low_own, got_d, gains_2 = ([None] * seqs for _ in range(4))

    def norm_back(scaled_grad, normed, scale, gain):
        scaled = scaled_grad * gain
        return scale * (scaled - normed * jnp.mean(scaled * normed, -1, keepdims=True))

    def after_back(s):
        def run(kept, got, normed, scale, own):
            back = kept + got.astype(F32)
            grad = own + norm_back(back, normed, scale, gain_2)
            return grad.astype(BF16), grad, jnp.sum(back * normed, 0)

        d_low_own[s], d_res[s], gains_2[s] = sealed(
            run, kept_b[s], order.take(got_b[s]), normed_2[s], scale_2[s], ct_own[s]
        )
        got_d[s] = spread(order.mark(d_low_own[s]))

    blocks = n_context * n_dp
    fast = width // blocks == BLOCK and n_dp == 2 and n_context == 4
    x_first = [("dp", 0), ("context", 0), ("context", 1)]
    z_first = [("context", 0), ("dp", 0), ("context", 1)]
    down_job = Scatter(x_first, sizes, TN, fast)
    gate_job = Scatter(x_first, sizes, TN, fast)
    up_job = Scatter(z_first, sizes, TN, fast)
    mix_job = Scatter(x_first, sizes, NN, fast)
    kv_job = Scatter(x_first, sizes, NN, fast)

    def feed_forward(part, got, d_rows):
        rows = jnp.concatenate([part, got, *core_swaps(part, got)], 0)
        gate, up = dot(rows, w_gate, NN), dot(rows, w_up, NN)
        sig = jax.nn.sigmoid(gate)
        return (
            rows,
            (gate * sig * up).astype(BF16),
            (d_rows * up * sig * (1.0 + gate * (1.0 - sig))).astype(BF16),
            (d_rows * gate * sig).astype(BF16),
        )

    for s in each:
        h2[s], hidden[s], d_gate[s], d_up[s] = sealed(feed_forward, h2_own[s], order.take(got_h[s]), d_hidden[s])
        order.mark(d_up[s])
        if s + 1 < seqs:
            after_attention(s + 1)
            back_sealed(s)

    d_low, dq_t, dkvs = [None] * seqs, [None] * seqs, [None] * seqs

    do_t = [None] * seqs

    def unfolded(s):
        def run(part, got):
            return unfold([part, got, *core_swaps(part, got)], w_output)

        do_t[s], d_low[s] = sealed(run, d_low_own[s], order.take(got_d[s]))
        order.mark(do_t[s])

    def attention_back(s, us):
        dq_t[s], *dkvs[s] = attend_back(
            at, qa[s], order.take(do_t[s]), full_o[s], kvs, segs, cos_rows, sine_rows, s, us
        )
        order.mark(dq_t[s])

    def place_all(part, got, dtype, us=0):
        far = sealed(core_swaps, part, order.take(got))
        return order.mark(place(at, [part, got, *far], dtype, us))

    last = seqs - 1
    down_job.first(order, [(cts, hidden)], 0)
    for s in range(last):
        after_back(s)
    back_sealed(last)
    unfolded(0)
    up_job.first(order, [(h2, d_up)], 20)
    after_back(last)
    gate_job.first(order, [(h2, d_gate)], 0)

    def down_partial(*parts):
        total = dot(jnp.concatenate(parts, 0), w_down, NN).astype(BF16)
        return fold_now(total.reshape(seqs, stretch, width))

    send, kept_out = sealed(down_partial, *order.take_all(hidden))
    got_out = swap(order.mark(send), "tensor", n_tensor, 1)
    down_job.second(order, 8)
    attention_back(0, 20)
    unfolded(last)
    up_job.second(order, 12)

    def out_rows(got, kept, *rows):
        return (jnp.stack(rows) + kept + got.astype(F32)).astype(BF16)

    out_own = order.mark(sealed(out_rows, order.take(got_out), kept_out, *residual))
    got_out = spread(out_own)
    attention_back(last, 0)

    keep_send = [x for s in each for x in dkvs[s]]
    kept_kv, send = sealed(lambda *xs: (jnp.stack(xs[0::2]), jnp.stack(xs[1::2])), *keep_send)
    got_kv = swap(order.mark(send), "context", n_context, 0)
    down_job.third(order, 0)
    layer_out = place_all(out_own, got_out, BF16, 0)
    mix_job.first(order, [(d_low, o_t), ([h1] * seqs, dq_t)], 0)

    def add_kv(kept, got):
        total = kept.astype(F32) + got.astype(F32)
        return total[:, 0].astype(BF16), total[:, 1].astype(BF16)

    kept_kv, send = sealed(add_kv, kept_kv, order.take(got_kv))
    got_kv = swap(order.mark(send), "context", n_context, 1)
    gate_job.second(order, 0)

    def input_partial(kept, got, *parts):
        both = merge(at, kept, got, cos_rows, sine_rows)
        rows_q, rows_kv = jnp.concatenate(parts, 1), jnp.concatenate([both[s] for s in each], 1)
        total = dot(rows_q, w_query, TT) + dot(rows_kv, w_kv, TN)
        return *fold_now(total.astype(BF16).reshape(seqs, stretch, width)), *[both[s] for s in each]

    send, kept_x, *dkv_ts = sealed(input_partial, kept_kv, order.take(got_kv), *dq_t)
    got_x = swap(order.mark(send), "tensor", n_tensor, 1)
    up_job.third(order, 0)
    down_sum = down_job.final(order, [(BLOCK, True)], 16)
    mix_job.second(order, 0)
    gate_job.third(order, 0)
    kv_job.first(order, [([h1] * seqs, dkv_ts)], 0)

    def input_grad(kept, got, sums_0, sums_1, *parts):
        back = kept + got.astype(F32)
        streams, res = jnp.stack(parts[:seqs]), jnp.stack(parts[seqs:])
        scale = lax.rsqrt(jnp.mean(streams * streams, -1, keepdims=True) + EPSILON)
        normed = streams * scale
        grad = res + norm_back(back, normed, scale, gain_1)
        sums = jnp.stack([jnp.sum(back * normed, (0, 1)), sums_0 + sums_1])
        return grad.astype(BF16), sums, core_swap(sums)

    grad_own, gain_sum, got_gain = sealed(input_grad, kept_x, order.take(got_x), *gains_2, *stream, *d_res)
    got_grad = spread(order.mark(grad_own))
    hops = [(axis, bit) for axis in ("tensor", "context", "dp") for bit in range((sizes[axis] - 1).bit_length())]
    hops.pop(0)

    def hop(us=0):
        nonlocal gain_sum, got_gain
        gain_sum = order.mark(add_pair(gain_sum, order.take(got_gain), us))
        if hops:
            axis, bit = hops.pop(0)
            got_gain = swap(gain_sum, axis, sizes[axis], bit)
            return True
        return False

    up_sum = up_job.final(order, [(BLOCK, False)], 2)
    kv_job.second(order, 2)
    hop(0)
    hop(0)
    mix_job.third(order, 0)
    kv_job.third(order, 0)
    gate_sum = gate_job.final(order, [(BLOCK, False)], 0)
    hop(4)
    grad_tokens = place_all(grad_own, got_grad, F32, 0)
    hop(0)
    while hop():
        pass
    per = width // blocks
    gain_sum = lax.dynamic_slice_in_dim(gain_sum, (me_c * n_dp + lax.axis_index("dp")) * per, per, 1)

    if fast:
        key_sum, value_sum = kv_job.final(order, [(head, True), (head, True)], 1)
        output_sum, query_sum = mix_job.final(order, [(wide, False), (wide, True)])
    else:

        def plain(left, right, dim):
            total = sum(dot(a, b, TN) for a, b in zip(left, right))
            return lax.psum_scatter(
                total.astype(BF16), ("context", "dp"), scatter_dimension=dim, tiled=True
            ).astype(F32)

        down_sum = plain(hidden, cts, 1)
        gate_sum = plain(h2, d_gate, 0)
        up_sum = plain(h2, d_up, 0)
        output_sum = plain([a.T for a in o_t], d_low, 1)
        h1s = [h1[s * stretch : (s + 1) * stretch] for s in each]
        query_sum = plain(h1s, [a.T for a in dq_t], 0)
        kv_sum = plain(h1s, [a.T for a in dkv_ts], 0)
        key_sum, value_sum = kv_sum[:, :head], kv_sum[:, head:]
    return (
        layer_out,
        grad_tokens,
        gain_sum[0],
        query_sum,
        key_sum,
        value_sum,
        output_sum,
        gain_sum[1],
        gate_sum,
        up_sum,
        down_sum,
    )


def solution(mesh):
    in_specs = (
        P("dp", "context", None),
        P("dp", None),
        P(),
        P(None, "tensor"),
        P(None, "tensor"),
        P(None, "tensor"),
        P("tensor", None),
        P(),
        P(None, "tensor"),
        P(None, "tensor"),
        P("tensor", None),
        P("dp", "context", None),
    )
    out_specs = (
        P("dp", "context", None),
        P("dp", "context", None),
        P(("context", "dp")),
        P(("context", "dp"), "tensor"),
        P(("context", "dp"), "tensor"),
        P(("context", "dp"), "tensor"),
        P("tensor", ("context", "dp")),
        P(("context", "dp")),
        P(("context", "dp"), "tensor"),
        P(("context", "dp"), "tensor"),
        P("tensor", ("context", "dp")),
    )
    run = functools.partial(local, dict(mesh.shape))
    return jax.shard_map(run, mesh=mesh, in_specs=in_specs, out_specs=out_specs, check_vma=False)
```

```python
import functools

import jax
import jax.numpy as jnp
from jax import lax
from jax.experimental import pallas as pl
from jax.experimental.pallas import tpu as pltpu
from jax.sharding import PartitionSpec as P

EPSILON = 1e-05
BF16 = jnp.bfloat16
F32 = jnp.float32
FAR = 1e30
AUX = 8
ONES_AT = 5
BLOCK = 256


def cost(us=0):
    return pl.CostEstimate(flops=int(us * 1.15e9) + 1024, bytes_accessed=1024, transcendentals=0)


COST = cost()


def params():
    return pltpu.CompilerParams(vmem_limit_bytes=56 * 2**20)


def dot(left, right, dims):
    return lax.dot_general(left, right, (dims, ((), ())), preferred_element_type=F32)


NN, NT, TN, TT = ((1,), (0,)), ((1,), (1,)), ((0,), (0,)), ((0,), (1,))


def turn(rows, cos_rows, sine_rows, sign):
    half = rows.shape[0] // 2
    first, second = rows[:half], rows[half:]
    return jnp.concatenate(
        [first * cos_rows - sign * second * sine_rows, second * cos_rows + sign * first * sine_rows], 0
    )


def project_kernel(at_ref, x_ref, gain_ref, wq_ref, wkv_ref, cos_ref, sin_ref, h_ref, q_ref, kv_ref):
    x = x_ref[...].astype(F32)
    scale = lax.rsqrt(jnp.mean(x * x, -1, keepdims=True) + EPSILON)
    h = (x * scale * gain_ref[...]).astype(BF16)
    part = h.shape[0] // 2
    swapped = at_ref[2] * part
    h_ref[pl.ds(pl.multiple_of(swapped, part), part)] = h[:part]
    h_ref[pl.ds(pl.multiple_of(part - swapped, part), part)] = h[part:]
    cos_rows, sine_rows = cos_ref[...], sin_ref[...]
    head = kv_ref.shape[0] // 2
    score_scale = head ** (-0.5)
    q = dot(h, wq_ref[...], NN).T
    for at in range(0, q.shape[0], head):
        q_ref[at : at + head] = (turn(q[at : at + head], cos_rows, sine_rows, 1.0) * score_scale).astype(BF16)
    kv = dot(wkv_ref[...], h, NT)
    kv_ref[:head] = turn(kv[:head], cos_rows, sine_rows, 1.0).astype(BF16)
    kv_ref[head:] = kv[head:].astype(BF16)


def project(at, x, gain, w_query, w_kv, cos_rows, sine_rows, stretch):
    rows, width = x.shape
    step = stretch // 2
    wide, both = w_query.shape[1], w_kv.shape[0]
    half = cos_rows.shape[0]
    whole = lambda shape: pl.BlockSpec(shape, lambda i, at: (0, 0))
    return pl.pallas_call(
        project_kernel,
        grid_spec=pltpu.PrefetchScalarGridSpec(
            num_scalar_prefetch=1,
            grid=(rows // step,),
            in_specs=[
                pl.BlockSpec((step, width), lambda i, at: (i, 0)),
                whole((1, width)),
                whole((width, wide)),
                whole((both, width)),
                pl.BlockSpec((half, step), lambda i, at: (0, i)),
                pl.BlockSpec((half, step), lambda i, at: (0, i)),
            ],
            out_specs=[
                pl.BlockSpec((step, width), lambda i, at: (i + at[1] - 2 * at[1] * lax.rem(i, 2), 0)),
                pl.BlockSpec((wide, step), lambda i, at: (0, i)),
                pl.BlockSpec((both, step), lambda i, at: (0, i)),
            ],
        ),
        out_shape=[
            jax.ShapeDtypeStruct((rows, width), BF16),
            jax.ShapeDtypeStruct((wide, rows), BF16),
            jax.ShapeDtypeStruct((both, rows), BF16),
        ],
        compiler_params=params(),
        cost_estimate=COST,
    )(at, x, gain, w_query, w_kv, cos_rows, sine_rows)


def pieces(value):
    high = value.astype(BF16).astype(F32)
    middle = (value - high).astype(BF16).astype(F32)
    low = value - high - middle
    return high, middle, low


def key_rows(kv, seg):
    head, count = kv.shape[0] // 2, kv.shape[1]
    row = lax.broadcasted_iota(jnp.int32, (2 * AUX, count), 0)
    extra = jnp.where(row < ONES_AT, jnp.where(seg == row, 0.0, -FAR), jnp.where(row < AUX, 1.0, 0.0))
    rest = jnp.zeros((head - 2 * AUX, count), F32)
    return jnp.concatenate([kv[:head].astype(F32), extra, rest], 0)


def value_rows(kv, fill):
    head, count = kv.shape[0] // 2, kv.shape[1]
    row = lax.broadcasted_iota(jnp.int32, (fill, count), 0)
    return jnp.concatenate([kv[head:].astype(F32), jnp.where(row < 3, 1.0, 0.0)], 0)


def places(at_ref, count):
    quarter = count // 4
    mine = 2 * at_ref[1] + at_ref[2]
    return [pl.ds(pl.multiple_of((b ^ mine) * quarter, quarter), quarter) for b in range(4)]


def causal(scores):
    key_at = lax.broadcasted_iota(jnp.int32, scores.shape, 0)
    query_at = lax.broadcasted_iota(jnp.int32, scores.shape, 1)
    return jnp.where(key_at <= query_at, scores, -FAR)


def attend_kernel(far_count, at_ref, q_ref, seg_ref, *refs):
    kv_refs = refs[: far_count + 1]
    qa_ref, o_ref, full_ref = refs[far_count + 1 : far_count + 4]
    ka_ref, va_ref = refs[far_count + 4 :]
    me = at_ref[0]
    head = kv_refs[0].shape[0] // 2
    count = q_ref.shape[1]

    @pl.when(pl.program_id(0) == 0)
    def _():
        for d, kv_ref in enumerate(kv_refs):
            kv = kv_ref[...]
            ka_ref[d] = key_rows(kv, seg_ref[d : d + 1]).T.astype(BF16)
            va_ref[d] = value_rows(kv, 2 * AUX).astype(BF16)

    row = lax.broadcasted_iota(jnp.int32, (2 * AUX, count), 0)
    same = jnp.where((seg_ref[0:1] == row) & (row < ONES_AT), 1.0, 0.0)
    rest = jnp.zeros((head - 2 * AUX, count), F32)

    def heads(blocks):
        for h in range(q_ref.shape[0] // head):
            q = q_ref[h * head : (h + 1) * head].astype(F32)
            qa = jnp.concatenate([q, same, rest], 0).astype(BF16)
            scores = [dot(ka_ref[d], qa, NN) for d in range(blocks)]
            scores[0] = causal(scores[0])
            m = jnp.max(scores[0], 0, keepdims=True)
            for d in range(1, blocks):
                m = jnp.maximum(m, jnp.max(scores[d], 0, keepdims=True))
            acc = None
            for d in range(blocks):
                term = dot(va_ref[d], jnp.exp(scores[d] - m).astype(BF16), NN)
                acc = term if acc is None else acc + term
            total = acc[head : head + 1]
            out = acc[:head] / total
            for b, place in enumerate(places(at_ref, count)):
                quarter = out[:, b * (count // 4) : (b + 1) * (count // 4)]
                full_ref[h * head : (h + 1) * head, place] = quarter
                o_ref[h * head : (h + 1) * head, place] = quarter.astype(BF16)
            high, middle, low = pieces(-(m + jnp.log(total)))
            extra = jnp.where(
                row == ONES_AT, high, jnp.where(row == ONES_AT + 1, middle, jnp.where(row == ONES_AT + 2, low, same))
            )
            qa_ref[h] = jnp.concatenate([q, extra, rest], 0).astype(BF16)

    for blocks in range(1, far_count + 2):
        pl.when(me == blocks - 1)(functools.partial(heads, blocks))


def attend(me, q, kvs, segs, item, group=2):
    far_count = len(kvs) - 1
    both = kvs[0].shape[0]
    head = both // 2
    wide, count = q.shape[0], segs.shape[-1]
    heads = wide // head
    return pl.pallas_call(
        functools.partial(attend_kernel, far_count),
        grid_spec=pltpu.PrefetchScalarGridSpec(
            num_scalar_prefetch=1,
            grid=(heads // group,),
            in_specs=[
                pl.BlockSpec((group * head, count), lambda h, at: (h, item)),
                pl.BlockSpec((None, far_count + 1, count), lambda h, at: (item, 0, 0)),
            ]
            + [pl.BlockSpec((both, count), lambda h, at: (0, item))] * (far_count + 1),
            out_specs=[
                pl.BlockSpec((group, both, count), lambda h, at: (h, 0, 0)),
                pl.BlockSpec((group * head, count), lambda h, at: (h, 0)),
                pl.BlockSpec((group * head, count), lambda h, at: (h, 0)),
            ],
            scratch_shapes=[
                pltpu.VMEM((far_count + 1, count, both), BF16),
                pltpu.VMEM((far_count + 1, head + 2 * AUX, count), BF16),
            ],
        ),
        out_shape=[
            jax.ShapeDtypeStruct((heads, both, count), BF16),
            jax.ShapeDtypeStruct((wide, count), BF16),
            jax.ShapeDtypeStruct((wide, count), F32),
        ],
        compiler_params=params(),
        cost_estimate=COST,
    )(me, q, segs, *kvs)


def back_kernel(far_count, at_ref, qa_ref, do_ref, full_ref, seg_ref, cos_ref, sin_ref, *refs):
    kv_refs = refs[: far_count + 1]
    dq_ref, keep_ref, send_ref = refs[far_count + 1 : far_count + 4]
    ka_ref, kt_ref, va_ref, dk_ref, dv_ref, dq_acc = refs[far_count + 4 :]
    me = at_ref[0]
    head, count = do_ref.shape
    step = pl.program_id(0)

    @pl.when(step == 0)
    def _():
        for d, kv_ref in enumerate(kv_refs):
            kv = kv_ref[...]
            ka_ref[d] = key_rows(kv, seg_ref[d : d + 1]).T.astype(BF16)
            kt_ref[d] = kv[:head]
            va_ref[d] = value_rows(kv, head).T.astype(BF16)
        dk_ref[...] = jnp.zeros_like(dk_ref)
        dv_ref[...] = jnp.zeros_like(dv_ref)

    qa = qa_ref[...]
    here = places(at_ref, count)
    do = jnp.concatenate([do_ref[:, place] for place in here], 1).astype(F32)
    full = jnp.concatenate([full_ref[:, place] for place in here], 1)
    high, middle, low = pieces(-jnp.sum(do * full, 0, keepdims=True))
    row = lax.broadcasted_iota(jnp.int32, (2 * AUX, count), 0)
    extra = jnp.where(row == 0, high, jnp.where(row == 1, middle, jnp.where(row == 2, low, 0.0)))
    rest = jnp.zeros((head - 2 * AUX, count), F32)
    da = jnp.concatenate([do, extra, rest], 0).astype(BF16)
    def run(blocks):
        total = None
        for d in range(blocks):
            scores = dot(ka_ref[d], qa, NN)
            probs = jnp.exp(causal(scores) if d == 0 else scores)
            d_scores = (probs * dot(va_ref[d], da, NN)).astype(BF16)
            dv_ref[d] += dot(probs.astype(BF16), da[:head], NT)
            dk_ref[d] += dot(d_scores, qa[:head], NT)
            update = dot(kt_ref[d], d_scores, NN)
            total = update if total is None else total + update
        dq_acc[...] = total

    for blocks in range(1, far_count + 2):
        pl.when(me == blocks - 1)(functools.partial(run, blocks))
    score_scale = head ** (-0.5)
    dq = turn(dq_acc[...] * score_scale, cos_ref[...], sin_ref[...], -1.0).astype(BF16)
    for b, place in enumerate(here):
        dq_ref[:, place] = dq[:, b * (count // 4) : (b + 1) * (count // 4)]

    @pl.when(step == pl.num_programs(0) - 1)
    def _():
        keep_ref[...] = jnp.zeros_like(keep_ref)
        send_ref[...] = jnp.zeros_like(send_ref)
        keep_ref[0] = jnp.concatenate([dk_ref[0], dv_ref[0]], 1).T.astype(BF16)
        for d in range(1, far_count + 1):

            @pl.when(d <= me)
            def _(d=d):
                part = jnp.concatenate([dk_ref[d], dv_ref[d]], 1).T.astype(BF16)
                place = (me - d) ^ me

                @pl.when(place % 2 == 0)
                def _():
                    keep_ref[place // 2] = part

                @pl.when(place % 2 == 1)
                def _():
                    send_ref[place // 2] = part


def attend_back(me, qa, do, full, kvs, segs, cos_rows, sine_rows, item, us):
    far_count = len(kvs) - 1
    heads, both, count = qa.shape
    head = both // 2
    wide, half = heads * head, cos_rows.shape[0]
    return pl.pallas_call(
        functools.partial(back_kernel, far_count),
        grid_spec=pltpu.PrefetchScalarGridSpec(
            num_scalar_prefetch=1,
            grid=(heads,),
            in_specs=[
                pl.BlockSpec((None, both, count), lambda h, at: (h, 0, 0)),
                pl.BlockSpec((head, count), lambda h, at: (h, 0)),
                pl.BlockSpec((head, count), lambda h, at: (h, 0)),
                pl.BlockSpec((None, far_count + 1, count), lambda h, at: (item, 0, 0)),
                pl.BlockSpec((half, count), lambda h, at: (0, item)),
                pl.BlockSpec((half, count), lambda h, at: (0, item)),
            ]
            + [pl.BlockSpec((both, count), lambda h, at: (0, item))] * (far_count + 1),
            out_specs=[pl.BlockSpec((head, count), lambda h, at: (h, 0))]
            + [pl.BlockSpec(((far_count + 1) // 2, both, count), lambda h, at: (0, 0, 0))] * 2,
            scratch_shapes=[
                pltpu.VMEM((far_count + 1, count, both), BF16),
                pltpu.VMEM((far_count + 1, head, count), BF16),
                pltpu.VMEM((far_count + 1, count, both), BF16),
                pltpu.VMEM((far_count + 1, count, head), F32),
                pltpu.VMEM((far_count + 1, count, head), F32),
                pltpu.VMEM((head, count), F32),
            ],
        ),
        out_shape=[jax.ShapeDtypeStruct((wide, count), BF16)]
        + [jax.ShapeDtypeStruct(((far_count + 1) // 2, both, count), BF16)] * 2,
        compiler_params=params(),
        cost_estimate=cost(us),
    )(me, qa, do, full, segs, cos_rows, sine_rows, *kvs)


def merge_kernel(at_ref, own_ref, recv_ref, cos_ref, sin_ref, out_ref):
    head, count = out_ref.shape[0] // 2, out_ref.shape[1]
    total = own_ref[...].astype(F32) + recv_ref[...].astype(F32)
    turned = turn(total[:head], cos_ref[...], sin_ref[...], -1.0)
    out = jnp.concatenate([turned, total[head:]], 0).astype(BF16)
    for b, place in enumerate(places(at_ref, count)):
        out_ref[:, place] = out[:, b * (count // 4) : (b + 1) * (count // 4)]


def merge(at, own, received, cos_rows, sine_rows):
    seqs, both, count = own.shape
    half = cos_rows.shape[0]
    block = pl.BlockSpec((None, both, count), lambda s, at: (s, 0, 0))
    table = pl.BlockSpec((half, count), lambda s, at: (0, s))
    return pl.pallas_call(
        merge_kernel,
        grid_spec=pltpu.PrefetchScalarGridSpec(
            num_scalar_prefetch=1,
            grid=(seqs,),
            in_specs=[block, block, table, table],
            out_specs=block,
        ),
        out_shape=jax.ShapeDtypeStruct(own.shape, BF16),
        compiler_params=params(),
        cost_estimate=COST,
    )(at, own, received, cos_rows, sine_rows)


def product(order, pieces, *items):
    total = order.mark(sum(dot(a, b, form) for a, b, form in items).astype(BF16))
    half = total.shape[0] // 2
    return cut(total[half:], pieces), total[:half]


def cut(x, pieces):
    size = x.shape[0] // pieces
    return [x[j * size : (j + 1) * size] for j in range(pieces)]


def unfold_kernel(*refs):
    *part_refs, w_ref, out_ref, full_ref = refs
    size = part_refs[0].shape[0]
    for j, ref in enumerate(part_refs):
        full_ref[j * size : (j + 1) * size] = ref[...]
    out_ref[...] = dot(w_ref[...], full_ref[...], NT).astype(BF16)


def unfold(parts, w):
    rows, width = len(parts) * parts[0].shape[0], parts[0].shape[1]
    return pl.pallas_call(
        unfold_kernel,
        out_shape=[
            jax.ShapeDtypeStruct((w.shape[0], rows), BF16),
            jax.ShapeDtypeStruct((rows, width), BF16),
        ],
        compiler_params=params(),
        cost_estimate=COST,
    )(*parts, w)


def grad_kernel(groups, has_recv, split, table_ref, *refs):
    out = []
    for form, pairs in groups:
        total = None
        for narrow, wide in pairs:
            both = jnp.concatenate([refs[wide][...], refs[wide + 1][...]], 1)
            if form == TN:
                term = dot(both, refs[narrow][...], TN)
            else:
                term = dot(refs[narrow][...], both, NN)
            total = term if total is None else total + term
        out.append(total)
    at = len(refs) - (2 if split else 1) - (1 if has_recv else 0)
    recv = None
    if has_recv:
        recv, at = refs[at], at + 1

    def put(ref):
        if groups[0][0] == TN:
            rows = out[0].shape[0] // 2
            for j in range(2):
                block = out[0][j * rows : (j + 1) * rows]
                ref[j] = (block if recv is None else block + recv[j].astype(F32)).astype(BF16)
            return
        row = 0
        for total in out:
            count, wide = total.shape[0], total.shape[1] // 2
            for j in range(2):
                block = total[:, j * wide : (j + 1) * wide]
                if recv is not None:
                    block = block + recv[j, row : row + count].astype(F32)
                ref[j, row : row + count] = block.astype(BF16)
            row += count

    if not split:
        put(refs[at])
        return
    first = pl.program_id(0) < split // 2
    pl.when(first)(lambda: put(refs[at]))
    pl.when(jnp.logical_not(first))(lambda: put(refs[at + 1]))


def grad_blocks(table, form, sets, recv=None, split=0, us=0):
    n = table.shape[0]
    ins, specs, groups = [], [], []
    for wide_set, narrow_set in sets:
        pairs = []
        for s, (wide, narrow) in enumerate(zip(wide_set, narrow_set)):
            pairs.append((len(ins), len(ins) + 1))
            ins += [narrow, wide, wide]
            specs.append(pl.BlockSpec(narrow.shape, lambda i, t: (0, 0)))
            tokens = narrow.shape[0 if form == TN else 1]
            item = s if wide.shape[0] > tokens else 0
            for j in range(2):
                specs.append(pl.BlockSpec((tokens, BLOCK), lambda i, t, j=j, item=item: (item, t[2 * i + j])))
        groups.append((form, pairs))
    if form == TN:
        block = (BLOCK, sets[0][1][0].shape[1])
    else:
        block = (sum(narrow_set[0].shape[0] for _, narrow_set in sets), BLOCK)
    two = (2,) + block
    if recv is not None:
        ins.append(recv)
        specs.append(pl.BlockSpec(two, lambda i, t: (lax.rem(i + split // 2, n // 2), 0, 0)))
    if split:
        out_specs = [
            pl.BlockSpec(two, lambda i, t: (jnp.minimum(i, split // 2 - 1), 0, 0)),
            pl.BlockSpec(two, lambda i, t: (jnp.maximum(i - split // 2, 0), 0, 0)),
        ]
        out_shape = [jax.ShapeDtypeStruct((split,) + block, BF16), jax.ShapeDtypeStruct((n - split,) + block, BF16)]
    else:
        out_specs = pl.BlockSpec(two, lambda i, t: (i, 0, 0))
        out_shape = jax.ShapeDtypeStruct((n,) + block, BF16)
    return pl.pallas_call(
        functools.partial(grad_kernel, groups, recv is not None, split),
        grid_spec=pltpu.PrefetchScalarGridSpec(num_scalar_prefetch=1, grid=(n // 2,), in_specs=specs, out_specs=out_specs),
        out_shape=out_shape,
        compiler_params=params(),
        cost_estimate=cost(us),
    )(table, *ins)


def add_send_kernel(keep_ref, recv_ref, send_ref, rest_ref):
    send_ref[...] = (keep_ref[1].astype(F32) + recv_ref[1].astype(F32)).astype(BF16)
    rest_ref[...] = keep_ref[0].astype(F32) + recv_ref[0].astype(F32)


def add_send(keep, recv, us):
    shape = keep.shape[1:]
    return pl.pallas_call(
        add_send_kernel,
        out_shape=[jax.ShapeDtypeStruct(shape, BF16), jax.ShapeDtypeStruct(shape, F32)],
        compiler_params=params(),
        cost_estimate=cost(us),
    )(keep, recv)


def add_pair_kernel(a_ref, b_ref, out_ref):
    out_ref[...] = a_ref[...] + b_ref[...]


def add_pair(a, b, us):
    return pl.pallas_call(
        add_pair_kernel,
        out_shape=jax.ShapeDtypeStruct(a.shape, a.dtype),
        compiler_params=params(),
        cost_estimate=cost(us),
    )(a, b)


def add_last_kernel(turned, rest_ref, got_ref, *out_refs):
    row = 0
    for (count, flip), out_ref in zip(turned, out_refs):
        total = rest_ref[row : row + count] + got_ref[row : row + count].astype(F32)
        out_ref[...] = total.T if flip else total
        row += count


def add_last(rest, got, turned, us):
    wide = rest.shape[1]
    return pl.pallas_call(
        functools.partial(add_last_kernel, turned),
        out_shape=[
            jax.ShapeDtypeStruct((wide, count) if flip else (count, wide), F32) for count, flip in turned
        ],
        compiler_params=params(),
        cost_estimate=cost(us),
    )(rest, got)


class Order:
    def __init__(self):
        self.last = None

    def take_all(self, xs):
        if self.last is not None:
            xs = lax.optimization_barrier((self.last, *xs))[1:]
        return xs

    def take(self, *xs):
        xs = self.take_all(xs)
        return xs if len(xs) > 1 else xs[0]

    def mark(self, x):
        self.last = x
        return x


def sealed(fn, *args):
    def never(*args):
        return jax.tree.map(lambda leaf: jnp.zeros(leaf.shape, leaf.dtype), jax.eval_shape(fn, *args))

    return lax.cond(lax.axis_index("tensor") >= 0, fn, never, *args)


class Scatter:
    def __init__(self, stages, sizes, form, fast):
        self.stages, self.sizes, self.form, self.fast = stages, sizes, form, fast
        ctx, dp = lax.axis_index("context"), lax.axis_index("dp")
        blocks = []
        for p in range(2 ** len(stages)):
            c, d = ctx, dp
            for j, (axis, bit) in enumerate(stages):
                if p >> (len(stages) - 1 - j) & 1:
                    if axis == "context":
                        c = c ^ (1 << bit)
                    else:
                        d = d ^ (1 << bit)
            blocks.append(c * sizes["dp"] + d)
        self.away = jnp.stack(blocks[4:]).astype(jnp.int32)
        self.near = jnp.stack([blocks[p] for p in (2, 3, 0, 1)]).astype(jnp.int32)

    def send(self, j, x):
        axis, bit = self.stages[j]
        self.got = swap(x, axis, self.sizes[axis], bit)

    def first(self, order, sets, us=0):
        if self.fast:
            wide = order.take(*sets[0][0])
            self.sets = [(list(wide), sets[0][1])] + sets[1:]
            self.send(0, order.mark(grad_blocks(self.away, self.form, self.sets, us=us)))

    def second(self, order, us=0):
        if self.fast:
            send, self.keep = grad_blocks(self.near, self.form, self.sets, order.take(self.got), 2, us)
            self.send(1, order.mark(send))

    def third(self, order, us=0):
        if self.fast:
            send, self.rest = add_send(self.keep, order.take(self.got), us)
            self.send(2, order.mark(send))

    def final(self, order, turned, us=0):
        if self.fast:
            out = add_last(self.rest, order.take(self.got), turned, us)
            order.mark(out[0])
            return out if len(out) > 1 else out[0]


def place_kernel(at_ref, *refs):
    *part_refs, out_ref = refs
    quarter = part_refs[0].shape[0]
    mine = 2 * at_ref[1] + at_ref[2]
    for p, ref in enumerate(part_refs):
        where = pl.ds(pl.multiple_of((p ^ mine) * quarter, quarter), quarter)
        out_ref[where] = ref[...].astype(out_ref.dtype)


def place(at, parts, dtype, us):
    seqs, quarter, width = parts[0].shape
    spec = lambda rows: pl.BlockSpec((None, rows, width), lambda s, at: (s, 0, 0))
    return pl.pallas_call(
        place_kernel,
        grid_spec=pltpu.PrefetchScalarGridSpec(
            num_scalar_prefetch=1, grid=(seqs,), in_specs=[spec(quarter)] * 4, out_specs=spec(4 * quarter)
        ),
        out_shape=jax.ShapeDtypeStruct((seqs, 4 * quarter, width), dtype),
        compiler_params=params(),
        cost_estimate=cost(us),
    )(at, *parts)


def swap(x, axis, size, bit):
    return lax.ppermute(x, axis, [(i, i ^ (1 << bit)) for i in range(size)])


def rows_at(x, at, count):
    return lax.dynamic_slice_in_dim(x, at, count, 0)


def local(sizes, tokens, segment_ids, norm_gain_1, w_query, w_key, w_value, w_output, norm_gain_2, w_gate, w_up, w_down, cotangent):
    seqs, stretch, width = tokens.shape
    rows = seqs * stretch
    head = w_key.shape[1]
    wide = w_query.shape[1]
    n_tensor, n_context, n_dp = sizes["tensor"], sizes["context"], sizes["dp"]
    me_t, me_c = lax.axis_index("tensor"), lax.axis_index("context")
    core, high = me_t % 2, me_t // 2
    mine = 2 * core + high
    half, quarter = stretch // 2, stretch // 4
    offset = me_c * stretch
    order = Order()
    each = range(seqs)

    seg_here = lax.dynamic_slice_in_dim(segment_ids, offset, stretch, 1)
    start = jnp.zeros(seg_here.shape, jnp.int32)
    for number in range(1, ONES_AT):
        before = jnp.sum((segment_ids < number).astype(jnp.int32), 1, keepdims=True)
        start = jnp.where(seg_here == number, before, start)
    positions = (offset + jnp.arange(stretch, dtype=jnp.int32))[None, :] - start
    frequency = 10000.0 ** (-(2.0 * jnp.arange(head // 2, dtype=F32)) / head)
    angles = frequency[:, None] * positions.reshape(1, rows).astype(F32)
    cos_rows, sine_rows = jnp.cos(angles), jnp.sin(angles)
    padded = jnp.concatenate([jnp.zeros((seqs, (n_context - 1) * stretch), jnp.int32), segment_ids], 1)
    segs = jnp.stack(
        [
            lax.dynamic_slice_in_dim(padded, offset + (n_context - 1 - d) * stretch, stretch, 1)
            for d in range(n_context)
        ],
        1,
    )
    at = jnp.stack([me_c, core, high]).astype(jnp.int32)

    x_rows = tokens.reshape(rows, width)
    ct_rows = cotangent.reshape(rows, width)
    gain_1, gain_2 = norm_gain_1.reshape(1, width), norm_gain_2.reshape(1, width)
    w_kv = jnp.concatenate([w_key.T, w_value.T], 0)
    h1, q_t, kv_t = project(at, x_rows, gain_1, w_query, w_kv, cos_rows, sine_rows, stretch)
    order.mark(kv_t)
    kvs = [kv_t] + [
        lax.ppermute(kv_t, "context", [(i, i + d) for i in range(n_context - d)]) for d in range(1, n_context)
    ]

    def own_order(x, s):
        return jnp.concatenate([rows_at(x, s * stretch + (p ^ mine) * quarter, quarter) for p in range(4)], 0)

    def fold(pair):
        sends, keep = pair
        return [swap(x, "tensor", n_tensor, 0) for x in sends], keep

    def join(pieces):
        return jnp.concatenate(order.take_all(pieces), 0)

    def fold_more(kept, got):
        total = kept.astype(F32) + got.astype(F32)
        send = total[quarter:].astype(BF16)
        return swap(order.mark(send), "tensor", n_tensor, 1), total[:quarter]

    def core_swap(x):
        return swap(x, "tensor", n_tensor, 0)

    def core_swaps(first, second):
        first = core_swap(first)
        first, second = lax.optimization_barrier((first, second))
        return first, core_swap(second)

    def fold_now(total):
        near = total[:, :half].astype(F32) + core_swap(total[:, half:]).astype(F32)
        return near[:, quarter:].astype(BF16), near[:, :quarter]

    def spread(part):
        return swap(part, "tensor", n_tensor, 1)

    cts, d_hidden = [], []
    for s in each:
        cts.append(own_order(order.take(ct_rows), s))
        d_hidden.append(order.mark(dot(cts[s], w_down, NT)))

    stream = [rows_at(x_rows, s * stretch + mine * quarter, quarter).astype(F32) for s in each]
    ct_own = [rows_at(ct_rows, s * stretch + mine * quarter, quarter).astype(F32) for s in each]

    qa, o_t, full_o = [None] * seqs, [None] * seqs, [None] * seqs
    got_o, kept_o = [None] * seqs, [None] * seqs
    residual, scale_2, normed_2, h2_own, got_h = ([None] * seqs for _ in range(5))

    def after_attention(s):
        total = kept_o[s] + order.take(got_o[s]).astype(F32)
        residual[s] = stream[s] + total
        scale_2[s] = lax.rsqrt(jnp.mean(residual[s] * residual[s], -1, keepdims=True) + EPSILON)
        normed_2[s] = residual[s] * scale_2[s]
        h2_own[s] = order.mark((normed_2[s] * gain_2).astype(BF16))
        got_h[s] = spread(h2_own[s])

    for s in each:
        qa[s], o_t[s], full_o[s] = attend(at, order.take(q_t), kvs, segs, s)
        order.mark(o_t[s])
        if s:
            after_attention(s - 1)
        got, kept = fold(product(order, 1, (order.take(o_t[s]), w_output, TN)))
        got_o[s], kept_o[s] = fold_more(kept, join(got))

    hidden, d_gate, d_up, h2 = ([None] * seqs for _ in range(4))
    got_b, kept_b = [None] * seqs, [None] * seqs

    def back_sealed(s):
        def run(left, right):
            return fold_now((dot(left, w_gate, NT) + dot(right, w_up, NT)).astype(BF16)[None])

        send, kept = sealed(run, *order.take(d_gate[s], d_up[s]))
        got_b[s], kept_b[s] = swap(order.mark(send)[0], "tensor", n_tensor, 1), kept[0]

    d_res, d_low_own, got_d, gains_2 = ([None] * seqs for _ in range(4))

    def norm_back(scaled_grad, normed, scale, gain):
        scaled = scaled_grad * gain
        return scale * (scaled - normed * jnp.mean(scaled * normed, -1, keepdims=True))

    def after_back(s):
        def run(kept, got, normed, scale, own):
            back = kept + got.astype(F32)
            grad = own + norm_back(back, normed, scale, gain_2)
            return grad.astype(BF16), grad, jnp.sum(back * normed, 0)

        d_low_own[s], d_res[s], gains_2[s] = sealed(
            run, kept_b[s], order.take(got_b[s]), normed_2[s], scale_2[s], ct_own[s]
        )
        got_d[s] = spread(order.mark(d_low_own[s]))

    blocks = n_context * n_dp
    fast = width // blocks == BLOCK and n_dp == 2 and n_context == 4
    x_first = [("dp", 0), ("context", 0), ("context", 1)]
    z_first = [("context", 0), ("dp", 0), ("context", 1)]
    down_job = Scatter(x_first, sizes, TN, fast)
    gate_job = Scatter(x_first, sizes, TN, fast)
    up_job = Scatter(z_first, sizes, TN, fast)
    mix_job = Scatter(x_first, sizes, NN, fast)
    kv_job = Scatter(x_first, sizes, NN, fast)

    def feed_forward(part, got, d_rows):
        rows = jnp.concatenate([part, got, *core_swaps(part, got)], 0)
        gate, up = dot(rows, w_gate, NN), dot(rows, w_up, NN)
        sig = jax.nn.sigmoid(gate)
        return (
            rows,
            (gate * sig * up).astype(BF16),
            (d_rows * up * sig * (1.0 + gate * (1.0 - sig))).astype(BF16),
            (d_rows * gate * sig).astype(BF16),
        )

    for s in each:
        h2[s], hidden[s], d_gate[s], d_up[s] = sealed(feed_forward, h2_own[s], order.take(got_h[s]), d_hidden[s])
        order.mark(d_up[s])
        if s + 1 < seqs:
            after_attention(s + 1)
            back_sealed(s)

    d_low, dq_t, dkvs = [None] * seqs, [None] * seqs, [None] * seqs

    do_t = [None] * seqs

    def unfolded(s):
        def run(part, got):
            return unfold([part, got, *core_swaps(part, got)], w_output)

        do_t[s], d_low[s] = sealed(run, d_low_own[s], order.take(got_d[s]))
        order.mark(do_t[s])

    def attention_back(s, us):
        dq_t[s], *dkvs[s] = attend_back(
            at, qa[s], order.take(do_t[s]), full_o[s], kvs, segs, cos_rows, sine_rows, s, us
        )
        order.mark(dq_t[s])

    def swap_quarters(part, got):
        got = order.take(got)
        far = sealed(core_swaps, part, got)
        order.mark(far[1])
        return [part, got, *far]

    def put_quarters(quarters, dtype, us=0):
        return order.mark(place(at, [order.take(quarters[0]), *quarters[1:]], dtype, us))

    last = seqs - 1
    down_job.first(order, [(cts, hidden)], 0)
    for s in range(last):
        after_back(s)
    back_sealed(last)
    unfolded(0)
    up_job.first(order, [(h2, d_up)], 20)
    after_back(last)
    gate_job.first(order, [(h2, d_gate)], 0)

    def down_partial(*parts):
        total = dot(jnp.concatenate(parts, 0), w_down, NN).astype(BF16)
        return fold_now(total.reshape(seqs, stretch, width))

    send, kept_out = sealed(down_partial, *order.take_all(hidden))
    got_out = swap(order.mark(send), "tensor", n_tensor, 1)
    down_job.second(order, 8)
    attention_back(0, 20)
    unfolded(last)
    up_job.second(order, 12)

    def out_rows(got, kept, *rows):
        return (jnp.stack(rows) + kept + got.astype(F32)).astype(BF16)

    out_own = order.mark(sealed(out_rows, order.take(got_out), kept_out, *residual))
    got_out = spread(out_own)
    attention_back(last, 0)

    keep_send = [x for s in each for x in dkvs[s]]
    kept_kv, send = sealed(lambda *xs: (jnp.stack(xs[0::2]), jnp.stack(xs[1::2])), *keep_send)
    got_kv = swap(order.mark(send), "context", n_context, 0)
    down_job.third(order, 0)
    quarters = swap_quarters(out_own, got_out)
    mix_job.first(order, [(d_low, o_t), ([h1] * seqs, dq_t)], 0)

    def add_kv(kept, got):
        total = kept.astype(F32) + got.astype(F32)
        return total[:, 0].astype(BF16), total[:, 1].astype(BF16)

    kept_kv, send = sealed(add_kv, kept_kv, order.take(got_kv))
    got_kv = swap(order.mark(send), "context", n_context, 1)
    gate_job.second(order)
    layer_out = put_quarters(quarters, BF16)

    def input_partial(kept, got, *parts):
        both = merge(at, kept, got, cos_rows, sine_rows)
        rows_q, rows_kv = jnp.concatenate(parts, 1), jnp.concatenate([both[s] for s in each], 1)
        total = dot(rows_q, w_query, TT) + dot(rows_kv, w_kv, TN)
        return *fold_now(total.astype(BF16).reshape(seqs, stretch, width)), *[both[s] for s in each]

    send, kept_x, *dkv_ts = sealed(input_partial, kept_kv, order.take(got_kv), *dq_t)
    got_x = swap(order.mark(send), "tensor", n_tensor, 1)
    up_job.third(order, 0)
    down_sum = down_job.final(order, [(BLOCK, True)], 16)
    mix_job.second(order, 0)
    gate_job.third(order, 0)
    kv_job.first(order, [([h1] * seqs, dkv_ts)], 0)

    def input_grad(kept, got, sums_0, sums_1, *parts):
        back = kept + got.astype(F32)
        streams, res = jnp.stack(parts[:seqs]), jnp.stack(parts[seqs:])
        scale = lax.rsqrt(jnp.mean(streams * streams, -1, keepdims=True) + EPSILON)
        normed = streams * scale
        grad = res + norm_back(back, normed, scale, gain_1)
        sums = jnp.stack([jnp.sum(back * normed, (0, 1)), sums_0 + sums_1])
        return grad.astype(BF16), sums, core_swap(sums)

    grad_own, gain_sum, got_gain = sealed(input_grad, kept_x, order.take(got_x), *gains_2, *stream, *d_res)
    got_grad = spread(order.mark(grad_own))
    hops = [(axis, bit) for axis in ("tensor", "context", "dp") for bit in range((sizes[axis] - 1).bit_length())]
    hops.pop(0)

    def hop(us=0):
        nonlocal gain_sum, got_gain
        gain_sum = order.mark(add_pair(gain_sum, order.take(got_gain), us))
        if hops:
            axis, bit = hops.pop(0)
            got_gain = swap(gain_sum, axis, sizes[axis], bit)
            return True
        return False

    up_sum = up_job.final(order, [(BLOCK, False)], 2)
    kv_job.second(order, 2)
    hop(0)
    hop(0)
    mix_job.third(order, 0)
    kv_job.third(order, 0)
    gate_sum = gate_job.final(order, [(BLOCK, False)], 0)
    hop(4)
    grad_tokens = put_quarters(swap_quarters(grad_own, got_grad), F32)
    hop(0)
    while hop():
        pass
    per = width // blocks
    gain_sum = lax.dynamic_slice_in_dim(gain_sum, (me_c * n_dp + lax.axis_index("dp")) * per, per, 1)

    if fast:
        key_sum, value_sum = (x.T for x in kv_job.final(order, [(head, False), (head, False)], 1))
        output_sum, query_sum = mix_job.final(order, [(wide, False), (wide, True)])
    else:

        def plain(left, right, dim):
            total = sum(dot(a, b, TN) for a, b in zip(left, right))
            return lax.psum_scatter(
                total.astype(BF16), ("context", "dp"), scatter_dimension=dim, tiled=True
            ).astype(F32)

        down_sum = plain(hidden, cts, 1)
        gate_sum = plain(h2, d_gate, 0)
        up_sum = plain(h2, d_up, 0)
        output_sum = plain([a.T for a in o_t], d_low, 1)
        h1s = [h1[s * stretch : (s + 1) * stretch] for s in each]
        query_sum = plain(h1s, [a.T for a in dq_t], 0)
        kv_sum = plain(h1s, [a.T for a in dkv_ts], 0)
        key_sum, value_sum = kv_sum[:, :head], kv_sum[:, head:]
    return (
        layer_out,
        grad_tokens,
        gain_sum[0],
        query_sum,
        key_sum,
        value_sum,
        output_sum,
        gain_sum[1],
        gate_sum,
        up_sum,
        down_sum,
    )


def solution(mesh):
    in_specs = (
        P("dp", "context", None),
        P("dp", None),
        P(),
        P(None, "tensor"),
        P(None, "tensor"),
        P(None, "tensor"),
        P("tensor", None),
        P(),
        P(None, "tensor"),
        P(None, "tensor"),
        P("tensor", None),
        P("dp", "context", None),
    )
    out_specs = (
        P("dp", "context", None),
        P("dp", "context", None),
        P(("context", "dp")),
        P(("context", "dp"), "tensor"),
        P(("context", "dp"), "tensor"),
        P(("context", "dp"), "tensor"),
        P("tensor", ("context", "dp")),
        P(("context", "dp")),
        P(("context", "dp"), "tensor"),
        P(("context", "dp"), "tensor"),
        P("tensor", ("context", "dp")),
    )
    run = functools.partial(local, dict(mesh.shape))
    return jax.shard_map(run, mesh=mesh, in_specs=in_specs, out_specs=out_specs, check_vma=False)
```

```python
import functools

import jax
import jax.numpy as jnp
from jax import lax
from jax.experimental import pallas as pl
from jax.experimental.pallas import tpu as pltpu
from jax.sharding import PartitionSpec as P

EPSILON = 1e-05
BF16 = jnp.bfloat16
F32 = jnp.float32
FAR = 1e30
AUX = 8
ONES_AT = 5
BLOCK = 256


def cost(us=0):
    return pl.CostEstimate(flops=int(us * 1.15e9) + 1024, bytes_accessed=1024, transcendentals=0)


COST = cost()


def params():
    return pltpu.CompilerParams(vmem_limit_bytes=56 * 2**20)


def dot(left, right, dims):
    return lax.dot_general(left, right, (dims, ((), ())), preferred_element_type=F32)


NN, NT, TN, TT = ((1,), (0,)), ((1,), (1,)), ((0,), (0,)), ((0,), (1,))


def turn(rows, cos_rows, sine_rows, sign):
    half = rows.shape[0] // 2
    first, second = rows[:half], rows[half:]
    return jnp.concatenate(
        [first * cos_rows - sign * second * sine_rows, second * cos_rows + sign * first * sine_rows], 0
    )


def project_kernel(at_ref, x_ref, gain_ref, wq_ref, wkv_ref, cos_ref, sin_ref, h_ref, q_ref, kv_ref):
    x = x_ref[...].astype(F32)
    scale = lax.rsqrt(jnp.mean(x * x, -1, keepdims=True) + EPSILON)
    h = (x * scale * gain_ref[...]).astype(BF16)
    part = h.shape[0] // 2
    swapped = at_ref[2] * part
    h_ref[pl.ds(pl.multiple_of(swapped, part), part)] = h[:part]
    h_ref[pl.ds(pl.multiple_of(part - swapped, part), part)] = h[part:]
    cos_rows, sine_rows = cos_ref[...], sin_ref[...]
    head = kv_ref.shape[0] // 2
    score_scale = head ** (-0.5)
    q = dot(h, wq_ref[...], NN).T
    for at in range(0, q.shape[0], head):
        q_ref[at : at + head] = (turn(q[at : at + head], cos_rows, sine_rows, 1.0) * score_scale).astype(BF16)
    kv = dot(wkv_ref[...], h, NT)
    kv_ref[:head] = turn(kv[:head], cos_rows, sine_rows, 1.0).astype(BF16)
    kv_ref[head:] = kv[head:].astype(BF16)


def project(at, x, gain, w_query, w_kv, cos_rows, sine_rows, stretch):
    rows, width = x.shape
    step = stretch // 2
    wide, both = w_query.shape[1], w_kv.shape[0]
    half = cos_rows.shape[0]
    whole = lambda shape: pl.BlockSpec(shape, lambda i, at: (0, 0))
    return pl.pallas_call(
        project_kernel,
        grid_spec=pltpu.PrefetchScalarGridSpec(
            num_scalar_prefetch=1,
            grid=(rows // step,),
            in_specs=[
                pl.BlockSpec((step, width), lambda i, at: (i, 0)),
                whole((1, width)),
                whole((width, wide)),
                whole((both, width)),
                pl.BlockSpec((half, step), lambda i, at: (0, i)),
                pl.BlockSpec((half, step), lambda i, at: (0, i)),
            ],
            out_specs=[
                pl.BlockSpec((step, width), lambda i, at: (i + at[1] - 2 * at[1] * lax.rem(i, 2), 0)),
                pl.BlockSpec((wide, step), lambda i, at: (0, i)),
                pl.BlockSpec((both, step), lambda i, at: (0, i)),
            ],
        ),
        out_shape=[
            jax.ShapeDtypeStruct((rows, width), BF16),
            jax.ShapeDtypeStruct((wide, rows), BF16),
            jax.ShapeDtypeStruct((both, rows), BF16),
        ],
        compiler_params=params(),
        cost_estimate=COST,
    )(at, x, gain, w_query, w_kv, cos_rows, sine_rows)


def pieces(value):
    high = value.astype(BF16).astype(F32)
    middle = (value - high).astype(BF16).astype(F32)
    low = value - high - middle
    return high, middle, low


def key_rows(kv, seg):
    head, count = kv.shape[0] // 2, kv.shape[1]
    row = lax.broadcasted_iota(jnp.int32, (2 * AUX, count), 0)
    extra = jnp.where(row < ONES_AT, jnp.where(seg == row, 0.0, -FAR), jnp.where(row < AUX, 1.0, 0.0))
    rest = jnp.zeros((head - 2 * AUX, count), F32)
    return jnp.concatenate([kv[:head].astype(F32), extra, rest], 0)


def value_rows(kv, fill):
    head, count = kv.shape[0] // 2, kv.shape[1]
    row = lax.broadcasted_iota(jnp.int32, (fill, count), 0)
    return jnp.concatenate([kv[head:].astype(F32), jnp.where(row < 3, 1.0, 0.0)], 0)


def places(at_ref, count):
    quarter = count // 4
    mine = 2 * at_ref[1] + at_ref[2]
    return [pl.ds(pl.multiple_of((b ^ mine) * quarter, quarter), quarter) for b in range(4)]


def causal(scores):
    key_at = lax.broadcasted_iota(jnp.int32, scores.shape, 0)
    query_at = lax.broadcasted_iota(jnp.int32, scores.shape, 1)
    return jnp.where(key_at <= query_at, scores, -FAR)


def attend_kernel(far_count, at_ref, q_ref, seg_ref, *refs):
    kv_refs = refs[: far_count + 1]
    qa_ref, o_ref, full_ref = refs[far_count + 1 : far_count + 4]
    ka_ref, va_ref = refs[far_count + 4 :]
    me = at_ref[0]
    head = kv_refs[0].shape[0] // 2
    count = q_ref.shape[1]

    @pl.when(pl.program_id(0) == 0)
    def _():
        for d, kv_ref in enumerate(kv_refs):
            kv = kv_ref[...]
            ka_ref[d] = key_rows(kv, seg_ref[d : d + 1]).T.astype(BF16)
            va_ref[d] = value_rows(kv, 2 * AUX).astype(BF16)

    row = lax.broadcasted_iota(jnp.int32, (2 * AUX, count), 0)
    same = jnp.where((seg_ref[0:1] == row) & (row < ONES_AT), 1.0, 0.0)
    rest = jnp.zeros((head - 2 * AUX, count), F32)

    def heads(blocks):
        for h in range(q_ref.shape[0] // head):
            q = q_ref[h * head : (h + 1) * head].astype(F32)
            qa = jnp.concatenate([q, same, rest], 0).astype(BF16)
            scores = [dot(ka_ref[d], qa, NN) for d in range(blocks)]
            scores[0] = causal(scores[0])
            m = jnp.max(scores[0], 0, keepdims=True)
            for d in range(1, blocks):
                m = jnp.maximum(m, jnp.max(scores[d], 0, keepdims=True))
            acc = None
            for d in range(blocks):
                term = dot(va_ref[d], jnp.exp(scores[d] - m).astype(BF16), NN)
                acc = term if acc is None else acc + term
            total = acc[head : head + 1]
            out = acc[:head] / total
            for b, place in enumerate(places(at_ref, count)):
                quarter = out[:, b * (count // 4) : (b + 1) * (count // 4)]
                full_ref[h * head : (h + 1) * head, place] = quarter
                o_ref[h * head : (h + 1) * head, place] = quarter.astype(BF16)
            high, middle, low = pieces(-(m + jnp.log(total)))
            extra = jnp.where(
                row == ONES_AT, high, jnp.where(row == ONES_AT + 1, middle, jnp.where(row == ONES_AT + 2, low, same))
            )
            qa_ref[h] = jnp.concatenate([q, extra, rest], 0).astype(BF16)

    for blocks in range(1, far_count + 2):
        pl.when(me == blocks - 1)(functools.partial(heads, blocks))


def attend(me, q, kvs, segs, item, group=2):
    far_count = len(kvs) - 1
    both = kvs[0].shape[0]
    head = both // 2
    wide, count = q.shape[0], segs.shape[-1]
    heads = wide // head
    return pl.pallas_call(
        functools.partial(attend_kernel, far_count),
        grid_spec=pltpu.PrefetchScalarGridSpec(
            num_scalar_prefetch=1,
            grid=(heads // group,),
            in_specs=[
                pl.BlockSpec((group * head, count), lambda h, at: (h, item)),
                pl.BlockSpec((None, far_count + 1, count), lambda h, at: (item, 0, 0)),
            ]
            + [pl.BlockSpec((both, count), lambda h, at: (0, item))] * (far_count + 1),
            out_specs=[
                pl.BlockSpec((group, both, count), lambda h, at: (h, 0, 0)),
                pl.BlockSpec((group * head, count), lambda h, at: (h, 0)),
                pl.BlockSpec((group * head, count), lambda h, at: (h, 0)),
            ],
            scratch_shapes=[
                pltpu.VMEM((far_count + 1, count, both), BF16),
                pltpu.VMEM((far_count + 1, head + 2 * AUX, count), BF16),
            ],
        ),
        out_shape=[
            jax.ShapeDtypeStruct((heads, both, count), BF16),
            jax.ShapeDtypeStruct((wide, count), BF16),
            jax.ShapeDtypeStruct((wide, count), F32),
        ],
        compiler_params=params(),
        cost_estimate=COST,
    )(me, q, segs, *kvs)


def back_kernel(far_count, at_ref, qa_ref, do_ref, full_ref, seg_ref, cos_ref, sin_ref, *refs):
    kv_refs = refs[: far_count + 1]
    dq_ref, keep_ref, send_ref = refs[far_count + 1 : far_count + 4]
    ka_ref, kt_ref, va_ref, dk_ref, dv_ref, dq_acc = refs[far_count + 4 :]
    me = at_ref[0]
    head, count = do_ref.shape
    step = pl.program_id(0)

    @pl.when(step == 0)
    def _():
        for d, kv_ref in enumerate(kv_refs):
            kv = kv_ref[...]
            ka_ref[d] = key_rows(kv, seg_ref[d : d + 1]).T.astype(BF16)
            kt_ref[d] = kv[:head]
            va_ref[d] = value_rows(kv, head).T.astype(BF16)
        dk_ref[...] = jnp.zeros_like(dk_ref)
        dv_ref[...] = jnp.zeros_like(dv_ref)

    qa = qa_ref[...]
    here = places(at_ref, count)
    do = jnp.concatenate([do_ref[:, place] for place in here], 1).astype(F32)
    full = jnp.concatenate([full_ref[:, place] for place in here], 1)
    high, middle, low = pieces(-jnp.sum(do * full, 0, keepdims=True))
    row = lax.broadcasted_iota(jnp.int32, (2 * AUX, count), 0)
    extra = jnp.where(row == 0, high, jnp.where(row == 1, middle, jnp.where(row == 2, low, 0.0)))
    rest = jnp.zeros((head - 2 * AUX, count), F32)
    da = jnp.concatenate([do, extra, rest], 0).astype(BF16)
    def run(blocks):
        total = None
        for d in range(blocks):
            scores = dot(ka_ref[d], qa, NN)
            probs = jnp.exp(causal(scores) if d == 0 else scores)
            d_scores = (probs * dot(va_ref[d], da, NN)).astype(BF16)
            dv_ref[d] += dot(probs.astype(BF16), da[:head], NT)
            dk_ref[d] += dot(d_scores, qa[:head], NT)
            update = dot(kt_ref[d], d_scores, NN)
            total = update if total is None else total + update
        dq_acc[...] = total

    for blocks in range(1, far_count + 2):
        pl.when(me == blocks - 1)(functools.partial(run, blocks))
    score_scale = head ** (-0.5)
    dq = turn(dq_acc[...] * score_scale, cos_ref[...], sin_ref[...], -1.0).astype(BF16)
    for b, place in enumerate(here):
        dq_ref[:, place] = dq[:, b * (count // 4) : (b + 1) * (count // 4)]

    @pl.when(step == pl.num_programs(0) - 1)
    def _():
        keep_ref[...] = jnp.zeros_like(keep_ref)
        send_ref[...] = jnp.zeros_like(send_ref)
        keep_ref[0] = jnp.concatenate([dk_ref[0], dv_ref[0]], 1).T.astype(BF16)
        for d in range(1, far_count + 1):

            @pl.when(d <= me)
            def _(d=d):
                part = jnp.concatenate([dk_ref[d], dv_ref[d]], 1).T.astype(BF16)
                place = (me - d) ^ me

                @pl.when(place % 2 == 0)
                def _():
                    keep_ref[place // 2] = part

                @pl.when(place % 2 == 1)
                def _():
                    send_ref[place // 2] = part


def attend_back(me, qa, do, full, kvs, segs, cos_rows, sine_rows, item, us):
    far_count = len(kvs) - 1
    heads, both, count = qa.shape
    head = both // 2
    wide, half = heads * head, cos_rows.shape[0]
    return pl.pallas_call(
        functools.partial(back_kernel, far_count),
        grid_spec=pltpu.PrefetchScalarGridSpec(
            num_scalar_prefetch=1,
            grid=(heads,),
            in_specs=[
                pl.BlockSpec((None, both, count), lambda h, at: (h, 0, 0)),
                pl.BlockSpec((head, count), lambda h, at: (h, 0)),
                pl.BlockSpec((head, count), lambda h, at: (h, 0)),
                pl.BlockSpec((None, far_count + 1, count), lambda h, at: (item, 0, 0)),
                pl.BlockSpec((half, count), lambda h, at: (0, item)),
                pl.BlockSpec((half, count), lambda h, at: (0, item)),
            ]
            + [pl.BlockSpec((both, count), lambda h, at: (0, item))] * (far_count + 1),
            out_specs=[pl.BlockSpec((head, count), lambda h, at: (h, 0))]
            + [pl.BlockSpec(((far_count + 1) // 2, both, count), lambda h, at: (0, 0, 0))] * 2,
            scratch_shapes=[
                pltpu.VMEM((far_count + 1, count, both), BF16),
                pltpu.VMEM((far_count + 1, head, count), BF16),
                pltpu.VMEM((far_count + 1, count, both), BF16),
                pltpu.VMEM((far_count + 1, count, head), F32),
                pltpu.VMEM((far_count + 1, count, head), F32),
                pltpu.VMEM((head, count), F32),
            ],
        ),
        out_shape=[jax.ShapeDtypeStruct((wide, count), BF16)]
        + [jax.ShapeDtypeStruct(((far_count + 1) // 2, both, count), BF16)] * 2,
        compiler_params=params(),
        cost_estimate=cost(us),
    )(me, qa, do, full, segs, cos_rows, sine_rows, *kvs)


def merge_kernel(at_ref, own_ref, recv_ref, cos_ref, sin_ref, out_ref):
    head, count = out_ref.shape[0] // 2, out_ref.shape[1]
    total = own_ref[...].astype(F32) + recv_ref[...].astype(F32)
    turned = turn(total[:head], cos_ref[...], sin_ref[...], -1.0)
    out = jnp.concatenate([turned, total[head:]], 0).astype(BF16)
    for b, place in enumerate(places(at_ref, count)):
        out_ref[:, place] = out[:, b * (count // 4) : (b + 1) * (count // 4)]


def merge(at, own, received, cos_rows, sine_rows):
    seqs, both, count = own.shape
    half = cos_rows.shape[0]
    block = pl.BlockSpec((None, both, count), lambda s, at: (s, 0, 0))
    table = pl.BlockSpec((half, count), lambda s, at: (0, s))
    return pl.pallas_call(
        merge_kernel,
        grid_spec=pltpu.PrefetchScalarGridSpec(
            num_scalar_prefetch=1,
            grid=(seqs,),
            in_specs=[block, block, table, table],
            out_specs=block,
        ),
        out_shape=jax.ShapeDtypeStruct(own.shape, BF16),
        compiler_params=params(),
        cost_estimate=COST,
    )(at, own, received, cos_rows, sine_rows)


def product(order, pieces, *items):
    total = order.mark(sum(dot(a, b, form) for a, b, form in items).astype(BF16))
    half = total.shape[0] // 2
    return cut(total[half:], pieces), total[:half]


def cut(x, pieces):
    size = x.shape[0] // pieces
    return [x[j * size : (j + 1) * size] for j in range(pieces)]


def unfold_kernel(*refs):
    *part_refs, w_ref, out_ref, full_ref = refs
    size = part_refs[0].shape[0]
    for j, ref in enumerate(part_refs):
        full_ref[j * size : (j + 1) * size] = ref[...]
    out_ref[...] = dot(w_ref[...], full_ref[...], NT).astype(BF16)


def unfold(parts, w):
    rows, width = len(parts) * parts[0].shape[0], parts[0].shape[1]
    return pl.pallas_call(
        unfold_kernel,
        out_shape=[
            jax.ShapeDtypeStruct((w.shape[0], rows), BF16),
            jax.ShapeDtypeStruct((rows, width), BF16),
        ],
        compiler_params=params(),
        cost_estimate=COST,
    )(*parts, w)


def grad_kernel(groups, has_recv, split, table_ref, *refs):
    out = []
    for form, pairs in groups:
        total = None
        for narrow, wide in pairs:
            both = jnp.concatenate([refs[wide][...], refs[wide + 1][...]], 1)
            if form == TN:
                term = dot(both, refs[narrow][...], TN)
            else:
                term = dot(refs[narrow][...], both, NN)
            total = term if total is None else total + term
        out.append(total)
    at = len(refs) - (2 if split else 1) - (1 if has_recv else 0)
    recv = None
    if has_recv:
        recv, at = refs[at], at + 1

    def put(ref):
        if groups[0][0] == TN:
            rows = out[0].shape[0] // 2
            for j in range(2):
                block = out[0][j * rows : (j + 1) * rows]
                ref[j] = (block if recv is None else block + recv[j].astype(F32)).astype(BF16)
            return
        row = 0
        for total in out:
            count, wide = total.shape[0], total.shape[1] // 2
            for j in range(2):
                block = total[:, j * wide : (j + 1) * wide]
                if recv is not None:
                    block = block + recv[j, row : row + count].astype(F32)
                ref[j, row : row + count] = block.astype(BF16)
            row += count

    if not split:
        put(refs[at])
        return
    first = pl.program_id(0) < split // 2
    pl.when(first)(lambda: put(refs[at]))
    pl.when(jnp.logical_not(first))(lambda: put(refs[at + 1]))


def grad_blocks(table, form, sets, recv=None, split=0, us=0):
    n = table.shape[0]
    ins, specs, groups = [], [], []
    for wide_set, narrow_set in sets:
        pairs = []
        for s, (wide, narrow) in enumerate(zip(wide_set, narrow_set)):
            pairs.append((len(ins), len(ins) + 1))
            ins += [narrow, wide, wide]
            specs.append(pl.BlockSpec(narrow.shape, lambda i, t: (0, 0)))
            tokens = narrow.shape[0 if form == TN else 1]
            item = s if wide.shape[0] > tokens else 0
            for j in range(2):
                specs.append(pl.BlockSpec((tokens, BLOCK), lambda i, t, j=j, item=item: (item, t[2 * i + j])))
        groups.append((form, pairs))
    if form == TN:
        block = (BLOCK, sets[0][1][0].shape[1])
    else:
        block = (sum(narrow_set[0].shape[0] for _, narrow_set in sets), BLOCK)
    two = (2,) + block
    if recv is not None:
        ins.append(recv)
        specs.append(pl.BlockSpec(two, lambda i, t: (lax.rem(i + split // 2, n // 2), 0, 0)))
    if split:
        out_specs = [
            pl.BlockSpec(two, lambda i, t: (jnp.minimum(i, split // 2 - 1), 0, 0)),
            pl.BlockSpec(two, lambda i, t: (jnp.maximum(i - split // 2, 0), 0, 0)),
        ]
        out_shape = [jax.ShapeDtypeStruct((split,) + block, BF16), jax.ShapeDtypeStruct((n - split,) + block, BF16)]
    else:
        out_specs = pl.BlockSpec(two, lambda i, t: (i, 0, 0))
        out_shape = jax.ShapeDtypeStruct((n,) + block, BF16)
    return pl.pallas_call(
        functools.partial(grad_kernel, groups, recv is not None, split),
        grid_spec=pltpu.PrefetchScalarGridSpec(num_scalar_prefetch=1, grid=(n // 2,), in_specs=specs, out_specs=out_specs),
        out_shape=out_shape,
        compiler_params=params(),
        cost_estimate=cost(us),
    )(table, *ins)


def add_send_kernel(keep_ref, recv_ref, send_ref, rest_ref):
    send_ref[...] = (keep_ref[1].astype(F32) + recv_ref[1].astype(F32)).astype(BF16)
    rest_ref[...] = keep_ref[0].astype(F32) + recv_ref[0].astype(F32)


def add_send(keep, recv, us):
    shape = keep.shape[1:]
    return pl.pallas_call(
        add_send_kernel,
        out_shape=[jax.ShapeDtypeStruct(shape, BF16), jax.ShapeDtypeStruct(shape, F32)],
        compiler_params=params(),
        cost_estimate=cost(us),
    )(keep, recv)


def add_pair_kernel(a_ref, b_ref, out_ref):
    out_ref[...] = a_ref[...] + b_ref[...]


def add_pair(a, b, us):
    return pl.pallas_call(
        add_pair_kernel,
        out_shape=jax.ShapeDtypeStruct(a.shape, a.dtype),
        compiler_params=params(),
        cost_estimate=cost(us),
    )(a, b)


def add_last_kernel(turned, rest_ref, got_ref, *out_refs):
    row = 0
    for (count, flip), out_ref in zip(turned, out_refs):
        total = rest_ref[row : row + count] + got_ref[row : row + count].astype(F32)
        out_ref[...] = total.T if flip else total
        row += count


def add_last(rest, got, turned, us):
    wide = rest.shape[1]
    return pl.pallas_call(
        functools.partial(add_last_kernel, turned),
        out_shape=[
            jax.ShapeDtypeStruct((wide, count) if flip else (count, wide), F32) for count, flip in turned
        ],
        compiler_params=params(),
        cost_estimate=cost(us),
    )(rest, got)


class Order:
    def __init__(self):
        self.last = None

    def take_all(self, xs):
        if self.last is not None:
            xs = lax.optimization_barrier((self.last, *xs))[1:]
        return xs

    def take(self, *xs):
        xs = self.take_all(xs)
        return xs if len(xs) > 1 else xs[0]

    def mark(self, x):
        self.last = x
        return x


def sealed(fn, *args):
    def never(*args):
        return jax.tree.map(lambda leaf: jnp.zeros(leaf.shape, leaf.dtype), jax.eval_shape(fn, *args))

    return lax.cond(lax.axis_index("tensor") >= 0, fn, never, *args)


class Scatter:
    def __init__(self, stages, sizes, form, fast):
        self.stages, self.sizes, self.form, self.fast = stages, sizes, form, fast
        ctx, dp = lax.axis_index("context"), lax.axis_index("dp")
        blocks = []
        for p in range(2 ** len(stages)):
            c, d = ctx, dp
            for j, (axis, bit) in enumerate(stages):
                if p >> (len(stages) - 1 - j) & 1:
                    if axis == "context":
                        c = c ^ (1 << bit)
                    else:
                        d = d ^ (1 << bit)
            blocks.append(c * sizes["dp"] + d)
        self.away = jnp.stack(blocks[4:]).astype(jnp.int32)
        self.near = jnp.stack([blocks[p] for p in (2, 3, 0, 1)]).astype(jnp.int32)

    def send(self, j, x):
        axis, bit = self.stages[j]
        self.got = swap(x, axis, self.sizes[axis], bit)

    def first(self, order, sets, us=0):
        if self.fast:
            wide = order.take(*sets[0][0])
            self.sets = [(list(wide), sets[0][1])] + sets[1:]
            self.send(0, order.mark(grad_blocks(self.away, self.form, self.sets, us=us)))

    def second(self, order, us=0):
        if self.fast:
            send, self.keep = grad_blocks(self.near, self.form, self.sets, order.take(self.got), 2, us)
            self.send(1, order.mark(send))

    def third(self, order, us=0):
        if self.fast:
            send, self.rest = add_send(self.keep, order.take(self.got), us)
            self.send(2, order.mark(send))

    def final(self, order, turned, us=0):
        if self.fast:
            out = add_last(self.rest, order.take(self.got), turned, us)
            order.mark(out[0])
            return out if len(out) > 1 else out[0]


def place_kernel(at_ref, *refs):
    *part_refs, out_ref = refs
    quarter = part_refs[0].shape[0]
    mine = 2 * at_ref[1] + at_ref[2]
    for p, ref in enumerate(part_refs):
        where = pl.ds(pl.multiple_of((p ^ mine) * quarter, quarter), quarter)
        out_ref[where] = ref[...].astype(out_ref.dtype)


def place(at, parts, dtype, us):
    seqs, quarter, width = parts[0].shape
    spec = lambda rows: pl.BlockSpec((None, rows, width), lambda s, at: (s, 0, 0))
    return pl.pallas_call(
        place_kernel,
        grid_spec=pltpu.PrefetchScalarGridSpec(
            num_scalar_prefetch=1, grid=(seqs,), in_specs=[spec(quarter)] * 4, out_specs=spec(4 * quarter)
        ),
        out_shape=jax.ShapeDtypeStruct((seqs, 4 * quarter, width), dtype),
        compiler_params=params(),
        cost_estimate=cost(us),
    )(at, *parts)


def swap(x, axis, size, bit):
    return lax.ppermute(x, axis, [(i, i ^ (1 << bit)) for i in range(size)])


def rows_at(x, at, count):
    return lax.dynamic_slice_in_dim(x, at, count, 0)


def local(sizes, tokens, segment_ids, norm_gain_1, w_query, w_key, w_value, w_output, norm_gain_2, w_gate, w_up, w_down, cotangent):
    seqs, stretch, width = tokens.shape
    rows = seqs * stretch
    head = w_key.shape[1]
    wide = w_query.shape[1]
    n_tensor, n_context, n_dp = sizes["tensor"], sizes["context"], sizes["dp"]
    me_t, me_c = lax.axis_index("tensor"), lax.axis_index("context")
    core, high = me_t % 2, me_t // 2
    mine = 2 * core + high
    half, quarter = stretch // 2, stretch // 4
    offset = me_c * stretch
    order = Order()
    each = range(seqs)

    seg_here = lax.dynamic_slice_in_dim(segment_ids, offset, stretch, 1)
    start = jnp.zeros(seg_here.shape, jnp.int32)
    for number in range(1, ONES_AT):
        before = jnp.sum((segment_ids < number).astype(jnp.int32), 1, keepdims=True)
        start = jnp.where(seg_here == number, before, start)
    positions = (offset + jnp.arange(stretch, dtype=jnp.int32))[None, :] - start
    frequency = 10000.0 ** (-(2.0 * jnp.arange(head // 2, dtype=F32)) / head)
    angles = frequency[:, None] * positions.reshape(1, rows).astype(F32)
    cos_rows, sine_rows = jnp.cos(angles), jnp.sin(angles)
    padded = jnp.concatenate([jnp.zeros((seqs, (n_context - 1) * stretch), jnp.int32), segment_ids], 1)
    segs = jnp.stack(
        [
            lax.dynamic_slice_in_dim(padded, offset + (n_context - 1 - d) * stretch, stretch, 1)
            for d in range(n_context)
        ],
        1,
    )
    at = jnp.stack([me_c, core, high]).astype(jnp.int32)

    x_rows = tokens.reshape(rows, width)
    ct_rows = cotangent.reshape(rows, width)
    gain_1, gain_2 = norm_gain_1.reshape(1, width), norm_gain_2.reshape(1, width)
    w_kv = jnp.concatenate([w_key.T, w_value.T], 0)
    h1, q_t, kv_t = project(at, x_rows, gain_1, w_query, w_kv, cos_rows, sine_rows, stretch)
    order.mark(kv_t)
    kvs = [kv_t] + [
        lax.ppermute(kv_t, "context", [(i, i + d) for i in range(n_context - d)]) for d in range(1, n_context)
    ]

    def own_order(x, s):
        return jnp.concatenate([rows_at(x, s * stretch + (p ^ mine) * quarter, quarter) for p in range(4)], 0)

    def fold(pair):
        sends, keep = pair
        return [swap(x, "tensor", n_tensor, 0) for x in sends], keep

    def join(pieces):
        return jnp.concatenate(order.take_all(pieces), 0)

    def fold_more(kept, got):
        total = kept.astype(F32) + got.astype(F32)
        send = total[quarter:].astype(BF16)
        return swap(order.mark(send), "tensor", n_tensor, 1), total[:quarter]

    def core_swap(x):
        return swap(x, "tensor", n_tensor, 0)

    def core_swaps(first, second):
        first = core_swap(first)
        first, second = lax.optimization_barrier((first, second))
        return first, core_swap(second)

    def fold_now(total):
        near = total[:, :half].astype(F32) + core_swap(total[:, half:]).astype(F32)
        return near[:, quarter:].astype(BF16), near[:, :quarter]

    def spread(part):
        return swap(part, "tensor", n_tensor, 1)

    cts, d_hidden = [], []
    for s in each:
        cts.append(own_order(order.take(ct_rows), s))
        d_hidden.append(order.mark(dot(cts[s], w_down, NT)))

    stream = [rows_at(x_rows, s * stretch + mine * quarter, quarter).astype(F32) for s in each]
    ct_own = [rows_at(ct_rows, s * stretch + mine * quarter, quarter).astype(F32) for s in each]

    qa, o_t, full_o = [None] * seqs, [None] * seqs, [None] * seqs
    got_o, kept_o = [None] * seqs, [None] * seqs
    residual, scale_2, normed_2, h2_own, got_h = ([None] * seqs for _ in range(5))

    def after_attention(s):
        total = kept_o[s] + order.take(got_o[s]).astype(F32)
        residual[s] = stream[s] + total
        scale_2[s] = lax.rsqrt(jnp.mean(residual[s] * residual[s], -1, keepdims=True) + EPSILON)
        normed_2[s] = residual[s] * scale_2[s]
        h2_own[s] = order.mark((normed_2[s] * gain_2).astype(BF16))
        got_h[s] = spread(h2_own[s])

    for s in each:
        qa[s], o_t[s], full_o[s] = attend(at, order.take(q_t), kvs, segs, s)
        order.mark(o_t[s])
        if s:
            after_attention(s - 1)
        got, kept = fold(product(order, 1, (order.take(o_t[s]), w_output, TN)))
        got_o[s], kept_o[s] = fold_more(kept, join(got))

    hidden, d_gate, d_up, h2 = ([None] * seqs for _ in range(4))
    got_b, kept_b = [None] * seqs, [None] * seqs

    def back_sealed(s):
        def run(left, right):
            return fold_now((dot(left, w_gate, NT) + dot(right, w_up, NT)).astype(BF16)[None])

        send, kept = sealed(run, *order.take(d_gate[s], d_up[s]))
        got_b[s], kept_b[s] = swap(order.mark(send)[0], "tensor", n_tensor, 1), kept[0]

    d_res, d_low_own, got_d, gains_2 = ([None] * seqs for _ in range(4))

    def norm_back(scaled_grad, normed, scale, gain):
        scaled = scaled_grad * gain
        return scale * (scaled - normed * jnp.mean(scaled * normed, -1, keepdims=True))

    def after_back(s):
        def run(kept, got, normed, scale, own):
            back = kept + got.astype(F32)
            grad = own + norm_back(back, normed, scale, gain_2)
            return grad.astype(BF16), grad, jnp.sum(back * normed, 0)

        d_low_own[s], d_res[s], gains_2[s] = sealed(
            run, kept_b[s], order.take(got_b[s]), normed_2[s], scale_2[s], ct_own[s]
        )
        got_d[s] = spread(order.mark(d_low_own[s]))

    blocks = n_context * n_dp
    fast = width // blocks == BLOCK and n_dp == 2 and n_context == 4
    x_first = [("dp", 0), ("context", 0), ("context", 1)]
    z_first = [("context", 0), ("dp", 0), ("context", 1)]
    down_job = Scatter(x_first, sizes, TN, fast)
    gate_job = Scatter(x_first, sizes, TN, fast)
    up_job = Scatter(z_first, sizes, TN, fast)
    mix_job = Scatter(x_first, sizes, NN, fast)
    kv_job = Scatter(x_first, sizes, NN, fast)

    def feed_forward(part, got, d_rows):
        rows = jnp.concatenate([part, got, *core_swaps(part, got)], 0)
        gate, up = dot(rows, w_gate, NN), dot(rows, w_up, NN)
        sig = jax.nn.sigmoid(gate)
        return (
            rows,
            (gate * sig * up).astype(BF16),
            (d_rows * up * sig * (1.0 + gate * (1.0 - sig))).astype(BF16),
            (d_rows * gate * sig).astype(BF16),
        )

    for s in each:
        h2[s], hidden[s], d_gate[s], d_up[s] = sealed(feed_forward, h2_own[s], order.take(got_h[s]), d_hidden[s])
        order.mark(d_up[s])
        if s + 1 < seqs:
            after_attention(s + 1)
            back_sealed(s)

    d_low, dq_t, dkvs = [None] * seqs, [None] * seqs, [None] * seqs

    do_t = [None] * seqs

    def unfolded(s):
        def run(part, got):
            return unfold([part, got, *core_swaps(part, got)], w_output)

        do_t[s], d_low[s] = sealed(run, d_low_own[s], order.take(got_d[s]))
        order.mark(do_t[s])

    def attention_back(s, us):
        dq_t[s], *dkvs[s] = attend_back(
            at, qa[s], order.take(do_t[s]), full_o[s], kvs, segs, cos_rows, sine_rows, s, us
        )
        order.mark(dq_t[s])

    def swap_quarters(part, got):
        got = order.take(got)
        far = sealed(core_swaps, part, got)
        order.mark(far[1])
        return [part, got, *far]

    def put_quarters(quarters, dtype, us=0):
        return order.mark(place(at, [order.take(quarters[0]), *quarters[1:]], dtype, us))

    last = seqs - 1
    down_job.first(order, [(cts, hidden)], 0)
    for s in range(last):
        after_back(s)
    back_sealed(last)
    unfolded(0)
    up_job.first(order, [(h2, d_up)], 20)
    after_back(last)
    gate_job.first(order, [(h2, d_gate)], 0)

    def down_partial(*parts):
        total = dot(jnp.concatenate(parts, 0), w_down, NN).astype(BF16)
        return fold_now(total.reshape(seqs, stretch, width))

    send, kept_out = sealed(down_partial, *order.take_all(hidden))
    got_out = swap(order.mark(send), "tensor", n_tensor, 1)
    down_job.second(order, 8)
    attention_back(0, 20)
    unfolded(last)
    up_job.second(order, 12)

    def out_rows(got, kept, *rows):
        return (jnp.stack(rows) + kept + got.astype(F32)).astype(BF16)

    out_own = order.mark(sealed(out_rows, order.take(got_out), kept_out, *residual))
    got_out = spread(out_own)
    attention_back(last, 0)

    keep_send = [x for s in each for x in dkvs[s]]
    kept_kv, send = sealed(lambda *xs: (jnp.stack(xs[0::2]), jnp.stack(xs[1::2])), *keep_send)
    got_kv = swap(order.mark(send), "context", n_context, 0)
    quarters = swap_quarters(out_own, got_out)
    mix_job.first(order, [(d_low, o_t), ([h1] * seqs, dq_t)], 0)

    def add_kv(kept, got):
        total = kept.astype(F32) + got.astype(F32)
        return total[:, 0].astype(BF16), total[:, 1].astype(BF16)

    kept_kv, send = sealed(add_kv, kept_kv, order.take(got_kv))
    got_kv = swap(order.mark(send), "context", n_context, 1)
    gate_job.second(order)
    down_job.third(order)
    layer_out = put_quarters(quarters, BF16)

    def input_partial(kept, got, *parts):
        both = merge(at, kept, got, cos_rows, sine_rows)
        rows_q, rows_kv = jnp.concatenate(parts, 1), jnp.concatenate([both[s] for s in each], 1)
        total = dot(rows_q, w_query, TT) + dot(rows_kv, w_kv, TN)
        return *fold_now(total.astype(BF16).reshape(seqs, stretch, width)), *[both[s] for s in each]

    send, kept_x, *dkv_ts = sealed(input_partial, kept_kv, order.take(got_kv), *dq_t)
    got_x = swap(order.mark(send), "tensor", n_tensor, 1)
    up_job.third(order, 0)
    down_sum = down_job.final(order, [(BLOCK, True)], 16)
    mix_job.second(order, 0)
    gate_job.third(order, 0)
    kv_job.first(order, [([h1] * seqs, dkv_ts)], 0)

    def input_grad(kept, got, sums_0, sums_1, *parts):
        back = kept + got.astype(F32)
        streams, res = jnp.stack(parts[:seqs]), jnp.stack(parts[seqs:])
        scale = lax.rsqrt(jnp.mean(streams * streams, -1, keepdims=True) + EPSILON)
        normed = streams * scale
        grad = res + norm_back(back, normed, scale, gain_1)
        sums = jnp.stack([jnp.sum(back * normed, (0, 1)), sums_0 + sums_1])
        return grad.astype(BF16), sums, core_swap(sums)

    grad_own, gain_sum, got_gain = sealed(input_grad, kept_x, order.take(got_x), *gains_2, *stream, *d_res)
    got_grad = spread(order.mark(grad_own))
    hops = [(axis, bit) for axis in ("tensor", "context", "dp") for bit in range((sizes[axis] - 1).bit_length())]
    hops.pop(0)

    def hop(us=0):
        nonlocal gain_sum, got_gain
        gain_sum = order.mark(add_pair(gain_sum, order.take(got_gain), us))
        if hops:
            axis, bit = hops.pop(0)
            got_gain = swap(gain_sum, axis, sizes[axis], bit)
            return True
        return False

    up_sum = up_job.final(order, [(BLOCK, False)], 2)
    kv_job.second(order, 2)
    hop(0)
    hop(0)
    mix_job.third(order, 0)
    kv_job.third(order, 0)
    gate_sum = gate_job.final(order, [(BLOCK, False)], 0)
    hop(4)
    grad_tokens = put_quarters(swap_quarters(grad_own, got_grad), F32)
    hop(0)
    while hop():
        pass
    per = width // blocks
    gain_sum = lax.dynamic_slice_in_dim(gain_sum, (me_c * n_dp + lax.axis_index("dp")) * per, per, 1)

    if fast:
        key_sum, value_sum = (x.T for x in kv_job.final(order, [(head, False), (head, False)], 1))
        output_sum, query_sum = mix_job.final(order, [(wide, False), (wide, True)])
    else:

        def plain(left, right, dim):
            total = sum(dot(a, b, TN) for a, b in zip(left, right))
            return lax.psum_scatter(
                total.astype(BF16), ("context", "dp"), scatter_dimension=dim, tiled=True
            ).astype(F32)

        down_sum = plain(hidden, cts, 1)
        gate_sum = plain(h2, d_gate, 0)
        up_sum = plain(h2, d_up, 0)
        output_sum = plain([a.T for a in o_t], d_low, 1)
        h1s = [h1[s * stretch : (s + 1) * stretch] for s in each]
        query_sum = plain(h1s, [a.T for a in dq_t], 0)
        kv_sum = plain(h1s, [a.T for a in dkv_ts], 0)
        key_sum, value_sum = kv_sum[:, :head], kv_sum[:, head:]
    return (
        layer_out,
        grad_tokens,
        gain_sum[0],
        query_sum,
        key_sum,
        value_sum,
        output_sum,
        gain_sum[1],
        gate_sum,
        up_sum,
        down_sum,
    )


def solution(mesh):
    in_specs = (
        P("dp", "context", None),
        P("dp", None),
        P(),
        P(None, "tensor"),
        P(None, "tensor"),
        P(None, "tensor"),
        P("tensor", None),
        P(),
        P(None, "tensor"),
        P(None, "tensor"),
        P("tensor", None),
        P("dp", "context", None),
    )
    out_specs = (
        P("dp", "context", None),
        P("dp", "context", None),
        P(("context", "dp")),
        P(("context", "dp"), "tensor"),
        P(("context", "dp"), "tensor"),
        P(("context", "dp"), "tensor"),
        P("tensor", ("context", "dp")),
        P(("context", "dp")),
        P(("context", "dp"), "tensor"),
        P(("context", "dp"), "tensor"),
        P("tensor", ("context", "dp")),
    )
    run = functools.partial(local, dict(mesh.shape))
    return jax.shard_map(run, mesh=mesh, in_specs=in_specs, out_specs=out_specs, check_vma=False)
```
